32 devices in a mesh: fsdp: 4 (over y, x), ctx: 2 (over core), tp: 4 (over z).
Axes of the slice: x: 2, y: 2, z: 4, core: 2. Of those that a mesh axis runs over, the one named last changes fastest.
Arguments:
- tokens: bfloat16 [8192, 1536], P(('fsdp', 'ctx')), may hold values from -6 to 6
- routes: int32 [8192, 8], P(('fsdp', 'ctx')), may hold values from 0 to 15, all different within a row; in each aligned block of 1024 rows (0 to 1023, 1024 to 2047, ...) at most 640 rows name the same one
- gain_attn: bfloat16 [1536], P(('fsdp', 'ctx')), may hold values from 0.5 to 1.5
- w_query: bfloat16 [1536, 1536], P(('fsdp', 'ctx'), 'tp'), may hold values from -0.15625 to 0.15625
- key_matrix: bfloat16 [1536, 512], P(('fsdp', 'ctx'), 'tp'), may hold values from -0.15625 to 0.15625
- value_matrix: bfloat16 [1536, 512], P(('fsdp', 'ctx'), 'tp'), may hold values from -0.15625 to 0.15625
- w_out: bfloat16 [1536, 1536], P('tp', ('fsdp', 'ctx')), may hold values from -0.625 to 0.625
- gain_moe: bfloat16 [1536], P(('fsdp', 'ctx')), may hold values from 0.5 to 1.5
- w_router: bfloat16 [1536, 16], P(('fsdp', 'ctx')), may hold values from -0.078125 to 0.078125
- w_gate: bfloat16 [16, 1536, 512], P(None, ('fsdp', 'ctx'), 'tp'), may hold values from -0.15625 to 0.15625
- w_up: bfloat16 [16, 1536, 512], P(None, ('fsdp', 'ctx'), 'tp'), may hold values from -0.15625 to 0.15625
- w_down: bfloat16 [16, 512, 1536], P(None, 'tp', ('fsdp', 'ctx')), may hold values from -0.75 to 0.75
- cotangent: bfloat16 [8192, 1536], P(('fsdp', 'ctx')), may hold values from -6 to 6
Outputs:
- activations: bfloat16 [8192, 1536], P(('fsdp', 'ctx'))
- input_grad: bfloat16 [8192, 1536], P(('fsdp', 'ctx'))
- grad_gain_attn: float32 [1536], P(('fsdp', 'ctx'))
- grad_query: float32 [1536, 1536], P(('fsdp', 'ctx'), 'tp')
- grad_key: float32 [1536, 512], P(('fsdp', 'ctx'), 'tp')
- grad_value: float32 [1536, 512], P(('fsdp', 'ctx'), 'tp')
- grad_out: float32 [1536, 1536], P('tp', ('fsdp', 'ctx'))
- grad_gain_moe: float32 [1536], P(('fsdp', 'ctx'))
- grad_router: float32 [1536, 16], P(('fsdp', 'ctx'))
- grad_gate: float32 [16, 1536, 512], P(None, ('fsdp', 'ctx'), 'tp')
- grad_up: float32 [16, 1536, 512], P(None, ('fsdp', 'ctx'), 'tp')
- grad_down: float32 [16, 512, 1536], P(None, 'tp', ('fsdp', 'ctx'))
The draws below stay inside these ranges and needn't reach their ends.
Inputs may be any that keep to these rules, and one draw needn't show every extreme that they name: `routes`: each row names 8 different experts; among the 1024 rows of one device no expert is named more than 640 times, and on some device one is named exactly 640 times.
All inputs are finite; a program needn't handle non-finite values.
Results may differ from the reference program's by a relative error of at most 0.017.
Values may be sent and summed in bfloat16 or wider, within the bound.
A program may use at most 384 MiB of HBM per device.

```python
import math
from functools import partial
import jax
import jax.numpy as jnp
import numpy as np
from jax import lax

MODEL_WIDTH = 1536
QUERY_HEADS = 24
KEY_VALUE_HEADS = 8
HEAD_SIZE = 64
FFE = 512
TOPK = 8
E = 16
SEQUENCE_LENGTH = 1024
SEQ_DEV = 2
TOK_DEV = 1024
TOKENS = 8192
CAP = 640
N_FSDP = 4
N_CTX = 2


def levels(key, extent, split, low, high):
    level, own = 1.0, jax.random.fold_in(key, 6)
    for position, parts in split:
        steps = jnp.exp(jax.random.uniform(jax.random.fold_in(own, position), (parts,), jnp.float32, low / len(split), high / len(split)))
        level = level * jnp.repeat(steps, extent[position] // parts).reshape([-1 if axis == position else 1 for axis in range(len(extent))])
    return level


def routed_block(stream_key, own, number, rows, amount, top, limit, lean):
    ranking = jax.random.permutation(stream_key, amount)
    heavy_load, ordinary = load_shares(amount, rows * top, limit, lean, True), load_shares(amount, rows * top, limit, lean, False)
    places = jnp.arange(amount)

    def named(lengths, rotation):
        used = int((lengths > 0).sum())
        fixed = max(1, used // 4)
        shifted = fixed + (places - fixed + rotation * (used - fixed)) % max(1, amount - fixed)
        return jnp.zeros((amount,), jnp.int32).at[ranking[jnp.where(places < fixed, places, shifted)]].set(jnp.asarray(lengths, jnp.int32))

    lengths = jnp.where(number % 4 == 0, named(heavy_load, number // 4), named(ordinary, number - number // 4 - 1))
    mixed = jax.random.permutation(jax.random.fold_in(own, 3), amount)
    giver, receiver = mixed[0:amount // 2 * 2:2], mixed[1:amount // 2 * 2:2]
    slack = jnp.minimum(lengths[giver] - 1, limit - lengths[receiver]) // 2
    slack = jnp.where((giver == ranking[0]) | (receiver == ranking[0]) | (lengths[receiver] == 0), 0, jnp.maximum(slack, 0))
    shifted = jax.random.randint(jax.random.fold_in(own, 4), (amount // 2,), 0, 1 << 20) % (slack + 1)
    lengths = lengths.at[giver].add(-shifted).at[receiver].add(shifted)
    labels = jnp.searchsorted(jnp.cumsum(lengths), jnp.arange(rows * top), side="right").astype(jnp.int32)
    table = labels.reshape(top, rows).T
    table = table[jax.random.permutation(jax.random.fold_in(own, 1), rows)]
    rotation = jax.random.randint(jax.random.fold_in(own, 2), (rows, 1), 0, top)
    return jnp.take_along_axis(table, (jnp.arange(top)[None, :] + rotation) % top, axis=1)


def load_shares(count, total, limit, lean, full):
    loads = [(1 << 20) // math.isqrt(rank ** lean) + 1 for rank in range(1, count + 1)]
    largest = limit if full else min(limit, max(-(-total // count), total * loads[0] // sum(loads)))
    least = 1 if total - largest >= count - 1 else 0
    given, spare = [largest] + [least] * (count - 1), total - largest - least * (count - 1)
    while spare > 0:
        free = [i for i in range(1, count) if given[i] < largest] or [i for i in range(1, count) if given[i] < limit]
        whole, left = sum([loads[i] for i in free]), spare
        for i in free:
            more = min(limit - given[i], max(1, left * loads[i] // whole), spare)
            given[i] = given[i] + more
            spare = spare - more
    return np.array(given)


def centred(rng, dims, spread, limit, cuts=(), held_as=jnp.bfloat16):
    drawn = spread * jax.random.normal(rng, dims, jnp.float32)
    if cuts:
        drawn = drawn * levels(rng, dims, cuts, -0.22, 0.18)
    return jnp.clip(drawn, -limit, limit).astype(held_as)


def setup_inputs(seed: int = 0) -> dict:
    key_list = jax.random.split(jax.random.key(seed), 14)
    tokens = centred(key_list[0], (TOKENS, MODEL_WIDTH), 1.0, 6.0, ((0, 8),))
    routes_keys = jax.random.split(jax.random.fold_in(key_list[1], 1), TOKENS // TOK_DEV)
    routes_turns = jax.random.permutation(jax.random.fold_in(key_list[1], 3), TOKENS // TOK_DEV)
    routes = jax.vmap(lambda own, number: routed_block(jax.random.fold_in(key_list[1], 2), own, number, TOK_DEV, E, TOPK, CAP, 1))(routes_keys, routes_turns).reshape((TOKENS, TOPK))
    gain_attn = jnp.clip(1.0 + 0.1 * jax.random.normal(key_list[2], (MODEL_WIDTH,), jnp.float32), 0.5, 1.5).astype(jnp.bfloat16)
    w_query = centred(key_list[3], (MODEL_WIDTH, QUERY_HEADS * HEAD_SIZE), MODEL_WIDTH ** -0.5, 0.15625, ((0, 8), (1, 4)))
    key_matrix = centred(key_list[4], (MODEL_WIDTH, KEY_VALUE_HEADS * HEAD_SIZE), MODEL_WIDTH ** -0.5, 0.15625, ((0, 8), (1, 4)))
    value_matrix = centred(key_list[5], (MODEL_WIDTH, KEY_VALUE_HEADS * HEAD_SIZE), MODEL_WIDTH ** -0.5, 0.15625, ((0, 8), (1, 4)))
    w_out = centred(key_list[6], (QUERY_HEADS * HEAD_SIZE, MODEL_WIDTH), (QUERY_HEADS * HEAD_SIZE // 16) ** -0.5, 0.625, ((0, 4), (1, 8)))
    gain_moe = jnp.clip(1.0 + 0.1 * jax.random.normal(key_list[7], (MODEL_WIDTH,), jnp.float32), 0.5, 1.5).astype(jnp.bfloat16)
    w_router = centred(key_list[8], (MODEL_WIDTH, E), (4 * MODEL_WIDTH) ** -0.5, 0.078125, ((0, 8),))
    w_gate = centred(key_list[9], (E, MODEL_WIDTH, FFE), MODEL_WIDTH ** -0.5, 0.15625, ((1, 8), (2, 4)))
    w_up = centred(key_list[10], (E, MODEL_WIDTH, FFE), MODEL_WIDTH ** -0.5, 0.15625, ((1, 8), (2, 4)))
    w_down = centred(key_list[11], (E, FFE, MODEL_WIDTH), (FFE // 8) ** -0.5, 0.75, ((1, 4), (2, 8)))
    cotangent = centred(key_list[12], (TOKENS, MODEL_WIDTH), 1.0, 6.0, ((0, 8),))
    return {"tokens": tokens, "routes": routes, "gain_attn": gain_attn, "w_query": w_query, "key_matrix": key_matrix, "value_matrix": value_matrix, "w_out": w_out, "gain_moe": gain_moe, "w_router": w_router, "w_gate": w_gate, "w_up": w_up, "w_down": w_down, "cotangent": cotangent}


@jax.custom_vjp
def lowered_state(v):
    return lax.optimization_barrier(v.astype(jnp.bfloat16)).astype(jnp.float32)

@jax.custom_vjp
def low_back(v):
    return v

def low_keep(v):
    return (lowered_state(v), None)

def low_pass(kept, grad):
    return (grad,)

def back_keep(v):
    return (v, None)

def back_low(kept, grad):
    return (lowered_state(grad),)
lowered_state.defvjp(low_keep, low_pass)
low_back.defvjp(back_keep, back_low)
epsilon = 1e-06
highest = lax.Precision.HIGHEST

def placed_rows():
    half = SEQUENCE_LENGTH // N_CTX
    quarter = half // 2
    steps = jnp.arange(half, dtype=jnp.int32)[None, :]
    ranks = jnp.arange(N_CTX, dtype=jnp.int32)[:, None]
    early = ranks * quarter + steps
    late = SEQUENCE_LENGTH - (ranks + 1) * quarter + steps - quarter
    return jnp.where(steps < quarter, early, late).reshape(SEQUENCE_LENGTH)

def rotary_embed(vectors, token_places):
    halfway = HEAD_SIZE // 2
    freqs = jnp.exp(jnp.arange(halfway, dtype=jnp.float32) * (-2.0 * math.log(10000.0) / HEAD_SIZE))
    angles = token_places.astype(jnp.float32)[:, None] * freqs[None, :]
    cosine = jnp.cos(angles)[:, None, :]
    sine = jnp.sin(angles)[:, None, :]
    lower = vectors[..., :halfway]
    upper = vectors[..., halfway:]
    return jnp.concatenate([lower * cosine - upper * sine, upper * cosine + lower * sine], -1)

def into_sequences(value_rows):
    width = value_rows.shape[-1]
    grid = value_rows.reshape(N_FSDP, N_CTX, SEQ_DEV, SEQUENCE_LENGTH // N_CTX, width)
    return grid.transpose(0, 2, 1, 3, 4).reshape(N_FSDP * SEQ_DEV, SEQUENCE_LENGTH, width)

def from_sequences(value_rows):
    width = value_rows.shape[-1]
    grid = value_rows.reshape(N_FSDP, SEQ_DEV, N_CTX, SEQUENCE_LENGTH // N_CTX, width)
    return grid.transpose(0, 2, 1, 3, 4).reshape(TOKENS, width)

def rms_norm(value_rows, gain):
    scale = lax.rsqrt(lax.optimization_barrier(jnp.mean(value_rows * value_rows, -1, keepdims=True)) + epsilon)
    return value_rows * scale * gain

def attend_one(token_places, pieces):
    query_rows, key_rows, value_rows = pieces
    query_group = QUERY_HEADS // KEY_VALUE_HEADS
    grouped_heads = query_rows.reshape(SEQUENCE_LENGTH, KEY_VALUE_HEADS, query_group, HEAD_SIZE)
    keyed_rows = key_rows.reshape(SEQUENCE_LENGTH, KEY_VALUE_HEADS, HEAD_SIZE)
    valued_rows = value_rows.reshape(SEQUENCE_LENGTH, KEY_VALUE_HEADS, HEAD_SIZE)
    scores = jnp.einsum('qkgd,skd->kgqs', grouped_heads, keyed_rows, precision=highest) * (1.0 / math.sqrt(HEAD_SIZE))
    scores = low_back(scores)
    allowed = token_places[None, :] <= token_places[:, None]
    scores = jnp.where(allowed, scores, -1e+30)
    top = lax.optimization_barrier(jnp.max(scores, -1, keepdims=True))
    weights = jnp.exp(scores - top)
    probs = lowered_state(weights / lax.optimization_barrier(jnp.sum(weights, -1, keepdims=True)))
    mixed = jnp.einsum('kgqs,skd->qkgd', probs, valued_rows, precision=highest)
    return mixed.reshape(SEQUENCE_LENGTH, QUERY_HEADS * HEAD_SIZE)

def slot_table(route_rows, capacity):
    count = route_rows.shape[0]
    flat = route_rows.reshape(-1).astype(jnp.int32)
    hits = (flat[:, None] == jnp.arange(E, dtype=jnp.int32)[None, :]).astype(jnp.int32)
    before = (jnp.cumsum(hits, 0).astype(jnp.int32) - hits).astype(jnp.int32)
    ranks = lax.optimization_barrier(jnp.sum(before * hits, 1)).astype(jnp.int32)
    where_rows = (flat * capacity + ranks).astype(jnp.int32)
    owners = (jnp.arange(count * TOPK, dtype=jnp.int32) // TOPK).astype(jnp.int32)
    table = jnp.full((E * capacity,), count, jnp.int32).at[where_rows].set(owners)
    return (where_rows, table)

def expert_rows(weights, pieces):
    gate_w, up_w, down_w = weights
    normed, route_rows = pieces
    where_rows, table = slot_table(route_rows, CAP)
    padded = jnp.concatenate([normed, jnp.zeros((1, MODEL_WIDTH), jnp.float32)], 0)
    buffer = padded[table].reshape(E, CAP, MODEL_WIDTH)
    gate = low_back(jnp.einsum('ecd,edf->ecf', buffer, gate_w, precision=highest))
    up = low_back(jnp.einsum('ecd,edf->ecf', buffer, up_w, precision=highest))
    hidden = lowered_state(jax.nn.silu(gate) * up)
    outputs = low_back(jnp.einsum('ecf,efd->ecd', hidden, down_w, precision=highest))
    return outputs.reshape(E * CAP, MODEL_WIDTH)[where_rows].reshape(TOK_DEV, TOPK, MODEL_WIDTH)

def layer(routes, x, gain_attn, w_query, key_matrix, value_matrix, w_out, gain_moe, w_router, w_gate, w_up, w_down):
    token_places = placed_rows()
    normed = lowered_state(rms_norm(x, gain_attn))
    query = low_back(jnp.dot(normed, w_query, precision=highest))
    key = low_back(jnp.dot(normed, key_matrix, precision=highest))
    value = lowered_state(low_back(jnp.dot(normed, value_matrix, precision=highest)))
    sequence_batch = N_FSDP * SEQ_DEV
    q_rot = lowered_state(rotary_embed(into_sequences(query).reshape(sequence_batch, SEQUENCE_LENGTH, QUERY_HEADS, HEAD_SIZE), token_places)).reshape(sequence_batch, SEQUENCE_LENGTH, QUERY_HEADS * HEAD_SIZE)
    rotated_key = lowered_state(rotary_embed(into_sequences(key).reshape(sequence_batch, SEQUENCE_LENGTH, KEY_VALUE_HEADS, HEAD_SIZE), token_places)).reshape(sequence_batch, SEQUENCE_LENGTH, KEY_VALUE_HEADS * HEAD_SIZE)
    v_seq = into_sequences(value)
    mixed = lax.map(jax.checkpoint(partial(attend_one, token_places)), (q_rot, rotated_key, v_seq))
    mixed = lowered_state(low_back(from_sequences(mixed)))
    state = x + low_back(jnp.dot(mixed, w_out, precision=highest))
    normed_two = lowered_state(rms_norm(state, gain_moe))
    logits = low_back(jnp.dot(normed_two, w_router, precision=highest))
    match = routes[:, :, None] == jnp.arange(E, dtype=jnp.int32)[None, None, :]
    picked = lax.optimization_barrier(jnp.sum(jnp.where(match, logits[:, None, :], 0.0), -1))
    gates = jax.nn.softmax(picked, -1)
    blocks = TOKENS // TOK_DEV
    rows_out = lax.map(jax.checkpoint(partial(expert_rows, (w_gate, w_up, w_down))), (normed_two.reshape(blocks, TOK_DEV, MODEL_WIDTH), routes.reshape(blocks, TOK_DEV, TOPK)))
    rows_out = rows_out.reshape(TOKENS, TOPK, MODEL_WIDTH)
    return state + lax.optimization_barrier(jnp.sum(gates[:, :, None] * rows_out, 1))

def reference(tokens, routes, gain_attn, w_query, key_matrix, value_matrix, w_out, gain_moe, w_router, w_gate, w_up, w_down, cotangent):
    floats = [a.astype(jnp.float32) for a in (tokens, gain_attn, w_query, key_matrix, value_matrix, w_out, gain_moe, w_router, w_gate, w_up, w_down)]
    result, pullback = jax.vjp(partial(layer, routes.astype(jnp.int32)), *floats)
    grads = pullback(cotangent.astype(jnp.float32))
    return (result.astype(jnp.bfloat16), grads[0].astype(jnp.bfloat16), grads[1], grads[2], grads[3], grads[4], grads[5], grads[6], grads[7], grads[8], grads[9], grads[10])
```

```python
import math

import jax
import jax.numpy as jnp
from jax import lax
from jax.sharding import PartitionSpec as P

HEAD_SIZE = 64
TOPK = 8
E = 16
SEQUENCE_LENGTH = 1024


epsilon = 1e-06


def placed(ranks, half):
    quarter = half // 2
    steps = jnp.arange(half, dtype=jnp.int32)
    early = ranks * quarter + steps
    late = SEQUENCE_LENGTH - (ranks + 1) * quarter + steps - quarter
    return jnp.where(steps < quarter, early, late)


def angle_tables(token_places):
    halfway = HEAD_SIZE // 2
    freqs = jnp.exp(jnp.arange(halfway, dtype=jnp.float32) * (-2.0 * math.log(10000.0) / HEAD_SIZE))
    angles = token_places.astype(jnp.float32)[:, None] * freqs[None, :]
    return (jnp.cos(angles)[:, None, :], jnp.sin(angles)[:, None, :])


def rotary_embed(vectors, token_places):
    cosine, sine = angle_tables(token_places)
    halfway = HEAD_SIZE // 2
    lower = vectors[..., :halfway]
    upper = vectors[..., halfway:]
    return jnp.concatenate([lower * cosine - upper * sine, upper * cosine + lower * sine], -1)


def rotary_back(grads, token_places):
    cosine, sine = angle_tables(token_places)
    halfway = HEAD_SIZE // 2
    lower = grads[..., :halfway]
    upper = grads[..., halfway:]
    return jnp.concatenate([lower * cosine + upper * sine, upper * cosine - lower * sine], -1)


def norm_back(value_rows, scale, gain, grad):
    scaled = grad * gain
    inner = jnp.mean(scaled * value_rows, -1, keepdims=True)
    return (
        scale * scaled - value_rows * scale * scale * scale * inner,
        jnp.sum(grad * value_rows * scale, 0),
    )


def score_block(grouped_heads, keyed_rows, q_places, k_places):
    scores = jnp.einsum(
        "qkgd,skd->kgqs", grouped_heads, keyed_rows, preferred_element_type=jnp.float32
    ) * (1.0 / math.sqrt(HEAD_SIZE))
    allowed = k_places[None, :] <= q_places[:, None]
    return jnp.where(allowed, scores, -1e30)


def attend(query_rows, key_rows, value_rows, q_places, k_places):
    kv_here = key_rows.shape[-1] // HEAD_SIZE
    q_len = query_rows.shape[0]
    grouped_heads = query_rows.reshape(q_len, kv_here, -1, HEAD_SIZE)
    keyed_rows = key_rows.reshape(-1, kv_here, HEAD_SIZE)
    valued_rows = value_rows.reshape(-1, kv_here, HEAD_SIZE)
    scores = score_block(grouped_heads, keyed_rows, q_places, k_places)
    top = jnp.max(scores, -1, keepdims=True)
    weights = jnp.exp(scores - top)
    total = jnp.sum(weights, -1, keepdims=True)
    probs = (weights / total).astype(jnp.bfloat16)
    mixed = jnp.einsum("kgqs,skd->qkgd", probs, valued_rows, preferred_element_type=jnp.float32)
    return (mixed.reshape(q_len, -1), top + jnp.log(total))


def attend_back(query_rows, key_rows, value_rows, log_total, mixed_grad, q_places, k_places):
    kv_here = key_rows.shape[-1] // HEAD_SIZE
    q_len = query_rows.shape[0]
    k_len = key_rows.shape[0]
    grouped_heads = query_rows.reshape(q_len, kv_here, -1, HEAD_SIZE)
    keyed_rows = key_rows.reshape(k_len, kv_here, HEAD_SIZE)
    valued_rows = value_rows.reshape(k_len, kv_here, HEAD_SIZE)
    out_grouped = mixed_grad.reshape(q_len, kv_here, -1, HEAD_SIZE)
    scores = score_block(grouped_heads, keyed_rows, q_places, k_places)
    probs = jnp.exp(scores - log_total)
    prob_grad = jnp.einsum(
        "qkgd,skd->kgqs", out_grouped, valued_rows, preferred_element_type=jnp.float32
    )
    score_grad = (probs * (prob_grad - jnp.sum(probs * prob_grad, -1, keepdims=True))).astype(
        jnp.bfloat16
    )
    factor = 1.0 / math.sqrt(HEAD_SIZE)
    query_grad = (
        jnp.einsum("kgqs,skd->qkgd", score_grad, keyed_rows, preferred_element_type=jnp.float32)
        * factor
    )
    key_grad = (
        jnp.einsum("kgqs,qkgd->skd", score_grad, grouped_heads, preferred_element_type=jnp.float32)
        * factor
    )
    value_grad = jnp.einsum(
        "kgqs,qkgd->skd",
        probs.astype(jnp.bfloat16),
        out_grouped,
        preferred_element_type=jnp.float32,
    )
    return (
        query_grad.reshape(q_len, -1, HEAD_SIZE),
        key_grad.reshape(k_len, -1),
        value_grad.reshape(k_len, -1),
    )


def per_device(
    tokens,
    routes,
    gain_attn,
    w_query,
    key_matrix,
    value_matrix,
    w_out,
    gain_moe,
    w_router,
    w_gate,
    w_up,
    w_down,
    cotangent,
):
    f32 = jnp.float32
    bf16 = jnp.bfloat16
    rows, width = tokens.shape
    ctx_count = lax.axis_size("ctx")
    half = SEQUENCE_LENGTH // ctx_count
    seq_here = rows // half
    both = ("fsdp", "ctx")
    local_places = placed(lax.axis_index("ctx"), half)
    all_places = placed(jnp.arange(ctx_count, dtype=jnp.int32)[:, None], half).reshape(-1)
    q_wide, k_wide, o_wide = w_query.shape[1], key_matrix.shape[1], w_out.shape[0]
    small = jnp.concatenate(
        [
            w_query,
            key_matrix,
            value_matrix,
            w_out.T,
            w_router,
            gain_attn[:, None],
            gain_moe[:, None],
        ],
        1,
    )
    cuts = (q_wide, k_wide, k_wide, o_wide, E, 1, 1)
    pad = -small.shape[1] % 128
    small = jnp.pad(small, ((0, 0), (0, pad)))
    small_full = lax.all_gather(small, both, axis=0, tiled=True)
    qkv_wide = q_wide + 2 * k_wide
    qkv_w = small_full[:, :qkv_wide]
    out_wt = small_full[:, qkv_wide : qkv_wide + o_wide]
    router_w = small_full[:, qkv_wide + o_wide : qkv_wide + o_wide + E]
    gain_one_f = small_full[:, qkv_wide + o_wide + E].astype(f32)
    gain_two_f = small_full[:, qkv_wide + o_wide + E + 1].astype(f32)
    gate_up = jnp.concatenate([w_gate, w_up], -1)
    gate_up_full = lax.all_gather(gate_up, both, axis=1, tiled=True)
    down_full = lax.all_gather(jnp.swapaxes(w_down, 1, 2), both, axis=1, tiled=True)
    inputs = tokens.astype(f32)
    scale_one = lax.rsqrt(jnp.mean(inputs * inputs, -1, keepdims=True) + epsilon)
    normed = (inputs * scale_one * gain_one_f).astype(bf16)
    heads_here = q_wide // HEAD_SIZE
    kv_here = k_wide // HEAD_SIZE
    qkv = jnp.dot(normed, qkv_w, preferred_element_type=f32)
    rot = (
        rotary_embed(
            qkv[:, : q_wide + k_wide].reshape(seq_here, half, heads_here + kv_here, HEAD_SIZE),
            local_places,
        )
        .astype(bf16)
        .reshape(seq_here, half, q_wide + k_wide)
    )
    query_rot = rot[:, :, :q_wide]
    key_value = jnp.concatenate(
        [rot[:, :, q_wide:], qkv[:, q_wide + k_wide :].astype(bf16).reshape(seq_here, half, -1)], -1
    )
    kv_all = lax.all_gather(key_value, "ctx", axis=1, tiled=True)
    keys_all, values_all = kv_all[:, :, :k_wide], kv_all[:, :, k_wide:]

    def forward_one(pieces):
        return attend(pieces[0], pieces[1], pieces[2], local_places, all_places)

    mixed, log_total = lax.map(forward_one, (query_rot, keys_all, values_all))
    mixed_low = mixed.reshape(rows, q_wide).astype(bf16)
    head_part = lax.dot_general(
        mixed_low, out_wt, (((1,), (1,)), ((), ())), preferred_element_type=f32
    )
    head_total = lax.psum(head_part.astype(bf16), "tp").astype(f32)
    state = inputs + head_total
    scale_two = lax.rsqrt(jnp.mean(state * state, -1, keepdims=True) + epsilon)
    normed_two = (state * scale_two * gain_two_f).astype(bf16)
    logits = jnp.dot(normed_two, router_w, preferred_element_type=f32)
    named = jnp.any(routes[:, :, None] == jnp.arange(E, dtype=jnp.int32)[None, None, :], 1)
    top = jnp.max(jnp.where(named, logits, -jnp.inf), -1, keepdims=True)
    raised = jnp.where(named, jnp.exp(jnp.where(named, logits, top) - top), 0.0)
    gates = raised / jnp.sum(raised, -1, keepdims=True)
    upstream = cotangent.astype(f32)

    ffn = w_gate.shape[2]
    gu = jnp.einsum("td,edf->etf", normed_two, gate_up_full, preferred_element_type=f32)
    gate_pre, up_pre = gu[:, :, :ffn], gu[:, :, ffn:]
    sigma = jax.nn.sigmoid(gate_pre)
    hidden = (gate_pre * sigma * up_pre).astype(bf16).astype(f32)
    gate_e = gates.T[:, :, None]
    hidden_gated = (gate_e * hidden).astype(bf16)
    moe_part = jnp.einsum("etf,edf->td", hidden_gated, down_full, preferred_element_type=f32)
    raw = jnp.einsum("td,edf->etf", cotangent, down_full, preferred_element_type=f32)
    dots_part = jnp.sum(hidden * raw, -1).T
    moe_total = lax.psum(moe_part.astype(bf16), "tp").astype(f32)
    gate_dots = lax.psum(dots_part, "tp")
    activations = (state + moe_total).astype(bf16)
    gate_dots = jnp.where(named, gate_dots, 0.0)
    mix_grad = gates * (gate_dots - jnp.sum(gates * gate_dots, -1, keepdims=True))
    logit_grad = mix_grad.astype(bf16)
    hidden_grad = raw * gate_e
    gate_grad = (hidden_grad * up_pre * sigma * (1.0 + gate_pre * (1.0 - sigma))).astype(bf16)
    up_grad = (hidden_grad * gate_pre * sigma).astype(bf16)
    gu_grad = jnp.concatenate([gate_grad, up_grad], -1)
    normed_two_part = jnp.einsum("etf,edf->td", gu_grad, gate_up_full, preferred_element_type=f32)
    normed_two_grad = lax.psum(normed_two_part.astype(bf16), "tp").astype(f32)
    grad_gu = jnp.einsum("td,etf->edf", normed_two, gu_grad, preferred_element_type=f32)
    grad_dn = jnp.einsum("td,etf->edf", cotangent, hidden_gated, preferred_element_type=f32)
    grad_gu = lax.psum_scatter(grad_gu.astype(bf16), both, scatter_dimension=1, tiled=True)
    grad_dn = lax.psum_scatter(grad_dn.astype(bf16), both, scatter_dimension=1, tiled=True)
    grad_gu = grad_gu.astype(f32)
    grad_dn = jnp.swapaxes(grad_dn.astype(f32), 1, 2)

    normed_two_grad = normed_two_grad + jnp.einsum(
        "te,de->td", logit_grad, router_w, preferred_element_type=f32
    )
    grad_router = jnp.einsum("td,te->de", normed_two, logit_grad, preferred_element_type=f32)
    state_delta, grad_gain_two = norm_back(state, scale_two, gain_two_f, normed_two_grad)
    state_grad = upstream + state_delta
    state_low = state_grad.astype(bf16)
    grad_out = jnp.einsum("td,tc->dc", state_low, mixed_low, preferred_element_type=f32)
    mixed_grad = jnp.dot(state_low, out_wt, preferred_element_type=f32).astype(bf16)
    mixed_grad = mixed_grad.reshape(seq_here, half, heads_here, HEAD_SIZE)

    def backward_one(pieces):
        return attend_back(
            pieces[0], pieces[1], pieces[2], pieces[3], pieces[4], local_places, all_places
        )

    query_rot4 = query_rot.reshape(seq_here, half, heads_here, HEAD_SIZE)
    query_grad, key_grad, value_grad = lax.map(
        backward_one, (query_rot4, keys_all, values_all, log_total, mixed_grad)
    )
    kv_grad = jnp.concatenate([key_grad, value_grad], -1)
    kv_grad = lax.psum_scatter(kv_grad, "ctx", scatter_dimension=1, tiled=True)
    key_grad, value_grad = kv_grad[:, :, :k_wide], kv_grad[:, :, k_wide:]
    qk_grad = jnp.concatenate(
        [query_grad, key_grad.reshape(seq_here, half, kv_here, HEAD_SIZE)], 2
    )
    qkv_low = jnp.concatenate(
        [
            rotary_back(qk_grad, local_places).reshape(rows, q_wide + k_wide),
            value_grad.reshape(rows, k_wide),
        ],
        1,
    ).astype(bf16)
    normed_part = lax.dot_general(
        qkv_low, qkv_w, (((1,), (1,)), ((), ())), preferred_element_type=f32
    )
    normed_grad = lax.psum(normed_part.astype(bf16), "tp").astype(f32)
    input_delta, grad_gain_one = norm_back(inputs, scale_one, gain_one_f, normed_grad)
    input_grad = (state_grad + input_delta).astype(bf16)
    grad_qkv = jnp.einsum("td,tc->dc", normed, qkv_low, preferred_element_type=f32)
    grad_small = jnp.concatenate(
        [grad_qkv, grad_out, grad_router, grad_gain_one[:, None], grad_gain_two[:, None]], 1
    ).astype(bf16)
    grad_small = jnp.pad(grad_small, ((0, 0), (0, pad)))
    grad_small = lax.psum_scatter(grad_small, both, scatter_dimension=0, tiled=True).astype(f32)
    parts, at = [], 0
    for wide in cuts:
        parts.append(grad_small[:, at : at + wide])
        at += wide
    return (
        activations,
        input_grad,
        parts[5][:, 0],
        parts[0],
        parts[1],
        parts[2],
        parts[3].T,
        parts[6][:, 0],
        parts[4],
        grad_gu[:, :, :ffn],
        grad_gu[:, :, ffn:],
        grad_dn,
    )


def solution(mesh):
    placed = (
        P(("fsdp", "ctx"), None),
        P(("fsdp", "ctx"), None),
        P(("fsdp", "ctx")),
        P(("fsdp", "ctx"), "tp"),
        P(("fsdp", "ctx"), "tp"),
        P(("fsdp", "ctx"), "tp"),
        P("tp", ("fsdp", "ctx")),
        P(("fsdp", "ctx")),
        P(("fsdp", "ctx"), None),
        P(None, ("fsdp", "ctx"), "tp"),
        P(None, ("fsdp", "ctx"), "tp"),
        P(None, "tp", ("fsdp", "ctx")),
        P(("fsdp", "ctx"), None),
    )
    return jax.shard_map(
        per_device,
        mesh=mesh,
        in_specs=placed,
        out_specs=(
            P(("fsdp", "ctx"), None),
            P(("fsdp", "ctx"), None),
            P(("fsdp", "ctx")),
            P(("fsdp", "ctx"), "tp"),
            P(("fsdp", "ctx"), "tp"),
            P(("fsdp", "ctx"), "tp"),
            P("tp", ("fsdp", "ctx")),
            P(("fsdp", "ctx")),
            P(("fsdp", "ctx"), None),
            P(None, ("fsdp", "ctx"), "tp"),
            P(None, ("fsdp", "ctx"), "tp"),
            P(None, "tp", ("fsdp", "ctx")),
        ),
        check_vma=False,
    )
```

```python
import functools
import math

import jax
import jax.numpy as jnp
from jax import lax
from jax.experimental import pallas as pl
from jax.experimental.pallas import tpu as pltpu
from jax.sharding import PartitionSpec as P

HEAD_SIZE = 64
TOPK = 8
E = 16
SEQUENCE_LENGTH = 1024
LANES = 128
VMEM_BYTES = 58 * 2**20

epsilon = 1e-06
f32 = jnp.float32
bf16 = jnp.bfloat16
MESH = pl.DeviceIdType.MESH
WHOLE = pl.BlockSpec(memory_space=pltpu.VMEM)


def placed(ranks, half):
    quarter = half // 2
    steps = jnp.arange(half, dtype=jnp.int32)
    early = ranks * quarter + steps
    late = SEQUENCE_LENGTH - (ranks + 1) * quarter + steps - quarter
    return jnp.where(steps < quarter, early, late)


def angle_tables(token_places):
    halfway = HEAD_SIZE // 2
    freqs = jnp.exp(
        jnp.arange(halfway, dtype=f32) * (-2.0 * math.log(10000.0) / HEAD_SIZE)
    )
    angles = token_places.astype(f32)[:, None] * freqs[None, :]
    copies = LANES // halfway
    return jnp.tile(jnp.cos(angles), (1, copies)), jnp.tile(jnp.sin(angles), (1, copies))


def aligned(start, size):
    return pl.ds(pl.multiple_of(start, size), size)


def dot(a, b, at=(1, 0)):
    return lax.dot_general(a, b, (((at[0],), (at[1],)), ((), ())), preferred_element_type=f32)


def swapped_halves(y):
    wide, halfway = y.shape[1], HEAD_SIZE // 2
    lane = lax.broadcasted_iota(jnp.int32, y.shape, 1)
    lower = lax.rem(lane, HEAD_SIZE) < halfway
    return jnp.where(lower, -pltpu.roll(y, wide - halfway, 1), pltpu.roll(y, halfway, 1))


def widened(table, wide):
    return jnp.concatenate([table] * (wide // LANES), 1)


def line_scratch(rows, width, chunks):
    buffer = pltpu.VMEM((rows, width), bf16)
    sems = pltpu.SemaphoreType.DMA((chunks,))
    return [buffer] * 4 + [sems] * 4


def line_barrier(n, me, others=()):
    barrier = pltpu.get_barrier_semaphore()

    @pl.when(me > 0)
    def _():
        pl.semaphore_signal(
            barrier, inc=1, device_id={"tp": lax.rem(me + n - 1, n)}, device_id_type=MESH
        )

    @pl.when(me < n - 1)
    def _():
        pl.semaphore_signal(
            barrier, inc=1, device_id={"tp": lax.rem(me + 1, n)}, device_id_type=MESH
        )

    for other in others:
        pl.semaphore_signal(barrier, inc=1, device_id=other, device_id_type=MESH)
    count = jnp.where(me > 0, 1, 0) + jnp.where(me < n - 1, 1, 0) + len(others)
    pl.semaphore_wait(barrier, count)


class Line:
    def __init__(self, n, me, chunks, own, finish, scratch):
        self.n, self.me, self.chunks, self.own, self.finish = n, me, chunks, own, finish
        self.from_left, self.from_right, self.to_right, self.to_left = scratch[:4]
        self.send_right, self.recv_left, self.send_left, self.recv_right = scratch[4:]
        self.size = own.shape[0] // chunks
        self.steps = chunks + n - 1

    def clear(self):
        @pl.when(self.me == 0)
        def _():
            self.from_left[...] = jnp.zeros_like(self.from_left)

        @pl.when(self.me == self.n - 1)
        def _():
            self.from_right[...] = jnp.zeros_like(self.from_right)

    def rows(self, c):
        return aligned(c * self.size, self.size)

    def right(self, c):
        return pltpu.make_async_remote_copy(
            src_ref=self.to_right.at[self.rows(c)],
            dst_ref=self.from_left.at[self.rows(c)],
            send_sem=self.send_right.at[c],
            recv_sem=self.recv_left.at[c],
            device_id={"tp": lax.rem(self.me + 1, self.n)},
            device_id_type=MESH,
        )

    def left(self, c):
        return pltpu.make_async_remote_copy(
            src_ref=self.to_left.at[self.rows(c)],
            dst_ref=self.from_right.at[self.rows(c)],
            send_sem=self.send_left.at[c],
            recv_sem=self.recv_right.at[c],
            device_id={"tp": lax.rem(self.me + self.n - 1, self.n)},
            device_id_type=MESH,
        )

    def step(self, t):
        n, me, chunks = self.n, self.me, self.chunks
        to_go = t - me

        @pl.when((me < n - 1) & (to_go >= 0) & (to_go < chunks))
        def _():
            rows = self.rows(to_go)

            @pl.when(me > 0)
            def _():
                self.right(to_go).wait_recv()

            total = self.own[rows].astype(f32) + self.from_left[rows].astype(f32)
            self.to_right[rows] = total.astype(bf16)
            self.right(to_go).start()

        to_come = t - (n - 1 - me)

        @pl.when((me > 0) & (to_come >= 0) & (to_come < chunks))
        def _():
            rows = self.rows(to_come)

            @pl.when(me < n - 1)
            def _():
                self.left(to_come).wait_recv()

            total = self.own[rows].astype(f32) + self.from_right[rows].astype(f32)
            self.to_left[rows] = total.astype(bf16)
            self.left(to_come).start()

        done = t - jnp.maximum(me, n - 1 - me)

        @pl.when((done >= 0) & (done < chunks))
        def _():
            @pl.when(me == 0)
            def _():
                self.left(done).wait_recv()

            @pl.when(me == n - 1)
            def _():
                self.right(done).wait_recv()

            rows = self.rows(done)
            total = (
                self.own[rows].astype(f32)
                + self.from_left[rows].astype(f32)
                + self.from_right[rows].astype(f32)
            )
            self.finish(done, rows, total)

    def sent(self):
        def one(c, carry):
            @pl.when(self.me < self.n - 1)
            def _():
                self.right(c).wait_send()

            @pl.when(self.me > 0)
            def _():
                self.left(c).wait_send()

            return carry

        lax.fori_loop(0, self.chunks, one, 0)


def loop(low, high, body):
    lax.fori_loop(low, high, lambda i, carry: (body(i), carry)[1], 0)


def folded(values):
    rows, width = values.shape
    return jnp.sum(values.reshape(rows // 8, 8, width), 0)


class Places:
    def __init__(self, nc):
        self.nc = nc
        self.c = lax.axis_index("ctx")
        self.quarter = SEQUENCE_LENGTH // nc // 2

    def slot(self, rank, part):
        return rank if part == 0 else 2 * self.nc - 1 - rank

    def rows(self, rank, part):
        return aligned(self.slot(rank, part) * self.quarter, self.quarter)

    def own(self, s, part):
        return aligned((2 * s + part) * self.quarter, self.quarter)

    def keys(self, part):
        return self.quarter * (self.nc if part == 0 else 2 * self.nc)

    def after(self, o):
        return lax.rem(self.c + o, self.nc)

    def before(self, o):
        return lax.rem(self.c + self.nc - o, self.nc)


def front_kernel(
    n,
    nc,
    x_ref,
    wqkv_ref,
    wout_ref,
    router_ref,
    named_ref,
    gain_one_ref,
    gain_two_ref,
    cos_ref,
    sin_ref,
    query_ref,
    kv_ref,
    mixed_ref,
    state_ref,
    normed_ref,
    gates_ref,
    kv_all,
    own,
    send_kv,
    recv_kv,
    *scratch,
):
    me = lax.axis_index("tp")
    places = Places(nc)
    quarter = places.quarter
    seqs = kv_ref.shape[0]
    q_wide, k_wide = query_ref.shape[1], kv_ref.shape[2] // 2
    group = q_wide // k_wide

    def finish(c, rows, total):
        state = x_ref[rows].astype(f32) + total
        scale = lax.rsqrt(jnp.mean(state * state, -1, keepdims=True) + epsilon)
        normed = (state * scale * gain_two_ref[...]).astype(bf16)
        state_ref[rows] = state
        normed_ref[rows] = normed
        named = named_ref[rows] > 0.5
        logits = jnp.where(named, dot(normed, router_ref[...]), -1e30)
        top = jnp.max(logits, -1, keepdims=True)
        raised = jnp.where(named, jnp.exp(logits - top), 0.0)
        gates_ref[rows] = raised / jnp.sum(raised, -1, keepdims=True)

    line = Line(n, me, own.shape[0] // 128, own, finish, scratch)
    line_barrier(n, me, [{"ctx": places.after(o)} for o in range(1, nc)])
    line.clear()

    def kv_copy(s, part, o, rank):
        where = kv_all.at[s, places.rows(rank, part)]
        return pltpu.make_async_remote_copy(
            src_ref=where,
            dst_ref=where,
            send_sem=send_kv.at[o - 1, s, part],
            recv_sem=recv_kv.at[o - 1, s, part],
            device_id={"ctx": places.after(o)},
            device_id_type=MESH,
        )

    def project(s):
        for part in range(2):
            rows = places.own(s, part)
            x = x_ref[rows].astype(f32)
            scale = lax.rsqrt(jnp.mean(x * x, -1, keepdims=True) + epsilon)
            normed = (x * scale * gain_one_ref[...]).astype(bf16)
            qkv = dot(normed, wqkv_ref[...])
            qk = qkv[:, : q_wide + k_wide]
            here = pl.ds(part * quarter, quarter)
            cos, sin = widened(cos_ref[here], q_wide + k_wide), widened(sin_ref[here], q_wide + k_wide)
            rot = qk * cos + swapped_halves(qk) * sin
            query_ref[rows] = (rot[:, :q_wide] * (1.0 / math.sqrt(HEAD_SIZE))).astype(bf16)
            slot = places.rows(places.c, part)
            kv_all[s, slot, :k_wide] = rot[:, q_wide:].astype(bf16)
            kv_all[s, slot, k_wide:] = qkv[:, q_wide + k_wide :].astype(bf16)
            for o in range(1, nc):
                kv_copy(s, part, o, places.c).start()

    loop(0, seqs, project)

    def attend(s):
        for part in range(2):
            for o in range(1, nc):
                kv_copy(s, part, o, places.before(o)).wait_recv()
        for part in range(2):
            rows = places.own(s, part)
            keys = places.keys(part)
            base = places.slot(places.c, part) * quarter
            allowed = lax.broadcasted_iota(jnp.int32, (quarter, keys), 1) <= (
                base + lax.broadcasted_iota(jnp.int32, (quarter, keys), 0)
            )
            for h in range(q_wide // HEAD_SIZE):
                at = h // group * HEAD_SIZE
                query = query_ref[rows, h * HEAD_SIZE : (h + 1) * HEAD_SIZE]
                key = kv_all[s, :keys, at : at + HEAD_SIZE]
                value = kv_all[s, :keys, k_wide + at : k_wide + at + HEAD_SIZE]
                scores = jnp.where(allowed, dot(query, key, (1, 1)), -1e30)
                raised = jnp.exp(scores - jnp.max(scores, -1, keepdims=True))
                probs = (raised * (1.0 / jnp.sum(raised, -1, keepdims=True))).astype(bf16)
                mixed_ref[rows, h * HEAD_SIZE : (h + 1) * HEAD_SIZE] = dot(probs, value).astype(bf16)
            own[rows] = dot(mixed_ref[rows], wout_ref[...], (1, 1)).astype(bf16)
            per = quarter // line.size
            for i in range(per):
                line.step((2 * s + part) * per + i)

    loop(0, seqs, attend)
    loop(line.chunks, line.steps, line.step)
    kv_ref[...] = kv_all[...]
    line.sent()

    def kv_sent(s):
        for part in range(2):
            for o in range(1, nc):
                kv_copy(s, part, o, places.c).wait_send()

    loop(0, seqs, kv_sent)


def moe_kernel(x_ref, dy_ref, gates_ref, w_ref, hidden_ref, grad_ref, dots_ref, out_ref, dx_ref):
    rows = x_ref.shape[0]
    pair = hidden_ref.shape[1] // (E // 2)
    single = pair // 2
    gu_wide = grad_ref.shape[1]
    lane = lax.broadcasted_iota(jnp.int32, (rows, LANES), 1)
    first = lax.broadcasted_iota(jnp.int32, (rows, pair), 1) < single
    dots_ref[...] = jnp.zeros_like(dots_ref)

    def experts(p):
        gu = dot(x_ref[...], w_ref[:, aligned(p * 2 * pair, 2 * pair)])
        raw = dot(dy_ref[...], w_ref[:, aligned(gu_wide + p * pair, pair)])
        gate_pre, up_pre = gu[:, :pair], gu[:, pair:]
        gates = gates_ref[...]
        gate = jnp.where(
            first,
            jnp.sum(jnp.where(lane == 2 * p, gates, 0.0), 1, keepdims=True),
            jnp.sum(jnp.where(lane == 2 * p + 1, gates, 0.0), 1, keepdims=True),
        )
        sigma = jax.nn.sigmoid(gate_pre)
        silu = gate_pre * sigma
        hidden = (silu * up_pre).astype(bf16).astype(f32)
        hidden_ref[:, aligned(p * pair, pair)] = (hidden * gate).astype(bf16)
        both = hidden * raw
        dots_ref[...] += jnp.where(
            lane == 2 * p, jnp.sum(both[:, :single], 1, keepdims=True), 0.0
        ) + jnp.where(lane == 2 * p + 1, jnp.sum(both[:, single:], 1, keepdims=True), 0.0)
        dh = raw * gate
        grad_ref[:, aligned(p * 2 * pair, pair)] = (
            dh * up_pre * (sigma + silu * (1.0 - sigma))
        ).astype(bf16)
        grad_ref[:, aligned(p * 2 * pair + pair, pair)] = (dh * silu).astype(bf16)

    loop(0, E // 2, experts)
    tile = 256

    def outward(i):
        at = aligned(i * tile, tile)
        out_ref[:, at] = dot(hidden_ref[...], w_ref[at, gu_wide:], (1, 1)).astype(bf16)
        dx_ref[:, at] = dot(grad_ref[...], w_ref[at, :gu_wide], (1, 1)).astype(bf16)

    loop(0, out_ref.shape[1] // tile, outward)


def weight_kernel(gu_blocks, x_ref, dy_ref, grad_ref, hidden_ref, out_ref):
    step = pl.program_id(0)

    @pl.when(step < gu_blocks)
    def _():
        out_ref[...] = dot(x_ref[...], grad_ref[...]).astype(bf16)

    @pl.when(step >= gu_blocks)
    def _():
        out_ref[...] = dot(dy_ref[...], hidden_ref[...]).astype(bf16)


def middle_kernel(
    n,
    own,
    state_ref,
    dy_ref,
    gates_ref,
    dots_ref,
    router_ref,
    gain_ref,
    dstate_ref,
    dlogits_ref,
    dgain_ref,
    *scratch,
):
    me = lax.axis_index("tp")
    dgain_ref[...] = jnp.zeros_like(dgain_ref)

    def finish(c, rows, total):
        gates = gates_ref[rows]
        lane = lax.broadcasted_iota(jnp.int32, gates.shape, 1)
        product = gates * dots_ref[rows]
        dlogits = product - gates * jnp.sum(product, -1, keepdims=True)
        dlogits = jnp.where(lane < E, dlogits, 0.0).astype(bf16)
        dlogits_ref[rows] = dlogits
        dn = total + dot(dlogits, router_ref[...], (1, 1))
        state = state_ref[rows]
        scale = lax.rsqrt(jnp.mean(state * state, -1, keepdims=True) + epsilon)
        unit = state * scale
        scaled = dn * gain_ref[...]
        inner = jnp.mean(scaled * unit, -1, keepdims=True)
        dstate_ref[rows] = dy_ref[rows].astype(f32) + scale * (scaled - unit * inner)
        dgain_ref[...] += folded(dn * unit)

    line = Line(n, me, own.shape[0] // 64, own, finish, scratch)
    line_barrier(n, me)
    line.clear()
    loop(0, line.steps, line.step)
    line.sent()


def output_kernel(n, own, state_ref, out_ref, *scratch):
    me = lax.axis_index("tp")

    def finish(c, rows, total):
        out_ref[rows] = (state_ref[rows] + total).astype(bf16)

    line = Line(n, me, own.shape[0] // 64, own, finish, scratch)
    line_barrier(n, me)
    line.clear()
    loop(0, line.steps, line.step)
    line.sent()


def back_kernel(
    nc,
    dstate_ref,
    wout_ref,
    query_ref,
    kv_ref,
    cos_ref,
    sin_ref,
    low_ref,
    dqkv_ref,
    dmixed,
    dquery,
    dkv,
    dkv_in,
    send_kv,
    recv_kv,
):
    places = Places(nc)
    quarter = places.quarter
    seqs = kv_ref.shape[0]
    q_wide, k_wide = query_ref.shape[1], kv_ref.shape[2] // 2
    group = q_wide // k_wide
    factor = 1.0 / math.sqrt(HEAD_SIZE)
    barrier = pltpu.get_barrier_semaphore()
    for o in range(1, nc):
        pl.semaphore_signal(
            barrier, inc=1, device_id={"ctx": places.after(o)}, device_id_type=MESH
        )
    pl.semaphore_wait(barrier, nc - 1)

    def kv_copy(s, part, o, rank):
        return pltpu.make_async_remote_copy(
            src_ref=dkv.at[s, places.rows(rank, part)],
            dst_ref=dkv_in.at[o - 1, s, part],
            send_sem=send_kv.at[o - 1, s, part],
            recv_sem=recv_kv.at[o - 1, s, part],
            device_id={"ctx": places.after(o)},
            device_id_type=MESH,
        )

    def attend(s):
        for part in (1, 0):
            rows = places.own(s, part)
            keys = places.keys(part)
            low = dstate_ref[rows].astype(bf16)
            low_ref[rows] = low
            dmixed[...] = dot(low, wout_ref[...]).astype(bf16)
            base = places.slot(places.c, part) * quarter
            allowed = lax.broadcasted_iota(jnp.int32, (keys, quarter), 0) <= (
                base + lax.broadcasted_iota(jnp.int32, (keys, quarter), 1)
            )
            for k in range(k_wide // HEAD_SIZE):
                at = k * HEAD_SIZE
                key = kv_ref[s, :keys, at : at + HEAD_SIZE]
                value = kv_ref[s, :keys, k_wide + at : k_wide + at + HEAD_SIZE]
                dkey = dvalue = None
                for h in range(k * group, (k + 1) * group):
                    head = slice(h * HEAD_SIZE, (h + 1) * HEAD_SIZE)
                    query = query_ref[rows, head]
                    dout = dmixed[:, head]
                    scores = jnp.where(allowed, dot(key, query, (1, 1)), -1e30)
                    raised = jnp.exp(scores - jnp.max(scores, 0, keepdims=True))
                    probs = raised * (1.0 / jnp.sum(raised, 0, keepdims=True))
                    product = probs * dot(value, dout, (1, 1))
                    dscores = product - probs * jnp.sum(product, 0, keepdims=True)
                    dscores = dscores.astype(bf16)
                    dquery[rows, head] = dot(dscores, key, (0, 0)) * factor
                    dk, dv = dot(dscores, query), dot(probs.astype(bf16), dout)
                    dkey = dk if dkey is None else dkey + dk
                    dvalue = dv if dvalue is None else dvalue + dv
                for start, add in ((at, dkey), (k_wide + at, dvalue)):
                    lanes = slice(start, start + HEAD_SIZE)
                    if part == 1:
                        dkv[s, :keys, lanes] = add
                    else:
                        dkv[s, :keys, lanes] += add
        for part in range(2):
            for o in range(1, nc):
                kv_copy(s, part, o, places.after(o)).start()

    loop(0, seqs, attend)

    def turn_back(s):
        for part in range(2):
            rows = places.own(s, part)
            mine = dkv[s, places.rows(places.c, part)]
            for o in range(1, nc):
                kv_copy(s, part, o, places.after(o)).wait()
                mine = mine + dkv_in[o - 1, s, part]
            turned = jnp.concatenate([dquery[rows], mine[:, :k_wide]], 1)
            here = pl.ds(part * quarter, quarter)
            cos, sin = widened(cos_ref[here], q_wide + k_wide), widened(sin_ref[here], q_wide + k_wide)
            dqkv_ref[rows, : q_wide + k_wide] = (
                turned * cos - swapped_halves(turned) * sin
            ).astype(bf16)
            dqkv_ref[rows, q_wide + k_wide :] = mine[:, k_wide:].astype(bf16)

    loop(0, seqs, turn_back)


def tail_kernel(
    n, dqkv_ref, wqkv_ref, x_ref, dstate_ref, gain_ref, out_ref, dgain_ref, own, *scratch
):
    me = lax.axis_index("tp")
    dgain_ref[...] = jnp.zeros_like(dgain_ref)

    def finish(c, rows, total):
        x = x_ref[rows].astype(f32)
        scale = lax.rsqrt(jnp.mean(x * x, -1, keepdims=True) + epsilon)
        unit = x * scale
        scaled = total * gain_ref[...]
        inner = jnp.mean(scaled * unit, -1, keepdims=True)
        out_ref[rows] = (dstate_ref[rows] + scale * (scaled - unit * inner)).astype(bf16)
        dgain_ref[...] += folded(total * unit)

    line = Line(n, me, own.shape[0] // 64, own, finish, scratch)
    line_barrier(n, me)
    line.clear()
    block = 256

    def start(i):
        rows = aligned(i * block, block)
        own[rows] = dot(dqkv_ref[rows], wqkv_ref[...], (1, 1)).astype(bf16)
        for j in range(block // line.size):
            line.step(i * (block // line.size) + j)

    loop(0, own.shape[0] // block, start)
    loop(line.chunks, line.steps, line.step)
    line.sent()


def call(kernel, outs, scratch, collective_id, operands, flops=0):
    total = sum(math.prod(o.shape) * o.dtype.itemsize for o in [*outs, *operands])
    return pl.pallas_call(
        kernel,
        out_shape=tuple(outs),
        in_specs=[WHOLE] * len(operands),
        out_specs=tuple([WHOLE] * len(outs)),
        scratch_shapes=scratch,
        compiler_params=pltpu.CompilerParams(
            collective_id=collective_id, has_side_effects=True, vmem_limit_bytes=VMEM_BYTES
        ),
        cost_estimate=pl.CostEstimate(flops=flops, bytes_accessed=total, transcendentals=0),
    )(*operands)


def per_device(
    tokens,
    routes,
    gain_attn,
    w_query,
    key_matrix,
    value_matrix,
    w_out,
    gain_moe,
    w_router,
    w_gate,
    w_up,
    w_down,
    cotangent,
):
    shaped = jax.ShapeDtypeStruct
    rows, width = tokens.shape
    nc, n = lax.axis_size("ctx"), lax.axis_size("tp")
    half = SEQUENCE_LENGTH // nc
    seqs = rows // half
    both = ("fsdp", "ctx")
    cos, sin = angle_tables(placed(lax.axis_index("ctx"), half))
    q_wide, k_wide, o_wide = w_query.shape[1], key_matrix.shape[1], w_out.shape[0]
    qkv_wide = q_wide + 2 * k_wide
    ffn = w_gate.shape[2]
    shard = w_gate.shape[1]

    small = jnp.concatenate(
        [
            w_query,
            key_matrix,
            value_matrix,
            w_out.T,
            w_router,
            gain_attn[:, None],
            gain_moe[:, None],
            jnp.zeros((shard, LANES - E - 2), bf16),
        ],
        1,
    )
    small_full = lax.all_gather(small, both, axis=0, tiled=True)
    wqkv = small_full[:, :qkv_wide]
    wout = small_full[:, qkv_wide : qkv_wide + o_wide]
    router = small_full[:, qkv_wide + o_wide :]
    gains = router[:, E : E + 2].astype(f32).T
    gain_one, gain_two = gains[:1], gains[1:]

    pairs = E // 2
    gates_up = jnp.stack(
        [w_gate.reshape(pairs, 2, shard, ffn), w_up.reshape(pairs, 2, shard, ffn)], 1
    )
    gates_up = gates_up.transpose(3, 0, 1, 2, 4).reshape(shard, 2 * E * ffn)
    down = w_down.transpose(2, 0, 1).reshape(shard, E * ffn)
    experts = lax.all_gather(jnp.concatenate([gates_up, down], 1), both, axis=0, tiled=True)

    named = jnp.any(routes[:, :, None] == jnp.arange(LANES, dtype=jnp.int32)[None, None, :], 1)
    named = named.astype(f32)
    kv_sems = pltpu.SemaphoreType.DMA((nc - 1, seqs, 2))

    query, kv, mixed, state, normed_two, gates = call(
        functools.partial(front_kernel, n, nc),
        [
            shaped((rows, q_wide), bf16),
            shaped((seqs, SEQUENCE_LENGTH, 2 * k_wide), bf16),
            shaped((rows, q_wide), bf16),
            shaped((rows, width), f32),
            shaped((rows, width), bf16),
            shaped((rows, LANES), f32),
        ],
        [
            pltpu.VMEM((seqs, SEQUENCE_LENGTH, 2 * k_wide), bf16),
            pltpu.VMEM((rows, width), bf16),
            kv_sems,
            kv_sems,
            *line_scratch(rows, width, rows // 128),
        ],
        0,
        (tokens, wqkv, wout, router, named, gain_one, gain_two, cos, sin),
    )

    block = 256
    gu_wide, down_wide = 2 * E * ffn, E * ffn

    def by_rows(wide):
        return pl.BlockSpec((block, wide), lambda i: (i, 0))

    hidden, gu_grad, dots, moe_part, dx_part = pl.pallas_call(
        moe_kernel,
        grid=(rows // block,),
        out_shape=(
            shaped((rows, down_wide), bf16),
            shaped((rows, gu_wide), bf16),
            shaped((rows, LANES), f32),
            shaped((rows, width), bf16),
            shaped((rows, width), bf16),
        ),
        in_specs=[
            by_rows(width),
            by_rows(width),
            by_rows(LANES),
            pl.BlockSpec(
                (width, gu_wide + down_wide), lambda i: (0, 0), pipeline_mode=pl.Buffered(1)
            ),
        ],
        out_specs=(
            by_rows(down_wide),
            by_rows(gu_wide),
            by_rows(LANES),
            by_rows(width),
            by_rows(width),
        ),
        compiler_params=pltpu.CompilerParams(vmem_limit_bytes=VMEM_BYTES),
        cost_estimate=pl.CostEstimate(
            flops=12 * rows * width * down_wide,
            bytes_accessed=2 * width * (gu_wide + down_wide),
            transcendentals=0,
        ),
    )(normed_two, cotangent, gates, experts)
    dots = lax.psum(dots[:, :E], "tp")
    dots = jnp.pad(dots, ((0, 0), (0, LANES - E)))

    column = 512
    gu_blocks, down_blocks = gu_wide // column, down_wide // column
    grad_experts = pl.pallas_call(
        functools.partial(weight_kernel, gu_blocks),
        grid=(gu_blocks + down_blocks,),
        out_shape=shaped((width, gu_wide + down_wide), bf16),
        in_specs=[
            pl.BlockSpec((width, rows), lambda i: (0, 0), pipeline_mode=pl.Buffered(1)),
            pl.BlockSpec((width, rows), lambda i: (0, 0), pipeline_mode=pl.Buffered(1)),
            pl.BlockSpec((rows, column), lambda i: (0, jnp.minimum(i, gu_blocks - 1))),
            pl.BlockSpec((rows, column), lambda i: (0, jnp.maximum(i - gu_blocks, 0))),
        ],
        out_specs=pl.BlockSpec((width, column), lambda i: (0, i)),
        compiler_params=pltpu.CompilerParams(vmem_limit_bytes=VMEM_BYTES),
        cost_estimate=pl.CostEstimate(
            flops=6 * rows * width * down_wide,
            bytes_accessed=2 * width * (gu_wide + down_wide),
            transcendentals=0,
        ),
    )(normed_two.T, cotangent.T, gu_grad, hidden)
    grad_experts = lax.psum_scatter(grad_experts, both, scatter_dimension=0, tiled=True)

    scratch = line_scratch(rows, width, rows // 64)
    dstate, dlogits, dgain_two = call(
        functools.partial(middle_kernel, n),
        [shaped((rows, width), f32), shaped((rows, LANES), bf16), shaped((8, width), f32)],
        scratch,
        1,
        (dx_part, state, cotangent, gates, dots, router, gain_two),
    )
    low, dqkv = call(
        functools.partial(back_kernel, nc),
        [shaped((rows, width), bf16), shaped((rows, qkv_wide), bf16)],
        [
            pltpu.VMEM((half // 2, q_wide), bf16),
            pltpu.VMEM((rows, q_wide), f32),
            pltpu.VMEM((seqs, SEQUENCE_LENGTH, 2 * k_wide), f32),
            pltpu.VMEM((nc - 1, seqs, 2, half // 2, 2 * k_wide), f32),
            kv_sems,
            kv_sems,
        ],
        2,
        (dstate, wout, query, kv, cos, sin),
    )
    inputs = tokens.astype(f32)
    scale_one = lax.rsqrt(jnp.mean(inputs * inputs, -1, keepdims=True) + epsilon)
    normed = (inputs * scale_one * gain_one).astype(bf16)
    grad_qkv = jnp.einsum("td,tc->dc", normed, dqkv, preferred_element_type=f32)
    grad_out = jnp.einsum("td,tc->dc", low, mixed, preferred_element_type=f32)
    grad_router = jnp.einsum("td,te->de", normed_two, dlogits, preferred_element_type=f32)
    grad_small = jnp.concatenate(
        [grad_qkv.astype(bf16), grad_out.astype(bf16), grad_router.astype(bf16)], 1
    )
    grad_small = lax.psum_scatter(grad_small, both, scatter_dimension=0, tiled=True)
    input_grad, dgain_one = call(
        functools.partial(tail_kernel, n),
        [shaped((rows, width), bf16), shaped((8, width), f32)],
        [pltpu.VMEM((rows, width), bf16), *scratch],
        3,
        (dqkv, wqkv, tokens, dstate, gain_one),
    )
    (activations,) = call(
        functools.partial(output_kernel, n),
        [shaped((rows, width), bf16)],
        scratch,
        4,
        (moe_part, state),
    )
    dgains = jnp.stack([jnp.sum(dgain_one, 0), jnp.sum(dgain_two, 0)])
    dgains = lax.psum_scatter(dgains, both, scatter_dimension=1, tiled=True)
    grad_small = grad_small.astype(f32)
    grad_experts = grad_experts.astype(f32)
    grad_gu = grad_experts[:, :gu_wide].reshape(shard, pairs, 2, 2, ffn).transpose(2, 1, 3, 0, 4)
    grad_gu = grad_gu.reshape(2, E, shard, ffn)
    grad_down = grad_experts[:, gu_wide:].reshape(shard, E, ffn).transpose(1, 2, 0)
    at = q_wide + k_wide
    return (
        activations,
        input_grad,
        dgains[0],
        grad_small[:, :q_wide],
        grad_small[:, q_wide:at],
        grad_small[:, at:qkv_wide],
        grad_small[:, qkv_wide : qkv_wide + o_wide].T,
        dgains[1],
        grad_small[:, qkv_wide + o_wide : qkv_wide + o_wide + E],
        grad_gu[0],
        grad_gu[1],
        grad_down,
    )


def solution(mesh):
    specs = (
        P(("fsdp", "ctx"), None),
        P(("fsdp", "ctx"), None),
        P(("fsdp", "ctx")),
        P(("fsdp", "ctx"), "tp"),
        P(("fsdp", "ctx"), "tp"),
        P(("fsdp", "ctx"), "tp"),
        P("tp", ("fsdp", "ctx")),
        P(("fsdp", "ctx")),
        P(("fsdp", "ctx"), None),
        P(None, ("fsdp", "ctx"), "tp"),
        P(None, ("fsdp", "ctx"), "tp"),
        P(None, "tp", ("fsdp", "ctx")),
        P(("fsdp", "ctx"), None),
    )
    return jax.shard_map(
        per_device,
        mesh=mesh,
        in_specs=specs,
        out_specs=(
            P(("fsdp", "ctx"), None),
            P(("fsdp", "ctx"), None),
            P(("fsdp", "ctx")),
            P(("fsdp", "ctx"), "tp"),
            P(("fsdp", "ctx"), "tp"),
            P(("fsdp", "ctx"), "tp"),
            P("tp", ("fsdp", "ctx")),
            P(("fsdp", "ctx")),
            P(("fsdp", "ctx"), None),
            P(None, ("fsdp", "ctx"), "tp"),
            P(None, ("fsdp", "ctx"), "tp"),
            P(None, "tp", ("fsdp", "ctx")),
        ),
        check_vma=False,
    )
```

```python
import functools
import math

import jax
import jax.numpy as jnp
from jax import lax
from jax.experimental import pallas as pl
from jax.experimental.pallas import tpu as pltpu
from jax.sharding import PartitionSpec as P

HEAD_SIZE = 64
TOPK = 8
E = 16
SEQUENCE_LENGTH = 1024
LANES = 128
VMEM_BYTES = 58 * 2**20

epsilon = 1e-06
f32 = jnp.float32
bf16 = jnp.bfloat16
MESH = pl.DeviceIdType.MESH
WHOLE = pl.BlockSpec(memory_space=pltpu.VMEM)


def placed(ranks, half):
    quarter = half // 2
    steps = jnp.arange(half, dtype=jnp.int32)
    early = ranks * quarter + steps
    late = SEQUENCE_LENGTH - (ranks + 1) * quarter + steps - quarter
    return jnp.where(steps < quarter, early, late)


def angle_tables(token_places):
    halfway = HEAD_SIZE // 2
    freqs = jnp.exp(
        jnp.arange(halfway, dtype=f32) * (-2.0 * math.log(10000.0) / HEAD_SIZE)
    )
    angles = token_places.astype(f32)[:, None] * freqs[None, :]
    copies = LANES // halfway
    return jnp.tile(jnp.cos(angles), (1, copies)), jnp.tile(jnp.sin(angles), (1, copies))


def aligned(start, size):
    return pl.ds(pl.multiple_of(start, size), size)


def dot(a, b, at=(1, 0)):
    return lax.dot_general(a, b, (((at[0],), (at[1],)), ((), ())), preferred_element_type=f32)


def swapped_halves(y):
    wide, halfway = y.shape[1], HEAD_SIZE // 2
    lane = lax.broadcasted_iota(jnp.int32, y.shape, 1)
    lower = lax.rem(lane, HEAD_SIZE) < halfway
    return jnp.where(lower, -pltpu.roll(y, wide - halfway, 1), pltpu.roll(y, halfway, 1))


def widened(table, wide):
    return jnp.concatenate([table] * (wide // LANES), 1)


SLOTS = 4


def line_scratch(rows, width, size):
    sems = pltpu.SemaphoreType.DMA((rows // size,))
    slots = pltpu.VMEM((SLOTS * size, width), bf16)
    return [pltpu.VMEM((2 * rows, width), bf16), slots, slots, *[sems] * 4]


def greet(me, n, others=()):
    barrier = pltpu.get_barrier_semaphore()

    @pl.when(me > 0)
    def _():
        pl.semaphore_signal(
            barrier, inc=1, device_id={"tp": lax.rem(me + n - 1, n)}, device_id_type=MESH
        )

    @pl.when(me < n - 1)
    def _():
        pl.semaphore_signal(
            barrier, inc=1, device_id={"tp": lax.rem(me + 1, n)}, device_id_type=MESH
        )

    for other in others:
        pl.semaphore_signal(barrier, inc=1, device_id=other, device_id_type=MESH)
    count = jnp.where(me > 0, 1, 0) + jnp.where(me < n - 1, 1, 0) + len(others)
    pl.semaphore_wait(barrier, count)


class Line:
    def __init__(self, n, me, own, finish, scratch, base=0, lag=0, hop=1):
        self.n, self.me, self.own, self.finish = n, me, own, finish
        self.arrived, self.to_right, self.to_left = scratch[:3]
        self.send_right, self.recv_left, self.send_left, self.recv_right = scratch[3:]
        self.size = self.to_right.shape[0] // SLOTS
        self.total = self.arrived.shape[0] // 2
        self.chunks = self.total // self.size
        self.base, self.lag, self.hop = base, lag, hop
        self.steps = self.chunks + lag + hop * (n - 3)
        self.middle = (me > 0) & (me < n - 1)

    def rows(self, c):
        return aligned(self.base + c * self.size, self.size)

    def left_rows(self, c):
        return aligned(c * self.size, self.size)

    def right_rows(self, c):
        return aligned(self.total + c * self.size, self.size)

    def slot(self, c):
        return aligned(lax.rem(c, SLOTS) * self.size, self.size)

    def right(self, c, end=False):
        return pltpu.make_async_remote_copy(
            src_ref=self.own.at[self.rows(c)] if end else self.to_right.at[self.slot(c)],
            dst_ref=self.arrived.at[self.left_rows(c)],
            send_sem=self.send_right.at[c],
            recv_sem=self.recv_left.at[c],
            device_id={"tp": lax.rem(self.me + 1, self.n)},
            device_id_type=MESH,
        )

    def left(self, c, end=False):
        return pltpu.make_async_remote_copy(
            src_ref=self.own.at[self.rows(c)] if end else self.to_left.at[self.slot(c)],
            dst_ref=self.arrived.at[self.right_rows(c)],
            send_sem=self.send_left.at[c],
            recv_sem=self.recv_right.at[c],
            device_id={"tp": lax.rem(self.me + self.n - 1, self.n)},
            device_id_type=MESH,
        )

    def offer(self, c):
        @pl.when(self.me == 0)
        def _():
            self.right(c, True).start()

        @pl.when(self.me == self.n - 1)
        def _():
            self.left(c, True).start()

    def step(self, t):
        n, me, chunks = self.n, self.me, self.chunks
        go, come = t - self.lag - self.hop * (me - 1), t - self.lag - self.hop * (n - 2 - me)
        done = jnp.minimum(go, come)
        nearer_left = me < n - 1 - me

        def arrival(c):
            return self.middle & (c >= 0) & (c < chunks)

        @pl.when(arrival(go) & nearer_left)
        def _():
            self.right_pass(go)

        @pl.when(arrival(come))
        def _():
            self.left_pass(come)

        @pl.when(arrival(go) & jnp.logical_not(nearer_left))
        def _():
            self.right_pass(go)

        @pl.when(arrival(done))
        def _():
            rows = self.rows(done)
            total = (
                self.own[rows].astype(f32)
                + self.arrived[self.left_rows(done)].astype(f32)
                + self.arrived[self.right_rows(done)].astype(f32)
            )
            self.finish(done, rows, total)

    def right_pass(self, c):
        self.right(c).wait_recv()

        @pl.when(c >= SLOTS)
        def _():
            self.right(c - SLOTS).wait_send()

        total = self.own[self.rows(c)].astype(f32) + self.arrived[self.left_rows(c)].astype(f32)
        self.to_right[self.slot(c)] = total.astype(bf16)
        self.right(c).start()

    def left_pass(self, c):
        self.left(c).wait_recv()

        @pl.when(c >= SLOTS)
        def _():
            self.left(c - SLOTS).wait_send()

        total = self.own[self.rows(c)].astype(f32) + self.arrived[self.right_rows(c)].astype(f32)
        self.to_left[self.slot(c)] = total.astype(bf16)
        self.left(c).start()

    def rest(self, start):
        @pl.when(self.middle)
        def _():
            loop(start, self.steps, self.step)

            def sent(c):
                self.right(c).wait_send()
                self.left(c).wait_send()

            loop(max(self.chunks - SLOTS, 0), self.chunks, sent)

        @pl.when(jnp.logical_not(self.middle))
        def _():
            def end(c):
                @pl.when(self.me == 0)
                def _():
                    self.left(c).wait_recv()

                @pl.when(self.me == self.n - 1)
                def _():
                    self.right(c).wait_recv()

                rows = self.rows(c)
                other = aligned(
                    jnp.where(self.me == 0, self.total, 0) + c * self.size, self.size
                )
                total = self.own[rows].astype(f32) + self.arrived[other].astype(f32)
                self.finish(c, rows, total)

            loop(0, self.chunks, end)

            def sent(c):
                @pl.when(self.me == 0)
                def _():
                    self.right(c, True).wait_send()

                @pl.when(self.me == self.n - 1)
                def _():
                    self.left(c, True).wait_send()

            loop(0, self.chunks, sent)


def loop(low, high, body):
    lax.fori_loop(low, high, lambda i, carry: (body(i), carry)[1], 0)


def folded(values):
    rows, width = values.shape
    return jnp.sum(values.reshape(rows // 8, 8, width), 0)


class Places:
    def __init__(self, nc):
        self.nc = nc
        self.c = lax.axis_index("ctx")
        self.quarter = SEQUENCE_LENGTH // nc // 2

    def slot(self, rank, part):
        return rank if part == 0 else 2 * self.nc - 1 - rank

    def rows(self, rank, part):
        return aligned(self.slot(rank, part) * self.quarter, self.quarter)

    def own(self, s, part):
        return aligned((2 * s + part) * self.quarter, self.quarter)

    def keys(self, part):
        return self.quarter * (self.nc if part == 0 else 2 * self.nc)

    def after(self, o):
        return lax.rem(self.c + o, self.nc)

    def before(self, o):
        return lax.rem(self.c + self.nc - o, self.nc)


def front_kernel(
    n,
    nc,
    x_ref,
    wqkv_ref,
    wout_ref,
    router_ref,
    named_ref,
    gain_one_ref,
    gain_two_ref,
    cos_ref,
    sin_ref,
    query_ref,
    kv_ref,
    mixed_ref,
    state_ref,
    normed_ref,
    gates_ref,
    kv_all,
    own,
    send_kv,
    recv_kv,
    *scratch,
):
    me = lax.axis_index("tp")
    places = Places(nc)
    quarter = places.quarter
    seqs = kv_ref.shape[0]
    q_wide, k_wide = query_ref.shape[1], kv_ref.shape[2] // 2
    group = q_wide // k_wide

    def finish(c, rows, total):
        state = x_ref[rows].astype(f32) + total
        scale = lax.rsqrt(jnp.mean(state * state, -1, keepdims=True) + epsilon)
        normed = (state * scale * gain_two_ref[...]).astype(bf16)
        state_ref[rows] = state
        normed_ref[rows] = normed
        named = named_ref[rows] > 0.5
        logits = jnp.where(named, dot(normed, router_ref[...]), -1e30)
        top = jnp.max(logits, -1, keepdims=True)
        raised = jnp.where(named, jnp.exp(logits - top), 0.0)
        gates_ref[rows] = raised / jnp.sum(raised, -1, keepdims=True)

    line = Line(n, me, own, finish, scratch, hop=2)
    greet(me, n, [{"ctx": places.after(o)} for o in range(1, nc)])

    def kv_copy(s, part, o, rank):
        where = kv_all.at[s, places.rows(rank, part)]
        return pltpu.make_async_remote_copy(
            src_ref=where,
            dst_ref=where,
            send_sem=send_kv.at[o - 1, s, part],
            recv_sem=recv_kv.at[o - 1, s, part],
            device_id={"ctx": places.after(o)},
            device_id_type=MESH,
        )

    def project(s):
        for part in range(2):
            rows = places.own(s, part)
            x = x_ref[rows].astype(f32)
            scale = lax.rsqrt(jnp.mean(x * x, -1, keepdims=True) + epsilon)
            normed = (x * scale * gain_one_ref[...]).astype(bf16)
            qkv = dot(normed, wqkv_ref[...])
            qk = qkv[:, : q_wide + k_wide]
            here = pl.ds(part * quarter, quarter)
            cos, sin = widened(cos_ref[here], q_wide + k_wide), widened(sin_ref[here], q_wide + k_wide)
            rot = qk * cos + swapped_halves(qk) * sin
            query_ref[rows] = (rot[:, :q_wide] * (1.0 / math.sqrt(HEAD_SIZE))).astype(bf16)
            slot = places.rows(places.c, part)
            kv_all[s, slot, :k_wide] = rot[:, q_wide:].astype(bf16)
            kv_all[s, slot, k_wide:] = qkv[:, q_wide + k_wide :].astype(bf16)
            for o in range(1, nc):
                kv_copy(s, part, o, places.c).start()

    loop(0, seqs, project)

    def attend(s):
        for part in range(2):
            for o in range(1, nc):
                kv_copy(s, part, o, places.before(o)).wait_recv()
        for part in range(2):
            rows = places.own(s, part)
            keys = places.keys(part)
            base = places.slot(places.c, part) * quarter
            allowed = lax.broadcasted_iota(jnp.int32, (quarter, keys), 1) <= (
                base + lax.broadcasted_iota(jnp.int32, (quarter, keys), 0)
            )
            for h in range(q_wide // HEAD_SIZE):
                at = h // group * HEAD_SIZE
                query = query_ref[rows, h * HEAD_SIZE : (h + 1) * HEAD_SIZE]
                key = kv_all[s, :keys, at : at + HEAD_SIZE]
                value = kv_all[s, :keys, k_wide + at : k_wide + at + HEAD_SIZE]
                scores = jnp.where(allowed, dot(query, key, (1, 1)), -1e30)
                raised = jnp.exp(scores - jnp.max(scores, -1, keepdims=True))
                probs = (raised * (1.0 / jnp.sum(raised, -1, keepdims=True))).astype(bf16)
                mixed_ref[rows, h * HEAD_SIZE : (h + 1) * HEAD_SIZE] = dot(probs, value).astype(bf16)
            own[rows] = dot(mixed_ref[rows], wout_ref[...], (1, 1)).astype(bf16)
            per = quarter // line.size
            first = (2 * s + part) * per
            loop(first, first + per, line.offer)
            loop(first, first + per, line.step)

    loop(0, seqs, attend)
    kv_ref[...] = kv_all[...]
    line.rest(line.chunks)

    def kv_sent(s):
        for part in range(2):
            for o in range(1, nc):
                kv_copy(s, part, o, places.c).wait_send()

    loop(0, seqs, kv_sent)


def expert_kernel(
    n,
    x_ref,
    dy_ref,
    gates_ref,
    w_ref,
    state_hbm,
    router_ref,
    gain_ref,
    hidden_ref,
    grad_ref,
    out_ref,
    dstate_hbm,
    dlogits_ref,
    dgain_ref,
    own,
    dots,
    dots_all,
    dots_rows,
    state_in,
    dstate_out,
    state_sem,
    dstate_sem,
    send_dots,
    recv_dots,
    *scratch,
):
    me = lax.axis_index("tp")
    block, steps = pl.program_id(0), pl.num_programs(0)
    size_in = x_ref.shape[0]
    width = x_ref.shape[1]
    pair = hidden_ref.shape[1] // (E // 2)
    single = pair // 2
    gu_wide = grad_ref.shape[1]
    here = aligned(block * size_in, size_in)

    def dots_copy(o, b):
        mine = dots_all.at[me, b]
        return pltpu.make_async_remote_copy(
            src_ref=mine,
            dst_ref=mine,
            send_sem=send_dots.at[o - 1, b],
            recv_sem=recv_dots.at[o - 1, b],
            device_id={"tp": lax.rem(me + o, n)},
            device_id_type=MESH,
        )

    def state_copy(c):
        return pltpu.make_async_copy(
            state_hbm.at[line.rows(c)], state_in.at[lax.rem(c, 2)], state_sem.at[lax.rem(c, 2)]
        )

    def dstate_copy(c):
        return pltpu.make_async_copy(
            dstate_out.at[lax.rem(c, 2)], dstate_hbm.at[line.rows(c)], dstate_sem.at[lax.rem(c, 2)]
        )

    def finish(c, rows, total):
        per = size_in // line.size

        @pl.when(lax.rem(c, per) == 0)
        def _():
            b = c // per
            for o in range(1, n):
                dots_copy(o, b).wait_recv()
            summed = dots_all[0, b]
            for i in range(1, n):
                summed = summed + dots_all[i, b]
            summed = jnp.concatenate(
                [summed, jnp.zeros((LANES - summed.shape[0], summed.shape[1]), f32)], 0
            )
            dots_rows[aligned(b * size_in, size_in)] = summed.T

        @pl.when(c == 0)
        def _():
            state_copy(c).start()

        @pl.when(c + 1 < line.chunks)
        def _():
            state_copy(c + 1).start()

        state_copy(c).wait()

        @pl.when(c >= 2)
        def _():
            dstate_copy(c - 2).wait()

        gates = gates_ref[rows]
        lane = lax.broadcasted_iota(jnp.int32, gates.shape, 1)
        product = gates * dots_rows[rows]
        dlogits = product - gates * jnp.sum(product, -1, keepdims=True)
        dlogits = jnp.where(lane < E, dlogits, 0.0).astype(bf16)
        dlogits_ref[rows] = dlogits
        dn = total + dot(dlogits, router_ref[...], (1, 1))
        state = state_in[lax.rem(c, 2)]
        scale = lax.rsqrt(jnp.mean(state * state, -1, keepdims=True) + epsilon)
        unit = state * scale
        scaled = dn * gain_ref[...]
        inner = jnp.mean(scaled * unit, -1, keepdims=True)
        dstate_out[lax.rem(c, 2)] = dy_ref[rows].astype(f32) + scale * (scaled - unit * inner)
        dstate_copy(c).start()
        dgain_ref[...] += folded(dn * unit)

    line = Line(n, me, own, finish, scratch, lag=size_in // (scratch[1].shape[0] // SLOTS), hop=2)
    per = size_in // line.size

    @pl.when(block == 0)
    def _():
        barrier = pltpu.get_barrier_semaphore()
        for o in range(1, n):
            pl.semaphore_signal(
                barrier, inc=1, device_id={"tp": lax.rem(me + o, n)}, device_id_type=MESH
            )
        pl.semaphore_wait(barrier, n - 1)
        dgain_ref[...] = jnp.zeros_like(dgain_ref)

    lane = lax.broadcasted_iota(jnp.int32, (size_in, LANES), 1)
    first = lax.broadcasted_iota(jnp.int32, (size_in, pair), 1) < single
    dots[...] = jnp.zeros_like(dots)

    def experts(p):
        gu = dot(x_ref[...], w_ref[:, aligned(p * 2 * pair, 2 * pair)])
        raw = dot(dy_ref[here], w_ref[:, aligned(gu_wide + p * pair, pair)])
        gate_pre, up_pre = gu[:, :pair], gu[:, pair:]
        gates = gates_ref[here]
        gate = jnp.where(
            first,
            jnp.sum(jnp.where(lane == 2 * p, gates, 0.0), 1, keepdims=True),
            jnp.sum(jnp.where(lane == 2 * p + 1, gates, 0.0), 1, keepdims=True),
        )
        sigma = jax.nn.sigmoid(gate_pre)
        silu = gate_pre * sigma
        hidden = (silu * up_pre).astype(bf16).astype(f32)
        hidden_ref[:, aligned(p * pair, pair)] = (hidden * gate).astype(bf16)
        both = hidden * raw
        dots[...] += jnp.where(
            lane == 2 * p, jnp.sum(both[:, :single], 1, keepdims=True), 0.0
        ) + jnp.where(lane == 2 * p + 1, jnp.sum(both[:, single:], 1, keepdims=True), 0.0)
        dh = raw * gate
        grad_ref[:, aligned(p * 2 * pair, pair)] = (
            dh * up_pre * (sigma + silu * (1.0 - sigma))
        ).astype(bf16)
        grad_ref[:, aligned(p * 2 * pair + pair, pair)] = (dh * silu).astype(bf16)

    tile = 256

    def outward(i):
        at = aligned(i * tile, tile)
        out_ref[:, at] = dot(hidden_ref[...], w_ref[at, gu_wide:], (1, 1)).astype(bf16)
        own[here, at] = dot(grad_ref[...], w_ref[at, :gu_wide], (1, 1)).astype(bf16)

    def experts_step(i):
        loop(i * (E // 4), (i + 1) * (E // 4), experts)
        line.step(block * per + i)

    loop(0, 2, experts_step)
    dots_all[me, block] = dots[...].T[:E]
    for o in range(1, n):
        dots_copy(o, block).start()
    tiles = width // tile // (per - 2)

    def outward_step(i):
        loop(i * tiles, (i + 1) * tiles, outward)
        line.step(block * per + 2 + i)

    loop(0, per - 2, outward_step)
    loop(block * per, block * per + per, line.offer)

    @pl.when(block == steps - 1)
    def _():
        line.rest(line.chunks)
        for c in range(line.chunks - 2, line.chunks):
            dstate_copy(c).wait()

        def dots_sent(b):
            for o in range(1, n):
                dots_copy(o, b).wait_send()

        loop(0, steps, dots_sent)


def weight_kernel(
    n, gu_blocks, x_ref, dy_ref, grad_ref, hidden_ref, moe_ref, state_ref, out_ref, act_ref, *scratch
):
    me = lax.axis_index("tp")
    step = pl.program_id(0)

    def finish(c, rows, total):
        act_ref[rows] = (state_ref[rows] + total).astype(bf16)

    line = Line(n, me, moe_ref, finish, scratch, lag=1, hop=3)

    @pl.when(step == 0)
    def _():
        greet(me, n)
        loop(0, line.chunks, line.offer)

    @pl.when(step < gu_blocks)
    def _():
        out_ref[...] = dot(x_ref[...], grad_ref[...]).astype(bf16)

    @pl.when(step >= gu_blocks)
    def _():
        out_ref[...] = dot(dy_ref[...], hidden_ref[...]).astype(bf16)

    line.step(step)

    @pl.when(step == pl.num_programs(0) - 1)
    def _():
        line.rest(pl.num_programs(0))


def back_kernel(
    n,
    nc,
    base,
    moe_ref,
    state_ref,
    dstate_ref,
    wout_ref,
    query_ref,
    kv_ref,
    cos_ref,
    sin_ref,
    low_ref,
    dqkv_ref,
    act_ref,
    dmixed,
    dquery,
    dkv,
    dkv_in,
    send_kv,
    recv_kv,
    *scratch,
):
    me = lax.axis_index("tp")
    places = Places(nc)
    quarter = places.quarter
    seqs = kv_ref.shape[0]
    q_wide, k_wide = query_ref.shape[1], kv_ref.shape[2] // 2
    group = q_wide // k_wide
    factor = 1.0 / math.sqrt(HEAD_SIZE)

    def finish(c, rows, total):
        act_ref[line.left_rows(c)] = (state_ref[rows] + total).astype(bf16)

    line = Line(n, me, moe_ref, finish, scratch, base=base, lag=2, hop=3)
    greet(me, n, [{"ctx": places.after(o)} for o in range(1, nc)])
    loop(0, line.chunks, line.offer)
    kv_heads = k_wide // HEAD_SIZE

    def kv_copy(s, part, o, rank):
        return pltpu.make_async_remote_copy(
            src_ref=dkv.at[s, places.rows(rank, part)],
            dst_ref=dkv_in.at[o - 1, s, part],
            send_sem=send_kv.at[o - 1, s, part],
            recv_sem=recv_kv.at[o - 1, s, part],
            device_id={"ctx": places.after(o)},
            device_id_type=MESH,
        )

    def attend(s):
        for part in (1, 0):
            rows = places.own(s, part)
            keys = places.keys(part)
            low = dstate_ref[rows].astype(bf16)
            low_ref[rows] = low
            dmixed[...] = dot(low, wout_ref[...]).astype(bf16)
            base = places.slot(places.c, part) * quarter
            allowed = lax.broadcasted_iota(jnp.int32, (keys, quarter), 0) <= (
                base + lax.broadcasted_iota(jnp.int32, (keys, quarter), 1)
            )
            for k in range(k_wide // HEAD_SIZE):
                at = k * HEAD_SIZE
                key = kv_ref[s, :keys, at : at + HEAD_SIZE]
                value = kv_ref[s, :keys, k_wide + at : k_wide + at + HEAD_SIZE]
                dkey = dvalue = None
                for h in range(k * group, (k + 1) * group):
                    head = slice(h * HEAD_SIZE, (h + 1) * HEAD_SIZE)
                    query = query_ref[rows, head]
                    dout = dmixed[:, head]
                    scores = jnp.where(allowed, dot(key, query, (1, 1)), -1e30)
                    raised = jnp.exp(scores - jnp.max(scores, 0, keepdims=True))
                    probs = raised * (1.0 / jnp.sum(raised, 0, keepdims=True))
                    product = probs * dot(value, dout, (1, 1))
                    dscores = product - probs * jnp.sum(product, 0, keepdims=True)
                    dscores = dscores.astype(bf16)
                    dquery[rows, head] = dot(dscores, key, (0, 0)) * factor
                    dk, dv = dot(dscores, query), dot(probs.astype(bf16), dout)
                    dkey = dk if dkey is None else dkey + dk
                    dvalue = dv if dvalue is None else dvalue + dv
                for start, add in ((at, dkey), (k_wide + at, dvalue)):
                    lanes = slice(start, start + HEAD_SIZE)
                    if part == 1:
                        dkv[s, :keys, lanes] = add
                    else:
                        dkv[s, :keys, lanes] += add
                turn = ((2 * s + 1 - part) * kv_heads + k) * 2
                line.step(turn)
                line.step(turn + 1)
        for part in range(2):
            for o in range(1, nc):
                kv_copy(s, part, o, places.after(o)).start()

    loop(0, seqs, attend)

    def turn_back(s):
        for part in range(2):
            rows = places.own(s, part)
            mine = dkv[s, places.rows(places.c, part)]
            for o in range(1, nc):
                kv_copy(s, part, o, places.after(o)).wait()
                mine = mine + dkv_in[o - 1, s, part]
            turned = jnp.concatenate([dquery[rows], mine[:, :k_wide]], 1)
            here = pl.ds(part * quarter, quarter)
            cos, sin = widened(cos_ref[here], q_wide + k_wide), widened(sin_ref[here], q_wide + k_wide)
            dqkv_ref[rows, : q_wide + k_wide] = (
                turned * cos - swapped_halves(turned) * sin
            ).astype(bf16)
            dqkv_ref[rows, q_wide + k_wide :] = mine[:, k_wide:].astype(bf16)

    loop(0, seqs, turn_back)
    line.rest(4 * seqs * kv_heads)


def tail_kernel(
    n,
    nf,
    nc,
    dqkv_ref,
    wqkv_ref,
    x_ref,
    dstate_ref,
    gain_ref,
    dgain_two_ref,
    low_ref,
    mixed_ref,
    normed_two_ref,
    dlogits_ref,
    out_ref,
    dgains_ref,
    grads_ref,
    own,
    normed,
    dgain,
    gains_in,
    grads,
    grads_in,
    send_gain,
    recv_gain,
    send_grad,
    recv_grad,
    *scratch,
):
    me = lax.axis_index("tp")
    flat = lax.axis_index("fsdp") * nc + lax.axis_index("ctx")
    peers, shard = grads.shape[0], grads.shape[1]
    dgain[...] = jnp.zeros_like(dgain)

    def peer(o):
        other = lax.rem(flat + o, peers)
        return {"fsdp": other // nc, "ctx": lax.rem(other, nc)}

    def grad_copy(o):
        return pltpu.make_async_remote_copy(
            src_ref=grads.at[lax.rem(flat + o, peers)],
            dst_ref=grads_in.at[o],
            send_sem=send_grad.at[o],
            recv_sem=recv_grad.at[o],
            device_id=peer(o),
            device_id_type=MESH,
        )

    def gain_copy(o):
        return pltpu.make_async_remote_copy(
            src_ref=gains_in.at[0],
            dst_ref=gains_in.at[o],
            send_sem=send_gain.at[o],
            recv_sem=recv_gain.at[o],
            device_id=peer(o),
            device_id_type=MESH,
        )

    def finish(c, rows, total):
        x = x_ref[rows].astype(f32)
        scale = lax.rsqrt(jnp.mean(x * x, -1, keepdims=True) + epsilon)
        unit = x * scale
        scaled = total * gain_ref[...]
        inner = jnp.mean(scaled * unit, -1, keepdims=True)
        out_ref[rows] = (dstate_ref[rows] + scale * (scaled - unit * inner)).astype(bf16)
        dgain[...] += folded(total * unit)

    line = Line(n, me, own, finish, scratch, hop=2)
    greet(me, n, [peer(o) for o in range(1, peers)])
    block = 256

    def start(i):
        rows = aligned(i * block, block)
        own[rows] = dot(dqkv_ref[rows], wqkv_ref[...], (1, 1)).astype(bf16)
        per = block // line.size
        loop(i * per, i * per + per, line.offer)
        x = x_ref[rows].astype(f32)
        scale = lax.rsqrt(jnp.mean(x * x, -1, keepdims=True) + epsilon)
        normed[rows] = (x * scale * gain_ref[...]).astype(bf16)

    loop(0, own.shape[0] // block, start)
    wide, mid = dqkv_ref.shape[1], dqkv_ref.shape[1] + mixed_ref.shape[1]
    span = max(LANES, shard * LANES // math.gcd(shard, LANES))
    count = span // shard
    turns = 2

    def weights(i):
        at = aligned(i * span, span)
        to = pl.ds(i * count, count)

        def put(lanes, value):
            grads[to, :, lanes] = value.reshape(count, shard, value.shape[1]).astype(grads.dtype)

        put(slice(0, wide), dot(normed[:, at], dqkv_ref[...], (0, 0)))
        put(slice(wide, mid), dot(low_ref[:, at], mixed_ref[...], (0, 0)))
        put(slice(mid, grads.shape[2]), dot(normed_two_ref[:, at], dlogits_ref[...], (0, 0)))
        for j in range(turns):
            line.step(i * turns + j)

    spans = normed.shape[1] // span
    loop(0, spans, weights)
    loop(1, peers, lambda o: grad_copy(o).start())
    line.rest(spans * turns)
    one = jnp.sum(dgain[...], 0, keepdims=True)
    two = jnp.sum(dgain_two_ref[...], 0, keepdims=True)
    gains_in[0] = jnp.concatenate([one, two, jnp.zeros((6, one.shape[1]), f32)], 0)
    loop(1, peers, lambda o: gain_copy(o).start())
    grads_ref[...] = grads[flat].astype(f32)

    def add_grad(o):
        grad_copy(o).wait()
        grads_ref[...] += grads_in[o].astype(f32)

    loop(1, peers, add_grad)
    loop(1, peers, lambda o: gain_copy(o).wait())
    dgains_ref[...] = gains_in[0]

    def add(o):
        dgains_ref[...] += gains_in[o]

    loop(1, peers, add)


def split_kernel(ffn, grads_ref, gate_ref, up_ref, down_ref):
    gu_wide = 2 * E * ffn
    for e in range(E):
        at = (e // 2) * 4 * ffn + (e % 2) * ffn
        gate_ref[e] = grads_ref[:, at : at + ffn].astype(f32)
        up_ref[e] = grads_ref[:, at + 2 * ffn : at + 3 * ffn].astype(f32)
        at = gu_wide + e * ffn
        down_ref[e] = grads_ref[:, at : at + ffn].astype(f32).T


def call(kernel, outs, scratch, collective_id, operands, flops=0):
    total = sum(math.prod(o.shape) * o.dtype.itemsize for o in [*outs, *operands])
    return pl.pallas_call(
        kernel,
        out_shape=tuple(outs),
        in_specs=[WHOLE] * len(operands),
        out_specs=tuple([WHOLE] * len(outs)),
        scratch_shapes=scratch,
        compiler_params=pltpu.CompilerParams(
            collective_id=collective_id, has_side_effects=True, vmem_limit_bytes=VMEM_BYTES
        ),
        cost_estimate=pl.CostEstimate(flops=flops, bytes_accessed=total, transcendentals=0),
    )(*operands)


def per_device(
    tokens,
    routes,
    gain_attn,
    w_query,
    key_matrix,
    value_matrix,
    w_out,
    gain_moe,
    w_router,
    w_gate,
    w_up,
    w_down,
    cotangent,
):
    shaped = jax.ShapeDtypeStruct
    rows, width = tokens.shape
    nc, n = lax.axis_size("ctx"), lax.axis_size("tp")
    half = SEQUENCE_LENGTH // nc
    seqs = rows // half
    both = ("fsdp", "ctx")
    cos, sin = angle_tables(placed(lax.axis_index("ctx"), half))
    q_wide, k_wide, o_wide = w_query.shape[1], key_matrix.shape[1], w_out.shape[0]
    qkv_wide = q_wide + 2 * k_wide
    ffn = w_gate.shape[2]
    shard = w_gate.shape[1]

    small = jnp.concatenate(
        [
            w_query,
            key_matrix,
            value_matrix,
            w_out.T,
            w_router,
            gain_attn[:, None],
            gain_moe[:, None],
            jnp.zeros((shard, LANES - E - 2), bf16),
        ],
        1,
    )
    small_full = lax.all_gather(small, both, axis=0, tiled=True)
    wqkv = small_full[:, :qkv_wide]
    wout = small_full[:, qkv_wide : qkv_wide + o_wide]
    router = small_full[:, qkv_wide + o_wide :]
    gains = router[:, E : E + 2].astype(f32).T
    gain_one, gain_two = gains[:1], gains[1:]

    pairs = E // 2
    gates_up = jnp.stack(
        [w_gate.reshape(pairs, 2, shard, ffn), w_up.reshape(pairs, 2, shard, ffn)], 1
    )
    gates_up = gates_up.transpose(3, 0, 1, 2, 4).reshape(shard, 2 * E * ffn)
    down = w_down.transpose(2, 0, 1).reshape(shard, E * ffn)
    experts = lax.all_gather(jnp.concatenate([gates_up, down], 1), both, axis=0, tiled=True)

    named = jnp.any(routes[:, :, None] == jnp.arange(LANES, dtype=jnp.int32)[None, None, :], 1)
    named = named.astype(f32)
    kv_sems = pltpu.SemaphoreType.DMA((nc - 1, seqs, 2))

    query, kv, mixed, state, normed_two, gates = call(
        functools.partial(front_kernel, n, nc),
        [
            shaped((rows, q_wide), bf16),
            shaped((seqs, SEQUENCE_LENGTH, 2 * k_wide), bf16),
            shaped((rows, q_wide), bf16),
            shaped((rows, width), f32),
            shaped((rows, width), bf16),
            shaped((rows, LANES), f32),
        ],
        [
            pltpu.VMEM((seqs, SEQUENCE_LENGTH, 2 * k_wide), bf16),
            pltpu.VMEM((rows, width), bf16),
            kv_sems,
            kv_sems,
            *line_scratch(rows, width, 32),
        ],
        0,
        (tokens, wqkv, wout, router, named, gain_one, gain_two, cos, sin),
    )

    block = 256
    gu_wide, down_wide = 2 * E * ffn, E * ffn

    def by_rows(wide):
        return pl.BlockSpec((block, wide), lambda i: (i, 0))

    def constant(*dims):
        return pl.BlockSpec(
            dims, lambda i: (0,) * len(dims), pipeline_mode=pl.Buffered(1)
        )

    anywhere = pl.BlockSpec(memory_space=pl.ANY)
    blocks = rows // block
    size = 64
    dots_sems = pltpu.SemaphoreType.DMA((n - 1, blocks))
    hidden, gu_grad, moe_part, dstate, dlogits, dgain_two = pl.pallas_call(
        functools.partial(expert_kernel, n),
        grid=(blocks,),
        out_shape=(
            shaped((rows, down_wide), bf16),
            shaped((rows, gu_wide), bf16),
            shaped((rows, width), bf16),
            shaped((rows, width), f32),
            shaped((rows, LANES), bf16),
            shaped((8, width), f32),
        ),
        in_specs=[
            by_rows(width),
            constant(rows, width),
            constant(rows, LANES),
            constant(width, gu_wide + down_wide),
            anywhere,
            constant(width, LANES),
            constant(1, width),
        ],
        out_specs=(
            by_rows(down_wide),
            by_rows(gu_wide),
            by_rows(width),
            anywhere,
            pl.BlockSpec((rows, LANES), lambda i: (0, 0)),
            pl.BlockSpec((8, width), lambda i: (0, 0)),
        ),
        scratch_shapes=[
            pltpu.VMEM((rows, width), bf16),
            pltpu.VMEM((block, LANES), f32),
            pltpu.VMEM((n, blocks, E, block), f32),
            pltpu.VMEM((rows, LANES), f32),
            pltpu.VMEM((2, size, width), f32),
            pltpu.VMEM((2, size, width), f32),
            pltpu.SemaphoreType.DMA((2,)),
            pltpu.SemaphoreType.DMA((2,)),
            dots_sems,
            dots_sems,
            *line_scratch(rows, width, size),
        ],
        compiler_params=pltpu.CompilerParams(
            collective_id=1, has_side_effects=True, vmem_limit_bytes=VMEM_BYTES
        ),
        cost_estimate=pl.CostEstimate(
            flops=12 * rows * width * down_wide,
            bytes_accessed=2 * width * (gu_wide + down_wide),
            transcendentals=0,
        ),
    )(normed_two, cotangent, gates, experts, state, router, gain_two)

    column = 512
    early = rows * 3 // 8
    gu_blocks, down_blocks = gu_wide // column, down_wide // column
    grad_experts, act_early = pl.pallas_call(
        functools.partial(weight_kernel, n, gu_blocks),
        grid=(gu_blocks + down_blocks,),
        out_shape=(shaped((width, gu_wide + down_wide), bf16), shaped((early, width), bf16)),
        in_specs=[
            constant(width, rows),
            constant(width, rows),
            pl.BlockSpec((rows, column), lambda i: (0, jnp.minimum(i, gu_blocks - 1))),
            pl.BlockSpec((rows, column), lambda i: (0, jnp.maximum(i - gu_blocks, 0))),
            constant(early, width),
            constant(early, width),
        ],
        out_specs=(
            pl.BlockSpec((width, column), lambda i: (0, i)),
            pl.BlockSpec((early, width), lambda i: (0, 0)),
        ),
        scratch_shapes=line_scratch(early, width, 32),
        compiler_params=pltpu.CompilerParams(
            collective_id=2, has_side_effects=True, vmem_limit_bytes=VMEM_BYTES
        ),
        cost_estimate=pl.CostEstimate(
            flops=6 * rows * width * down_wide,
            bytes_accessed=2 * width * (gu_wide + down_wide),
            transcendentals=0,
        ),
    )(normed_two.T, cotangent.T, gu_grad, hidden, moe_part, state)
    dstate, grad_experts = lax.optimization_barrier((dstate, grad_experts))
    grad_experts = lax.psum_scatter(grad_experts, both, scatter_dimension=0, tiled=True)

    low, dqkv, act_late = call(
        functools.partial(back_kernel, n, nc, early),
        [
            shaped((rows, width), bf16),
            shaped((rows, qkv_wide), bf16),
            shaped((rows - early, width), bf16),
        ],
        [
            pltpu.VMEM((half // 2, q_wide), bf16),
            pltpu.VMEM((rows, q_wide), f32),
            pltpu.VMEM((seqs, SEQUENCE_LENGTH, 2 * k_wide), f32),
            pltpu.VMEM((nc - 1, seqs, 2, half // 2, 2 * k_wide), f32),
            kv_sems,
            kv_sems,
            *line_scratch(rows - early, width, 32),
        ],
        3,
        (moe_part, state, dstate, wout, query, kv, cos, sin),
    )
    activations = jnp.concatenate([act_early, act_late], 0)
    nf = lax.axis_size("fsdp")
    peers = nf * nc
    link = bf16 if shard % 16 == 0 else f32
    peer_sems = pltpu.SemaphoreType.DMA((peers,))
    input_grad, dgains, grad_small = call(
        functools.partial(tail_kernel, n, nf, nc),
        [
            shaped((rows, width), bf16),
            shaped((8, width), f32),
            shaped((shard, small.shape[1]), f32),
        ],
        [
            pltpu.VMEM((rows, width), bf16),
            pltpu.VMEM((rows, width), bf16),
            pltpu.VMEM((8, width), f32),
            pltpu.VMEM((peers, 8, width), f32),
            pltpu.VMEM((peers, shard, small.shape[1]), link),
            pltpu.VMEM((peers, shard, small.shape[1]), link),
            *[peer_sems] * 4,
            *line_scratch(rows, width, 32),
        ],
        4,
        (dqkv, wqkv, tokens, dstate, gain_one, dgain_two, low, mixed, normed_two, dlogits),
    )
    flat = lax.axis_index("fsdp") * nc + lax.axis_index("ctx")
    dgains = lax.dynamic_slice_in_dim(dgains, flat * shard, shard, 1)
    grad_gate, grad_up, grad_down = pl.pallas_call(
        functools.partial(split_kernel, ffn),
        out_shape=(
            shaped((E, shard, ffn), f32),
            shaped((E, shard, ffn), f32),
            shaped((E, ffn, shard), f32),
        ),
        compiler_params=pltpu.CompilerParams(vmem_limit_bytes=VMEM_BYTES),
    )(grad_experts)
    at = q_wide + k_wide
    return (
        activations,
        input_grad,
        dgains[0],
        grad_small[:, :q_wide],
        grad_small[:, q_wide:at],
        grad_small[:, at:qkv_wide],
        grad_small[:, qkv_wide : qkv_wide + o_wide].T,
        dgains[1],
        grad_small[:, qkv_wide + o_wide : qkv_wide + o_wide + E],
        grad_gate,
        grad_up,
        grad_down,
    )


def solution(mesh):
    specs = (
        P(("fsdp", "ctx"), None),
        P(("fsdp", "ctx"), None),
        P(("fsdp", "ctx")),
        P(("fsdp", "ctx"), "tp"),
        P(("fsdp", "ctx"), "tp"),
        P(("fsdp", "ctx"), "tp"),
        P("tp", ("fsdp", "ctx")),
        P(("fsdp", "ctx")),
        P(("fsdp", "ctx"), None),
        P(None, ("fsdp", "ctx"), "tp"),
        P(None, ("fsdp", "ctx"), "tp"),
        P(None, "tp", ("fsdp", "ctx")),
        P(("fsdp", "ctx"), None),
    )
    return jax.shard_map(
        per_device,
        mesh=mesh,
        in_specs=specs,
        out_specs=(
            P(("fsdp", "ctx"), None),
            P(("fsdp", "ctx"), None),
            P(("fsdp", "ctx")),
            P(("fsdp", "ctx"), "tp"),
            P(("fsdp", "ctx"), "tp"),
            P(("fsdp", "ctx"), "tp"),
            P("tp", ("fsdp", "ctx")),
            P(("fsdp", "ctx")),
            P(("fsdp", "ctx"), None),
            P(None, ("fsdp", "ctx"), "tp"),
            P(None, ("fsdp", "ctx"), "tp"),
            P(None, "tp", ("fsdp", "ctx")),
        ),
        check_vma=False,
    )
```

```python
import functools
import math

import jax
import jax.numpy as jnp
from jax import lax
from jax.experimental import pallas as pl
from jax.experimental.pallas import tpu as pltpu
from jax.sharding import PartitionSpec as P

HEAD_SIZE = 64
TOPK = 8
E = 16
SEQUENCE_LENGTH = 1024
LANES = 128
VMEM_BYTES = 60 * 2**20

epsilon = 1e-06
f32 = jnp.float32
bf16 = jnp.bfloat16
MESH = pl.DeviceIdType.MESH
WHOLE = pl.BlockSpec(memory_space=pltpu.VMEM)


def placed(ranks, half):
    quarter = half // 2
    steps = jnp.arange(half, dtype=jnp.int32)
    early = ranks * quarter + steps
    late = SEQUENCE_LENGTH - (ranks + 1) * quarter + steps - quarter
    return jnp.where(steps < quarter, early, late)


def angle_tables(token_places):
    halfway = HEAD_SIZE // 2
    freqs = jnp.exp(
        jnp.arange(halfway, dtype=f32) * (-2.0 * math.log(10000.0) / HEAD_SIZE)
    )
    angles = token_places.astype(f32)[:, None] * freqs[None, :]
    copies = LANES // halfway
    return jnp.tile(jnp.cos(angles), (1, copies)), jnp.tile(jnp.sin(angles), (1, copies))


def aligned(start, size):
    return pl.ds(pl.multiple_of(start, size), size)


def dot(a, b, at=(1, 0)):
    return lax.dot_general(a, b, (((at[0],), (at[1],)), ((), ())), preferred_element_type=f32)


def swapped_halves(y):
    wide, halfway = y.shape[1], HEAD_SIZE // 2
    lane = lax.broadcasted_iota(jnp.int32, y.shape, 1)
    lower = lax.rem(lane, HEAD_SIZE) < halfway
    return jnp.where(lower, -pltpu.roll(y, wide - halfway, 1), pltpu.roll(y, halfway, 1))


def widened(table, wide):
    return jnp.concatenate([table] * (wide // LANES), 1)


SLOTS = 4


def line_scratch(rows, width, size):
    sems = pltpu.SemaphoreType.DMA((rows // size,))
    slots = pltpu.VMEM((SLOTS * size, width), bf16)
    return [pltpu.VMEM((2 * rows, width), bf16), slots, slots, *[sems] * 4]


def greet(me, n, others=()):
    barrier = pltpu.get_barrier_semaphore()

    @pl.when(me > 0)
    def _():
        pl.semaphore_signal(
            barrier, inc=1, device_id={"tp": lax.rem(me + n - 1, n)}, device_id_type=MESH
        )

    @pl.when(me < n - 1)
    def _():
        pl.semaphore_signal(
            barrier, inc=1, device_id={"tp": lax.rem(me + 1, n)}, device_id_type=MESH
        )

    for other in others:
        pl.semaphore_signal(barrier, inc=1, device_id=other, device_id_type=MESH)
    count = jnp.where(me > 0, 1, 0) + jnp.where(me < n - 1, 1, 0) + len(others)
    pl.semaphore_wait(barrier, count)


class Line:
    def __init__(self, n, me, own, finish, scratch, base=0, lag=0, hop=1):
        self.n, self.me, self.own, self.finish = n, me, own, finish
        self.arrived, self.to_right, self.to_left = scratch[:3]
        self.send_right, self.recv_left, self.send_left, self.recv_right = scratch[3:]
        self.size = self.to_right.shape[0] // SLOTS
        self.total = self.arrived.shape[0] // 2
        self.chunks = self.total // self.size
        self.base, self.lag, self.hop = base, lag, hop
        self.steps = self.chunks + lag + hop * (n - 2)
        self.middle = (me > 0) & (me < n - 1)

    def rows(self, c):
        return aligned(self.base + c * self.size, self.size)

    def left_rows(self, c):
        return aligned(c * self.size, self.size)

    def right_rows(self, c):
        return aligned(self.total + c * self.size, self.size)

    def slot(self, c):
        return aligned(lax.rem(c, SLOTS) * self.size, self.size)

    def right(self, c, end=False):
        return pltpu.make_async_remote_copy(
            src_ref=self.own.at[self.rows(c)] if end else self.to_right.at[self.slot(c)],
            dst_ref=self.arrived.at[self.left_rows(c)],
            send_sem=self.send_right.at[c],
            recv_sem=self.recv_left.at[c],
            device_id={"tp": lax.rem(self.me + 1, self.n)},
            device_id_type=MESH,
        )

    def left(self, c, end=False):
        return pltpu.make_async_remote_copy(
            src_ref=self.own.at[self.rows(c)] if end else self.to_left.at[self.slot(c)],
            dst_ref=self.arrived.at[self.right_rows(c)],
            send_sem=self.send_left.at[c],
            recv_sem=self.recv_right.at[c],
            device_id={"tp": lax.rem(self.me + self.n - 1, self.n)},
            device_id_type=MESH,
        )

    def offer(self, c):
        @pl.when(self.me == 0)
        def _():
            self.right(c, True).start()

        @pl.when(self.me == self.n - 1)
        def _():
            self.left(c, True).start()

    def step(self, t):
        n, me, chunks = self.n, self.me, self.chunks
        go, come = t - self.lag - self.hop * (me - 1), t - self.lag - self.hop * (n - 2 - me)
        done = jnp.minimum(go, come)
        nearer_left = me < n - 1 - me

        def inside(c):
            return (c >= 0) & (c < chunks)

        @pl.when(self.middle & inside(go) & nearer_left)
        def _():
            self.right_pass(go)

        @pl.when(self.middle & inside(come))
        def _():
            self.left_pass(come)

        @pl.when(self.middle & inside(go) & jnp.logical_not(nearer_left))
        def _():
            self.right_pass(go)

        @pl.when(inside(done))
        def _():
            @pl.when(me == 0)
            def _():
                self.left(done).wait_recv()
                self.right(done, True).wait_send()

            @pl.when(me == n - 1)
            def _():
                self.right(done).wait_recv()
                self.left(done, True).wait_send()

            rows = self.rows(done)
            at = done * self.size
            one = aligned(jnp.where(me == 0, self.total, 0) + at, self.size)
            two = aligned(jnp.where(me == n - 1, 0, self.total) + at, self.size)
            total = self.own[rows].astype(f32) + self.arrived[one].astype(f32)
            other = self.arrived[two].astype(f32)
            self.finish(done, rows, total + jnp.where(self.middle, other, 0.0))

    def right_pass(self, c):
        self.right(c).wait_recv()

        @pl.when(c >= SLOTS)
        def _():
            self.right(c - SLOTS).wait_send()

        total = self.own[self.rows(c)].astype(f32) + self.arrived[self.left_rows(c)].astype(f32)
        self.to_right[self.slot(c)] = total.astype(bf16)
        self.right(c).start()

    def left_pass(self, c):
        self.left(c).wait_recv()

        @pl.when(c >= SLOTS)
        def _():
            self.left(c - SLOTS).wait_send()

        total = self.own[self.rows(c)].astype(f32) + self.arrived[self.right_rows(c)].astype(f32)
        self.to_left[self.slot(c)] = total.astype(bf16)
        self.left(c).start()

    def rest(self, start):
        loop(start, self.steps, self.step)

        @pl.when(self.middle)
        def _():
            def sent(c):
                self.right(c).wait_send()
                self.left(c).wait_send()

            loop(max(self.chunks - SLOTS, 0), self.chunks, sent)


def loop(low, high, body):
    lax.fori_loop(low, high, lambda i, carry: (body(i), carry)[1], 0)


def folded(values):
    rows, width = values.shape
    return jnp.sum(values.reshape(rows // 8, 8, width), 0)


class Places:
    def __init__(self, nc):
        self.nc = nc
        self.c = lax.axis_index("ctx")
        self.quarter = SEQUENCE_LENGTH // nc // 2

    def slot(self, rank, part):
        return rank if part == 0 else 2 * self.nc - 1 - rank

    def rows(self, rank, part):
        return aligned(self.slot(rank, part) * self.quarter, self.quarter)

    def own(self, s, part):
        return aligned((2 * s + part) * self.quarter, self.quarter)

    def keys(self, part):
        return self.quarter * (self.nc if part == 0 else 2 * self.nc)

    def after(self, o):
        return lax.rem(self.c + o, self.nc)

    def before(self, o):
        return lax.rem(self.c + self.nc - o, self.nc)


def gather_kernel(
    nf,
    nc,
    ffn,
    query_ref,
    key_ref,
    value_ref,
    out_ref,
    router_ref,
    gain_one_ref,
    gain_two_ref,
    gate_ref,
    up_ref,
    down_ref,
    wqkv_ref,
    wout_ref,
    router_all_ref,
    gains_ref,
    experts_ref,
    small_all,
    send_f,
    recv_f,
    send_c,
    recv_c,
):
    f, c = lax.axis_index("fsdp"), lax.axis_index("ctx")
    shard = small_all.shape[1]
    kind = small_all.dtype
    mine = f * nc + c

    def from_f(o):
        return lax.rem(f + nf - o, nf)

    def to_peer(o):
        return {"fsdp": lax.rem(f + o, nf)}

    def to_near(p):
        return {"ctx": lax.rem(c + p, nc)}

    barrier = pltpu.get_barrier_semaphore()
    for other in [to_peer(o) for o in range(1, nf)] + [to_near(p) for p in range(1, nc)]:
        pl.semaphore_signal(barrier, inc=1, device_id=other, device_id_type=MESH)
    gains = [gain_one_ref[...].astype(f32), gain_two_ref[...].astype(f32)]
    blank = jnp.zeros((LANES - E - 2, shard), f32)
    last = jnp.concatenate([router_ref[...].astype(f32), *gains, blank], 0).T
    at = 0
    for piece in (query_ref[...], key_ref[...], value_ref[...], out_ref[...], last):
        small_all[mine, :, at : at + piece.shape[1]] = piece.astype(kind)
        at += piece.shape[1]
    pl.semaphore_wait(barrier, nf + nc - 2)

    def far_copy(o, rank):
        block = small_all.at[rank * nc + c]
        return pltpu.make_async_remote_copy(
            src_ref=block,
            dst_ref=block,
            send_sem=send_f.at[o],
            recv_sem=recv_f.at[o],
            device_id=to_peer(o),
            device_id_type=MESH,
        )

    def near_copy(p, o, rank):
        block = small_all.at[from_f(o) * nc + rank]
        return pltpu.make_async_remote_copy(
            src_ref=block,
            dst_ref=block,
            send_sem=send_c.at[p - 1, o],
            recv_sem=recv_c.at[p - 1, o],
            device_id=to_near(p),
            device_id_type=MESH,
        )

    def share(o):
        for p in range(1, nc):
            near_copy(p, o, c).start()

    loop(1, nf, lambda o: far_copy(o, f).start())
    share(0)
    for e in range(E):
        at = (e // 2) * 4 * ffn + (e % 2) * ffn
        experts_ref[:, at : at + ffn] = gate_ref[e]
        experts_ref[:, at + 2 * ffn : at + 3 * ffn] = up_ref[e]
        at = 2 * E * ffn + e * ffn
        experts_ref[:, at : at + ffn] = down_ref[e]

    def pass_on(o):
        far_copy(o, from_f(o)).wait_recv()
        share(o)

    loop(1, nf, pass_on)

    def shared(o):
        for p in range(1, nc):
            near_copy(p, o, lax.rem(c + nc - p, nc)).wait_recv()

    loop(0, nf, shared)
    at = 0
    for ref in (wqkv_ref, wout_ref, router_all_ref):
        rows, wide = ref.shape
        ref[...] = small_all[:, :, at : at + wide].reshape(rows, wide).astype(bf16)
        at += wide
    gains_ref[...] = router_all_ref[...].astype(f32).T[E : E + 8]
    loop(1, nf, lambda o: far_copy(o, f).wait_send())

    def near_sent(o):
        for p in range(1, nc):
            near_copy(p, o, c).wait_send()

    loop(0, nf, near_sent)


def front_kernel(
    n,
    nc,
    x_ref,
    wqkv_ref,
    wout_ref,
    router_ref,
    gains_ref,
    routes_ref,
    cos_ref,
    sin_ref,
    query_ref,
    kv_ref,
    mixed_ref,
    state_ref,
    normed_ref,
    gates_ref,
    kv_all,
    own,
    send_kv,
    recv_kv,
    *scratch,
):
    me = lax.axis_index("tp")
    places = Places(nc)
    quarter = places.quarter
    seqs = kv_ref.shape[0]
    q_wide, k_wide = query_ref.shape[1], kv_ref.shape[2] // 2
    group = q_wide // k_wide

    def finish(c, rows, total):
        state = x_ref[rows].astype(f32) + total
        scale = lax.rsqrt(jnp.mean(state * state, -1, keepdims=True) + epsilon)
        normed = (state * scale * gains_ref[1:2]).astype(bf16)
        state_ref[rows] = state.astype(bf16)
        normed_ref[rows] = normed
        routes = routes_ref[rows]
        lane = lax.broadcasted_iota(jnp.int32, (line.size, LANES), 1)
        named = lane == routes[:, :1]
        for k in range(1, TOPK):
            named = named | (lane == routes[:, k : k + 1])
        logits = jnp.where(named, dot(normed, router_ref[...]), -1e30)
        top = jnp.max(logits, -1, keepdims=True)
        raised = jnp.where(named, jnp.exp(logits - top), 0.0)
        gates_ref[rows] = raised / jnp.sum(raised, -1, keepdims=True)

    line = Line(n, me, own, finish, scratch, hop=2)

    greet(me, n, [{"ctx": places.after(o)} for o in range(1, nc)])

    def kv_copy(s, part, o, rank):
        where = kv_all.at[s, places.rows(rank, part)]
        return pltpu.make_async_remote_copy(
            src_ref=where,
            dst_ref=where,
            send_sem=send_kv.at[o - 1, s, part],
            recv_sem=recv_kv.at[o - 1, s, part],
            device_id={"ctx": places.after(o)},
            device_id_type=MESH,
        )

    def project(s):
        for part in range(2):
            rows = places.own(s, part)
            x = x_ref[rows].astype(f32)
            scale = lax.rsqrt(jnp.mean(x * x, -1, keepdims=True) + epsilon)
            normed = (x * scale * gains_ref[:1]).astype(bf16)
            qkv = dot(normed, wqkv_ref[...])
            qk = qkv[:, : q_wide + k_wide]
            here = pl.ds(part * quarter, quarter)
            cos, sin = widened(cos_ref[here], q_wide + k_wide), widened(sin_ref[here], q_wide + k_wide)
            rot = qk * cos + swapped_halves(qk) * sin
            query_ref[rows] = (rot[:, :q_wide] * (1.0 / math.sqrt(HEAD_SIZE))).astype(bf16)
            slot = places.rows(places.c, part)
            kv_all[s, slot, :k_wide] = rot[:, q_wide:].astype(bf16)
            kv_all[s, slot, k_wide:] = qkv[:, q_wide + k_wide :].astype(bf16)
            for o in range(1, nc):
                kv_copy(s, part, o, places.c).start()

    loop(0, seqs, project)

    def attend(s):
        for part in range(2):
            for o in range(1, nc):
                kv_copy(s, part, o, places.before(o)).wait_recv()
        for part in range(2):
            rows = places.own(s, part)
            keys = places.keys(part)
            base = places.slot(places.c, part) * quarter
            allowed = lax.broadcasted_iota(jnp.int32, (quarter, keys), 1) <= (
                base + lax.broadcasted_iota(jnp.int32, (quarter, keys), 0)
            )
            for h in range(q_wide // HEAD_SIZE):
                at = h // group * HEAD_SIZE
                query = query_ref[rows, h * HEAD_SIZE : (h + 1) * HEAD_SIZE]
                key = kv_all[s, :keys, at : at + HEAD_SIZE]
                value = kv_all[s, :keys, k_wide + at : k_wide + at + HEAD_SIZE]
                scores = jnp.where(allowed, dot(query, key, (1, 1)), -1e30)
                raised = jnp.exp(scores - jnp.max(scores, -1, keepdims=True))
                probs = (raised * (1.0 / jnp.sum(raised, -1, keepdims=True))).astype(bf16)
                mixed_ref[rows, h * HEAD_SIZE : (h + 1) * HEAD_SIZE] = dot(probs, value).astype(bf16)
            own[rows] = dot(mixed_ref[rows], wout_ref[...], (1, 1)).astype(bf16)
            per = quarter // line.size
            first = (2 * s + part) * per
            loop(first, first + per, line.offer)
            loop(first, first + per, line.step)

    loop(0, seqs, attend)
    kv_ref[...] = kv_all[...]
    line.rest(line.chunks)

    def kv_sent(s):
        for part in range(2):
            for o in range(1, nc):
                kv_copy(s, part, o, places.c).wait_send()

    loop(0, seqs, kv_sent)


def expert_kernel(
    n,
    x_ref,
    dy_ref,
    gates_ref,
    w_hbm,
    state_ref,
    router_ref,
    gains_ref,
    out_ref,
    grads_hbm,
    dstate_hbm,
    dlogits_ref,
    dgain_ref,
    own,
    hidden_ref,
    grad_ref,
    x_turned,
    dy_turned,
    dots,    dots_all,
    dots_rows,
    w_ref,
    dstate_out,
    w_sem,
    grads_sem,
    dstate_sem,
    send_dots,
    recv_dots,
    *scratch,
):
    me = lax.axis_index("tp")
    block, steps = pl.program_id(0), pl.num_programs(0)
    size_in, width = out_ref.shape
    pair = hidden_ref.shape[1] // (E // 2)
    single = pair // 2
    gu_wide = grad_ref.shape[1]
    here = aligned(block * size_in, size_in)

    def dots_copy(o, b):
        mine = dots_all.at[me, b]
        return pltpu.make_async_remote_copy(
            src_ref=mine,
            dst_ref=mine,
            send_sem=send_dots.at[o - 1, b],
            recv_sem=recv_dots.at[o - 1, b],
            device_id={"tp": lax.rem(me + o, n)},
            device_id_type=MESH,
        )

    def w_copies(p):
        spans = (aligned(p * 4 * pair, 4 * pair), aligned(gu_wide + p * 2 * pair, 2 * pair))
        return [
            pltpu.make_async_copy(w_hbm.at[:, span], w_ref.at[:, span], w_sem.at[i, p])
            for i, span in enumerate(spans)
        ]

    def dstate_copy(c):
        return pltpu.make_async_copy(
            dstate_out.at[lax.rem(c, 2)], dstate_hbm.at[line.rows(c)], dstate_sem.at[lax.rem(c, 2)]
        )

    def finish(c, rows, total):
        per = size_in // line.size

        @pl.when(lax.rem(c, per) == 0)
        def _():
            b = c // per
            for o in range(1, n):
                dots_copy(o, b).wait_recv()
            summed = dots_all[0, b]
            for i in range(1, n):
                summed = summed + dots_all[i, b]
            summed = jnp.concatenate(
                [summed, jnp.zeros((LANES - summed.shape[0], summed.shape[1]), f32)], 0
            )
            dots_rows[aligned(b * size_in, size_in)] = summed.T

        @pl.when(c >= 2)
        def _():
            dstate_copy(c - 2).wait()

        gates = gates_ref[rows]
        lane = lax.broadcasted_iota(jnp.int32, gates.shape, 1)
        product = gates * dots_rows[rows]
        dlogits = product - gates * jnp.sum(product, -1, keepdims=True)
        dlogits = jnp.where(lane < E, dlogits, 0.0).astype(bf16)
        dlogits_ref[rows] = dlogits
        dn = total + dot(dlogits, router_ref[...], (1, 1))
        state = state_ref[rows].astype(f32)
        scale = lax.rsqrt(jnp.mean(state * state, -1, keepdims=True) + epsilon)
        unit = state * scale
        scaled = dn * gains_ref[1:2]
        inner = jnp.mean(scaled * unit, -1, keepdims=True)
        dstate = dy_ref[rows].astype(f32) + scale * (scaled - unit * inner)
        dstate_out[lax.rem(c, 2)] = dstate.astype(bf16)
        dstate_copy(c).start()
        dgain_ref[...] += folded(dn * unit)

    line = Line(n, me, own, finish, scratch, lag=size_in // (scratch[1].shape[0] // SLOTS), hop=2)
    per = size_in // line.size

    @pl.when(block == 0)
    def _():
        barrier = pltpu.get_barrier_semaphore()
        for o in range(1, n):
            pl.semaphore_signal(
                barrier, inc=1, device_id={"tp": lax.rem(me + o, n)}, device_id_type=MESH
            )
        pl.semaphore_wait(barrier, n - 1)
        dgain_ref[...] = jnp.zeros_like(dgain_ref)

        def fetch(p):
            for copy in w_copies(p):
                copy.start()

        loop(0, E // 4, fetch)

    lane = lax.broadcasted_iota(jnp.int32, (size_in, LANES), 1)
    first = lax.broadcasted_iota(jnp.int32, (size_in, pair), 1) < single
    dots[...] = jnp.zeros_like(dots)

    def gating(p, gate_pre, up_pre, raw):
        gates = gates_ref[here]
        gate = jnp.where(
            first,
            jnp.sum(jnp.where(lane == 2 * p, gates, 0.0), 1, keepdims=True),
            jnp.sum(jnp.where(lane == 2 * p + 1, gates, 0.0), 1, keepdims=True),
        )
        sigma = jax.nn.sigmoid(gate_pre)
        silu = gate_pre * sigma
        hidden = (silu * up_pre).astype(bf16).astype(f32)
        hidden_ref[here, aligned(p * pair, pair)] = (hidden * gate).astype(bf16)
        both = hidden * raw
        dots[...] += jnp.where(
            lane == 2 * p, jnp.sum(both[:, :single], 1, keepdims=True), 0.0
        ) + jnp.where(lane == 2 * p + 1, jnp.sum(both[:, single:], 1, keepdims=True), 0.0)
        dh = raw * gate
        grad_ref[here, aligned(p * 2 * pair, pair)] = (
            dh * up_pre * (sigma + silu * (1.0 - sigma))
        ).astype(bf16)
        grad_ref[here, aligned(p * 2 * pair + pair, pair)] = (dh * silu).astype(bf16)

    def two_pairs(i):
        @pl.when(block == 0)
        def _():
            for copy in w_copies(i):
                copy.wait()

        gu = dot(x_ref[here], w_ref[:, aligned(i * 4 * pair, 4 * pair)])
        raw = dot(dy_ref[here], w_ref[:, aligned(gu_wide + i * 2 * pair, 2 * pair)])
        for j in range(2):
            at = 2 * j * pair
            gating(
                2 * i + j,
                gu[:, at : at + pair],
                gu[:, at + pair : at + 2 * pair],
                raw[:, j * pair : (j + 1) * pair],
            )

    tile = 512

    def outward(i):
        at = aligned(i * tile, tile)
        carried = jnp.where(me == n // 2, state_ref[here, at].astype(f32), 0.0)
        moe = dot(hidden_ref[here], w_ref[at, gu_wide:], (1, 1))
        out_ref[:, at] = (moe + carried).astype(bf16)
        own[here, at] = dot(grad_ref[here], w_ref[at, :gu_wide], (1, 1)).astype(bf16)

    halves = E // 8

    def experts_step(i):
        loop(i * 2, i * 2 + 2, two_pairs)
        line.step(block * per + i)

    loop(0, halves, experts_step)
    dots_all[me, block] = dots[...].T[:E]
    for o in range(1, n):
        dots_copy(o, block).start()
    tiles = width // tile

    def outward_step(i):
        outward(i)

        @pl.when(i != 1)
        def _():
            line.step(block * per + halves + jnp.minimum(i, 1))

    loop(0, tiles, outward_step)
    loop(block * per, block * per + per, line.offer)

    @pl.when(block == steps - 1)
    def _():
        tall = x_turned.shape[0]
        count = width // tall
        wide = 4 * pair

        def grads_copy(m):
            rows = aligned(m * tall, tall)
            return pltpu.make_async_copy(w_ref.at[rows], grads_hbm.at[rows], grads_sem.at[m])

        def gradients(m):
            at = aligned(m * tall, tall)
            x_turned[...] = x_ref[:, at].T
            dy_turned[...] = dy_ref[:, at].T
            for i in range(gu_wide // wide):
                to = slice(i * wide, (i + 1) * wide)
                w_ref[at, to] = dot(x_turned[...], grad_ref[:, to]).astype(bf16)
            for i in range(gu_wide // wide // 2):
                to = slice(i * wide, (i + 1) * wide)
                w_ref[at, gu_wide + i * wide : gu_wide + (i + 1) * wide] = dot(
                    dy_turned[...], hidden_ref[:, to]
                ).astype(bf16)
            grads_copy(m).start()
            line.step(steps * per + m)

        loop(0, count, gradients)
        line.rest(steps * per + count)
        for c in range(line.chunks - 2, line.chunks):
            dstate_copy(c).wait()

        def dots_sent(b):
            for o in range(1, n):
                dots_copy(o, b).wait_send()

        loop(0, steps, dots_sent)
        loop(0, count, lambda m: grads_copy(m).wait())


def rear_kernel(
    n,
    nf,
    nc,
    moe_hbm,
    low_hbm,
    x_hbm,
    normed_two_hbm,
    wout_ref,
    wqkv_ref,
    query_ref,
    kv_ref,
    mixed_ref,
    dlogits_ref,
    gains_ref,
    dgain_two_ref,
    cos_ref,
    sin_ref,
    act_hbm,
    input_hbm,
    dgains_ref,
    grads_ref,
    moe_ref,
    low_ref,
    x_ref,
    normed_two_ref,
    dmixed,
    dquery,
    dkv,
    dkv_in,
    dqkv_ref,
    own,
    scales,
    dgain,
    gains_in,
    grads,
    grads_in,
    load_sem,
    store_sem,
    send_kv,
    recv_kv,
    send_gain,
    recv_gain,
    send_grad,
    recv_grad,
    *scratch,
):
    me = lax.axis_index("tp")
    flat = lax.axis_index("fsdp") * nc + lax.axis_index("ctx")
    places = Places(nc)
    quarter = places.quarter
    seqs = kv_ref.shape[0]
    q_wide, k_wide = query_ref.shape[1], kv_ref.shape[2] // 2
    group = q_wide // k_wide
    kv_heads = k_wide // HEAD_SIZE
    factor = 1.0 / math.sqrt(HEAD_SIZE)
    peers, padded = grads.shape[:2]
    shard = grads_ref.shape[0]
    loads = [
        pltpu.make_async_copy(source, target, load_sem.at[i])
        for i, (source, target) in enumerate(
            (
                (moe_hbm, moe_ref),
                (low_hbm, low_ref),
                (x_hbm, x_ref),
                (normed_two_hbm, normed_two_ref),
            )
        )
    ]
    for load in loads:
        load.start()

    def peer(o):
        other = lax.rem(flat + o, peers)
        return {"fsdp": other // nc, "ctx": lax.rem(other, nc)}

    def grad_copy(o):
        return pltpu.make_async_remote_copy(
            src_ref=grads.at[lax.rem(flat + o, peers)],
            dst_ref=grads_in.at[o],
            send_sem=send_grad.at[o],
            recv_sem=recv_grad.at[o],
            device_id=peer(o),
            device_id_type=MESH,
        )

    def gain_copy(o):
        return pltpu.make_async_remote_copy(
            src_ref=gains_in.at[0],
            dst_ref=gains_in.at[o],
            send_sem=send_gain.at[o],
            recv_sem=recv_gain.at[o],
            device_id=peer(o),
            device_id_type=MESH,
        )

    def kv_copy(s, part, o, rank):
        return pltpu.make_async_remote_copy(
            src_ref=dkv.at[s, places.rows(rank, part)],
            dst_ref=dkv_in.at[o - 1, s, part],
            send_sem=send_kv.at[o - 1, s, part],
            recv_sem=recv_kv.at[o - 1, s, part],
            device_id={"ctx": places.after(o)},
            device_id_type=MESH,
        )

    def finish_out(c, rows, total):
        moe_ref[rows] = total.astype(bf16)

    def finish_in(c, rows, total):
        x = x_ref[rows].astype(f32)
        scale = lax.rsqrt(jnp.mean(x * x, -1, keepdims=True) + epsilon)
        unit = x * scale
        scaled = total * gains_ref[:1]
        inner = jnp.mean(scaled * unit, -1, keepdims=True)
        own[rows] = (low_ref[rows].astype(f32) + scale * (scaled - unit * inner)).astype(bf16)
        dgain[...] += folded(total * unit)

    outward = Line(n, me, moe_ref, finish_out, scratch[:7], lag=1, hop=2)
    inward = Line(n, me, own, finish_in, scratch[7:], hop=2)
    dgain[...] = jnp.zeros_like(dgain)
    greet(me, n, [peer(o) for o in range(1, peers)])
    loads[0].wait()
    loop(0, outward.chunks, outward.offer)
    loads[1].wait()

    def turned_back(y, part):
        wide = y.shape[1]
        here = pl.ds(part * quarter, quarter)
        return y * widened(cos_ref[here], wide) - swapped_halves(y) * widened(sin_ref[here], wide)

    def attend(s):
        for part in (1, 0):
            rows = places.own(s, part)
            keys = places.keys(part)
            dmixed[...] = dot(low_ref[rows], wout_ref[...]).astype(bf16)
            start = places.slot(places.c, part) * quarter
            allowed = lax.broadcasted_iota(jnp.int32, (keys, quarter), 0) <= (
                start + lax.broadcasted_iota(jnp.int32, (keys, quarter), 1)
            )
            for k in range(kv_heads):
                at = k * HEAD_SIZE
                key = kv_ref[s, :keys, at : at + HEAD_SIZE]
                value = kv_ref[s, :keys, k_wide + at : k_wide + at + HEAD_SIZE]
                dkey = dvalue = None
                for h in range(k * group, (k + 1) * group):
                    head = slice(h * HEAD_SIZE, (h + 1) * HEAD_SIZE)
                    query = query_ref[rows, head]
                    dout = dmixed[:, head]
                    scores = jnp.where(allowed, dot(key, query, (1, 1)), -1e30)
                    raised = jnp.exp(scores - jnp.max(scores, 0, keepdims=True))
                    probs = raised * (1.0 / jnp.sum(raised, 0, keepdims=True))
                    product = probs * dot(value, dout, (1, 1))
                    dscores = product - probs * jnp.sum(product, 0, keepdims=True)
                    dscores = dscores.astype(bf16)
                    dquery[:, head] = dot(dscores, key, (0, 0)) * factor
                    dk, dv = dot(dscores, query), dot(probs.astype(bf16), dout)
                    dkey = dk if dkey is None else dkey + dk
                    dvalue = dv if dvalue is None else dvalue + dv
                for first, add in ((at, dkey), (k_wide + at, dvalue)):
                    lanes = slice(first, first + HEAD_SIZE)
                    if part == 1:
                        dkv[s, :keys, lanes] = add
                    else:
                        dkv[s, :keys, lanes] += add
                outward.step((2 * s + 1 - part) * kv_heads + k)
            dqkv_ref[rows, :q_wide] = turned_back(dquery[...], part).astype(bf16)
        for part in range(2):
            for o in range(1, nc):
                kv_copy(s, part, o, places.after(o)).start()

    loop(0, seqs, attend)
    done = 2 * seqs * kv_heads
    loads[2].wait()
    loads[3].wait()
    per = quarter // inward.size

    def turn_back(s):
        for part in range(2):
            rows = places.own(s, part)
            mine = dkv[s, places.rows(places.c, part)]
            for o in range(1, nc):
                kv_copy(s, part, o, places.after(o)).wait()
                mine = mine + dkv_in[o - 1, s, part]
            dqkv_ref[rows, q_wide : q_wide + k_wide] = turned_back(mine[:, :k_wide], part).astype(
                bf16
            )
            dqkv_ref[rows, q_wide + k_wide :] = mine[:, k_wide:].astype(bf16)
            own[rows] = dot(dqkv_ref[rows], wqkv_ref[...], (1, 1)).astype(bf16)
            first = (2 * s + part) * per
            loop(first, first + per, inward.offer)
            outward.step(done + 2 * s + part)
            x = x_ref[rows].astype(f32)
            scale = lax.rsqrt(jnp.mean(x * x, -1, keepdims=True) + epsilon)
            scales[rows] = jnp.broadcast_to(scale, (quarter, LANES))

    loop(0, seqs, turn_back)
    wide, mid = dqkv_ref.shape[1], dqkv_ref.shape[1] + mixed_ref.shape[1]
    span = max(LANES, shard * LANES // math.gcd(shard, LANES))
    count = span // shard

    def weights(i):
        at = aligned(i * span, span)
        to = pl.ds(i * count, count)

        def put(lanes, value):
            value = value.reshape(count, shard, value.shape[1])
            if padded > shard:
                more = jnp.zeros((count, padded - shard, value.shape[2]), f32)
                value = jnp.concatenate([value, more], 1)
            grads[to, :, lanes] = value.astype(bf16)

        normed = x_ref[:, at].astype(f32) * widened(scales[...], span) * gains_ref[:1, at]
        put(slice(0, wide), dot(normed.astype(bf16), dqkv_ref[...], (0, 0)))
        put(slice(wide, mid), dot(low_ref[:, at], mixed_ref[...], (0, 0)))
        put(slice(mid, grads.shape[2]), dot(normed_two_ref[:, at], dlogits_ref[...], (0, 0)))
        outward.step(done + 2 * seqs + i)

    spans = x_ref.shape[1] // span
    loop(0, spans, weights)
    loop(1, peers, lambda o: grad_copy(o).start())
    outward.rest(done + 2 * seqs + spans)
    stores = [
        pltpu.make_async_copy(source, target, store_sem.at[i])
        for i, (source, target) in enumerate(((moe_ref, act_hbm), (own, input_hbm)))
    ]
    stores[0].start()
    inward.rest(0)
    stores[1].start()
    one = jnp.sum(dgain[...], 0, keepdims=True)
    two = jnp.sum(dgain_two_ref[...], 0, keepdims=True)
    gains_in[0] = jnp.concatenate([one, two], 1)
    loop(1, peers, lambda o: gain_copy(o).start())
    grads_ref[...] = grads[flat].astype(f32)[:shard]

    def add_grad(o):
        grad_copy(o).wait()
        grads_ref[...] += grads_in[o].astype(f32)[:shard]

    loop(1, peers, add_grad)
    loop(1, peers, lambda o: gain_copy(o).wait())
    dgains_ref[...] = gains_in[0]

    def add(o):
        dgains_ref[...] += gains_in[o]

    loop(1, peers, add)
    for store in stores:
        store.wait()


def split_kernel(
    ffn,
    grads_ref,
    small_ref,
    out_hbm,
    input_hbm,
    gate_ref,
    up_ref,
    down_ref,
    query_ref,
    key_ref,
    value_ref,
    out_ref,
    router_ref,
    act_hbm,
    grad_hbm,
    act,
    grad,
    load,
    store,
):
    loads = [
        pltpu.make_async_copy(input_hbm, grad, load.at[0]),
        pltpu.make_async_copy(out_hbm, act, load.at[1]),
    ]
    stores = [
        pltpu.make_async_copy(grad, grad_hbm, store.at[0]),
        pltpu.make_async_copy(act, act_hbm, store.at[1]),
    ]
    for copy in loads:
        copy.start()
    gu_wide = 2 * E * ffn
    at = 0
    for ref in (query_ref, key_ref, value_ref, out_ref, router_ref):
        ref[...] = small_ref[:, at : at + ref.shape[1]]
        at += ref.shape[1]
    loads[0].wait()
    stores[0].start()
    loads[1].wait()
    stores[1].start()
    for e in range(E):
        at = (e // 2) * 4 * ffn + (e % 2) * ffn
        gate_ref[e] = grads_ref[:, at : at + ffn].astype(f32)
        up_ref[e] = grads_ref[:, at + 2 * ffn : at + 3 * ffn].astype(f32)
        at = gu_wide + e * ffn
        down_ref[e] = grads_ref[:, at : at + ffn].astype(f32)
    for copy in stores:
        copy.wait()


def call(kernel, outs, scratch, collective_id, operands, flops=0):
    total = sum(math.prod(o.shape) * o.dtype.itemsize for o in [*outs, *operands])
    return pl.pallas_call(
        kernel,
        out_shape=tuple(outs),
        in_specs=[WHOLE] * len(operands),
        out_specs=tuple([WHOLE] * len(outs)),
        scratch_shapes=scratch,
        compiler_params=pltpu.CompilerParams(
            collective_id=collective_id, has_side_effects=True, vmem_limit_bytes=VMEM_BYTES
        ),
        cost_estimate=pl.CostEstimate(flops=flops, bytes_accessed=total, transcendentals=0),
    )(*operands)


def per_device(
    tokens,
    routes,
    gain_attn,
    w_query,
    key_matrix,
    value_matrix,
    w_out,
    gain_moe,
    w_router,
    w_gate,
    w_up,
    w_down,
    cotangent,
):
    shaped = jax.ShapeDtypeStruct
    rows, width = tokens.shape
    nc, n = lax.axis_size("ctx"), lax.axis_size("tp")
    half = SEQUENCE_LENGTH // nc
    seqs = rows // half
    both = ("fsdp", "ctx")
    cos, sin = angle_tables(placed(lax.axis_index("ctx"), half))
    q_wide, k_wide, o_wide = w_query.shape[1], key_matrix.shape[1], w_out.shape[0]
    qkv_wide = q_wide + 2 * k_wide
    ffn = w_gate.shape[2]
    shard = w_gate.shape[1]

    gu_wide, down_wide = 2 * E * ffn, E * ffn
    small_wide = qkv_wide + o_wide + LANES
    nf = lax.axis_size("fsdp")
    peers = nf * nc
    link = bf16 if shard % 16 == 0 else f32
    def sems(*dims):
        return pltpu.SemaphoreType.DMA(dims)

    wqkv, wout, router, gains, packed = call(
        functools.partial(gather_kernel, nf, nc, ffn),
        [
            shaped((width, qkv_wide), bf16),
            shaped((width, o_wide), bf16),
            shaped((width, LANES), bf16),
            shaped((8, width), f32),
            shaped((shard, gu_wide + down_wide), bf16),
        ],
        [
            pltpu.VMEM((peers, shard, small_wide), link),
            sems(nf),
            sems(nf),
            sems(nc - 1, nf),
            sems(nc - 1, nf),
        ],
        4,
        (
            w_query,
            key_matrix,
            value_matrix,
            w_out.T,
            w_router.T,
            gain_attn[None],
            gain_moe[None],
            w_gate,
            w_up,
            jnp.swapaxes(w_down, 1, 2),
        ),
    )
    experts = lax.all_gather(packed, both, axis=0, tiled=True)
    kv_sems = sems(nc - 1, seqs, 2)
    query, kv, mixed, state, normed_two, gates = call(
        functools.partial(front_kernel, n, nc),
        [
            shaped((rows, q_wide), bf16),
            shaped((seqs, SEQUENCE_LENGTH, 2 * k_wide), bf16),
            shaped((rows, q_wide), bf16),
            shaped((rows, width), bf16),
            shaped((rows, width), bf16),
            shaped((rows, LANES), f32),
        ],
        [
            pltpu.VMEM((seqs, SEQUENCE_LENGTH, 2 * k_wide), bf16),
            pltpu.VMEM((rows, width), bf16),
            kv_sems,
            kv_sems,
            *line_scratch(rows, width, 32),
        ],
        0,
        (tokens, wqkv, wout, router, gains, routes, cos, sin),
    )

    block = 256

    def by_rows(wide):
        return pl.BlockSpec((block, wide), lambda i: (i, 0))

    def constant(*dims):
        return pl.BlockSpec(
            dims, lambda i: (0,) * len(dims), pipeline_mode=pl.Buffered(1)
        )

    anywhere = pl.BlockSpec(memory_space=pl.ANY)
    blocks = rows // block
    size, tall = 64, 256
    dots_sems = pltpu.SemaphoreType.DMA((n - 1, blocks))
    moe_part, grad_experts, low, dlogits, dgain_two = pl.pallas_call(
        functools.partial(expert_kernel, n),
        grid=(blocks,),
        out_shape=(
            shaped((rows, width), bf16),
            shaped((width, gu_wide + down_wide), bf16),
            shaped((rows, width), bf16),
            shaped((rows, LANES), bf16),
            shaped((8, width), f32),
        ),
        in_specs=[
            constant(rows, width),
            constant(rows, width),
            constant(rows, LANES),
            anywhere,
            constant(rows, width),
            constant(width, LANES),
            constant(8, width),
        ],
        out_specs=(
            by_rows(width),
            anywhere,
            anywhere,
            pl.BlockSpec((rows, LANES), lambda i: (0, 0)),
            pl.BlockSpec((8, width), lambda i: (0, 0)),
        ),
        scratch_shapes=[
            pltpu.VMEM((rows, width), bf16),
            pltpu.VMEM((rows, down_wide), bf16),
            pltpu.VMEM((rows, gu_wide), bf16),
            pltpu.VMEM((tall, rows), bf16),
            pltpu.VMEM((tall, rows), bf16),
            pltpu.VMEM((block, LANES), f32),
            pltpu.VMEM((n, blocks, E, block), f32),
            pltpu.VMEM((rows, LANES), f32),
            pltpu.VMEM((width, gu_wide + down_wide), bf16),
            pltpu.VMEM((2, size, width), bf16),
            sems(2, E // 4),
            sems(width // tall),
            sems(2),
            dots_sems,
            dots_sems,
            *line_scratch(rows, width, size),
        ],
        compiler_params=pltpu.CompilerParams(
            collective_id=1, has_side_effects=True, vmem_limit_bytes=VMEM_BYTES
        ),
        cost_estimate=pl.CostEstimate(
            flops=18 * rows * width * down_wide,
            bytes_accessed=2 * width * (gu_wide + down_wide),
            transcendentals=0,
        ),
    )(normed_two, cotangent, gates, experts, state, router, gains)

    low, grad_experts = lax.optimization_barrier((low, grad_experts))
    grad_experts = lax.psum_scatter(grad_experts, both, scatter_dimension=0, tiled=True)

    small_block = pltpu.VMEM((peers, -(-shard // 16) * 16, small_wide), bf16)
    whole = pltpu.VMEM((rows, width), bf16)
    operands = (
        (moe_part, low, tokens, normed_two)
        + (wout, wqkv, query, kv, mixed, dlogits, gains, dgain_two, cos, sin)
    )
    activations, input_grad, dgains, grad_small = pl.pallas_call(
        functools.partial(rear_kernel, n, nf, nc),
        out_shape=(
            shaped((rows, width), bf16),
            shaped((rows, width), bf16),
            shaped((1, 2 * width), f32),
            shaped((shard, small_wide), f32),
        ),
        in_specs=[anywhere] * 4 + [WHOLE] * (len(operands) - 4),
        out_specs=(anywhere, anywhere, WHOLE, WHOLE),
        scratch_shapes=[
            whole,
            whole,
            whole,
            whole,
            pltpu.VMEM((half // 2, q_wide), bf16),
            pltpu.VMEM((half // 2, q_wide), f32),
            pltpu.VMEM((seqs, SEQUENCE_LENGTH, 2 * k_wide), f32),
            pltpu.VMEM((nc - 1, seqs, 2, half // 2, 2 * k_wide), f32),
            pltpu.VMEM((rows, qkv_wide), bf16),
            whole,
            pltpu.VMEM((rows, LANES), f32),
            pltpu.VMEM((8, width), f32),
            pltpu.VMEM((peers, 1, 2 * width), f32),
            small_block,
            small_block,
            sems(4),
            sems(2),
            kv_sems,
            kv_sems,
            *[sems(peers)] * 4,
            *line_scratch(rows, width, size),
            *line_scratch(rows, width, 32),
        ],
        compiler_params=pltpu.CompilerParams(
            collective_id=3, has_side_effects=True, vmem_limit_bytes=VMEM_BYTES
        ),
        cost_estimate=pl.CostEstimate(
            flops=12 * rows * width * small_wide,
            bytes_accessed=16 * rows * width,
            transcendentals=0,
        ),
    )(*operands)
    flat = lax.axis_index("fsdp") * nc + lax.axis_index("ctx")
    dgains = lax.dynamic_slice_in_dim(dgains.reshape(2, width), flat * shard, shard, 1)
    results = pl.pallas_call(
        functools.partial(split_kernel, ffn),
        out_shape=(
            shaped((E, shard, ffn), f32),
            shaped((E, shard, ffn), f32),
            shaped((E, shard, ffn), f32),
            shaped((shard, q_wide), f32),
            shaped((shard, k_wide), f32),
            shaped((shard, k_wide), f32),
            shaped((shard, o_wide), f32),
            shaped((shard, E), f32),
            shaped((rows, width), bf16),
            shaped((rows, width), bf16),
        ),
        in_specs=[WHOLE, WHOLE, anywhere, anywhere],
        out_specs=(*[WHOLE] * 8, anywhere, anywhere),
        scratch_shapes=[
            pltpu.VMEM((rows, width), bf16),
            pltpu.VMEM((rows, width), bf16),
            sems(2),
            sems(2),
        ],
        compiler_params=pltpu.CompilerParams(vmem_limit_bytes=VMEM_BYTES),
    )(grad_experts, grad_small, activations, input_grad)
    grad_gate, grad_up, grad_down, grad_query, grad_key, grad_value, grad_out, grad_router = results[:8]
    return (
        results[8],
        results[9],
        dgains[0],
        grad_query,
        grad_key,
        grad_value,
        grad_out.T,
        dgains[1],
        grad_router,
        grad_gate,
        grad_up,
        jnp.swapaxes(grad_down, 1, 2),
    )


def solution(mesh):
    specs = (
        P(("fsdp", "ctx"), None),
        P(("fsdp", "ctx"), None),
        P(("fsdp", "ctx")),
        P(("fsdp", "ctx"), "tp"),
        P(("fsdp", "ctx"), "tp"),
        P(("fsdp", "ctx"), "tp"),
        P("tp", ("fsdp", "ctx")),
        P(("fsdp", "ctx")),
        P(("fsdp", "ctx"), None),
        P(None, ("fsdp", "ctx"), "tp"),
        P(None, ("fsdp", "ctx"), "tp"),
        P(None, "tp", ("fsdp", "ctx")),
        P(("fsdp", "ctx"), None),
    )
    return jax.shard_map(
        per_device,
        mesh=mesh,
        in_specs=specs,
        out_specs=(
            P(("fsdp", "ctx"), None),
            P(("fsdp", "ctx"), None),
            P(("fsdp", "ctx")),
            P(("fsdp", "ctx"), "tp"),
            P(("fsdp", "ctx"), "tp"),
            P(("fsdp", "ctx"), "tp"),
            P("tp", ("fsdp", "ctx")),
            P(("fsdp", "ctx")),
            P(("fsdp", "ctx"), None),
            P(None, ("fsdp", "ctx"), "tp"),
            P(None, ("fsdp", "ctx"), "tp"),
            P(None, "tp", ("fsdp", "ctx")),
        ),
        check_vma=False,
    )
```

```python
import functools
import math

import jax
import jax.numpy as jnp
from jax import lax
from jax.experimental import pallas as pl
from jax.experimental.pallas import tpu as pltpu
from jax.sharding import PartitionSpec as P

HEAD_SIZE = 64
TOPK = 8
E = 16
SEQUENCE_LENGTH = 1024
LANES = 128
VMEM_BYTES = 60 * 2**20

epsilon = 1e-06
f32 = jnp.float32
bf16 = jnp.bfloat16
MESH = pl.DeviceIdType.MESH
WHOLE = pl.BlockSpec(memory_space=pltpu.VMEM)


def placed(ranks, half):
    quarter = half // 2
    steps = jnp.arange(half, dtype=jnp.int32)
    early = ranks * quarter + steps
    late = SEQUENCE_LENGTH - (ranks + 1) * quarter + steps - quarter
    return jnp.where(steps < quarter, early, late)


def angle_tables(token_places):
    halfway = HEAD_SIZE // 2
    lanes = jnp.arange(LANES, dtype=jnp.int32) % halfway
    freqs = jnp.exp(lanes.astype(f32) * (-2.0 * math.log(10000.0) / HEAD_SIZE))
    angles = token_places.astype(f32)[:, None] * freqs[None, :]
    return jnp.cos(angles), jnp.sin(angles)


def aligned(start, size):
    return pl.ds(pl.multiple_of(start, size), size)


def dot(a, b, at=(1, 0)):
    return lax.dot_general(a, b, (((at[0],), (at[1],)), ((), ())), preferred_element_type=f32)


def swapped_halves(y):
    wide, halfway = y.shape[1], HEAD_SIZE // 2
    lane = lax.broadcasted_iota(jnp.int32, y.shape, 1)
    lower = lax.rem(lane, HEAD_SIZE) < halfway
    return jnp.where(lower, -pltpu.roll(y, wide - halfway, 1), pltpu.roll(y, halfway, 1))


def widened(table, wide):
    return jnp.concatenate([table] * (wide // LANES), 1)


SLOTS = 4


def line_scratch(rows, width, size):
    sems = pltpu.SemaphoreType.DMA((rows // size,))
    slots = pltpu.VMEM((SLOTS * size, width), bf16)
    return [pltpu.VMEM((2 * rows, width), bf16), slots, slots, *[sems] * 4]


def greet(me, n, others=()):
    barrier = pltpu.get_barrier_semaphore()

    @pl.when(me > 0)
    def _():
        pl.semaphore_signal(
            barrier, inc=1, device_id={"tp": lax.rem(me + n - 1, n)}, device_id_type=MESH
        )

    @pl.when(me < n - 1)
    def _():
        pl.semaphore_signal(
            barrier, inc=1, device_id={"tp": lax.rem(me + 1, n)}, device_id_type=MESH
        )

    for other in others:
        pl.semaphore_signal(barrier, inc=1, device_id=other, device_id_type=MESH)
    count = jnp.where(me > 0, 1, 0) + jnp.where(me < n - 1, 1, 0) + len(others)
    pl.semaphore_wait(barrier, count)


class Line:
    def __init__(self, n, me, own, finish, scratch, lag=0, hop=1, late=0):
        self.n, self.me, self.own, self.finish = n, me, own, finish
        self.arrived, self.to_right, self.to_left = scratch[:3]
        self.send_right, self.recv_left, self.send_left, self.recv_right = scratch[3:]
        self.size = self.to_right.shape[0] // SLOTS
        self.total = self.arrived.shape[0] // 2
        self.chunks = self.total // self.size
        self.lag, self.hop, self.late = lag, hop, late
        self.steps = self.chunks + lag + hop * (n - 2) + late
        self.middle = (me > 0) & (me < n - 1)

    def rows(self, c):
        return aligned(c * self.size, self.size)

    def left_rows(self, c):
        return aligned(c * self.size, self.size)

    def right_rows(self, c):
        return aligned(self.total + c * self.size, self.size)

    def slot(self, c):
        return aligned(lax.rem(c, SLOTS) * self.size, self.size)

    def right(self, c, end=False):
        return pltpu.make_async_remote_copy(
            src_ref=self.own.at[self.rows(c)] if end else self.to_right.at[self.slot(c)],
            dst_ref=self.arrived.at[self.left_rows(c)],
            send_sem=self.send_right.at[c],
            recv_sem=self.recv_left.at[c],
            device_id={"tp": lax.rem(self.me + 1, self.n)},
            device_id_type=MESH,
        )

    def left(self, c, end=False):
        return pltpu.make_async_remote_copy(
            src_ref=self.own.at[self.rows(c)] if end else self.to_left.at[self.slot(c)],
            dst_ref=self.arrived.at[self.right_rows(c)],
            send_sem=self.send_left.at[c],
            recv_sem=self.recv_right.at[c],
            device_id={"tp": lax.rem(self.me + self.n - 1, self.n)},
            device_id_type=MESH,
        )

    def offer(self, c):
        @pl.when(self.me == 0)
        def _():
            self.right(c, True).start()

        @pl.when(self.me == self.n - 1)
        def _():
            self.left(c, True).start()

    def step(self, t):
        n, me, chunks = self.n, self.me, self.chunks
        go, come = t - self.lag - self.hop * (me - 1), t - self.lag - self.hop * (n - 2 - me)
        done = jnp.minimum(go, come) - jnp.where(self.middle, 0, self.late)
        nearer_left = me < n - 1 - me

        def inside(c):
            return (c >= 0) & (c < chunks)

        @pl.when(self.middle & inside(go) & nearer_left)
        def _():
            self.right_pass(go)

        @pl.when(self.middle & inside(come))
        def _():
            self.left_pass(come)

        @pl.when(self.middle & inside(go) & jnp.logical_not(nearer_left))
        def _():
            self.right_pass(go)

        @pl.when(inside(done))
        def _():
            @pl.when(me == 0)
            def _():
                self.left(done).wait_recv()
                self.right(done, True).wait_send()

            @pl.when(me == n - 1)
            def _():
                self.right(done).wait_recv()
                self.left(done, True).wait_send()

            rows = self.rows(done)
            at = done * self.size
            one = aligned(jnp.where(me == 0, self.total, 0) + at, self.size)
            two = aligned(jnp.where(me == n - 1, 0, self.total) + at, self.size)
            total = self.own[rows].astype(f32) + self.arrived[one].astype(f32)
            other = self.arrived[two].astype(f32)
            self.finish(done, rows, total + jnp.where(self.middle, other, 0.0))

    def right_pass(self, c):
        self.right(c).wait_recv()

        @pl.when(c >= SLOTS)
        def _():
            self.right(c - SLOTS).wait_send()

        total = self.own[self.rows(c)].astype(f32) + self.arrived[self.left_rows(c)].astype(f32)
        self.to_right[self.slot(c)] = total.astype(bf16)
        self.right(c).start()

    def left_pass(self, c):
        self.left(c).wait_recv()

        @pl.when(c >= SLOTS)
        def _():
            self.left(c - SLOTS).wait_send()

        total = self.own[self.rows(c)].astype(f32) + self.arrived[self.right_rows(c)].astype(f32)
        self.to_left[self.slot(c)] = total.astype(bf16)
        self.left(c).start()

    def rest(self, start):
        loop(start, self.steps, self.step)

        @pl.when(self.middle)
        def _():
            def sent(c):
                self.right(c).wait_send()
                self.left(c).wait_send()

            loop(max(self.chunks - SLOTS, 0), self.chunks, sent)


def loop(low, high, body):
    lax.fori_loop(low, high, lambda i, carry: (body(i), carry)[1], 0)


def folded(values):
    rows, width = values.shape
    return jnp.sum(values.reshape(rows // 8, 8, width), 0)


class Places:
    def __init__(self, nc):
        self.nc = nc
        self.c = lax.axis_index("ctx")
        self.quarter = SEQUENCE_LENGTH // nc // 2

    def slot(self, rank, part):
        return rank if part == 0 else 2 * self.nc - 1 - rank

    def rows(self, rank, part):
        return aligned(self.slot(rank, part) * self.quarter, self.quarter)

    def own(self, s, part):
        return aligned((2 * s + part) * self.quarter, self.quarter)

    def keys(self, part):
        return self.quarter * (self.nc if part == 0 else 2 * self.nc)

    def after(self, o):
        return lax.rem(self.c + o, self.nc)

    def before(self, o):
        return lax.rem(self.c + self.nc - o, self.nc)


def gather_kernel(
    nf,
    nc,
    ffn,
    query_ref,
    key_ref,
    value_ref,
    out_ref,
    router_ref,
    gain_one_ref,
    gain_two_ref,
    gate_ref,
    up_ref,
    down_ref,
    small_all,
    gains_ref,
    experts_ref,
    send_f,
    recv_f,
    send_c,
    recv_c,
):
    f, c = lax.axis_index("fsdp"), lax.axis_index("ctx")
    shard = small_all.shape[1]
    kind = small_all.dtype
    mine = f * nc + c

    def from_f(o):
        return lax.rem(f + nf - o, nf)

    def to_peer(o):
        return {"fsdp": lax.rem(f + o, nf)}

    def to_near(p):
        return {"ctx": lax.rem(c + p, nc)}

    barrier = pltpu.get_barrier_semaphore()
    for other in [to_peer(o) for o in range(1, nf)] + [to_near(p) for p in range(1, nc)]:
        pl.semaphore_signal(barrier, inc=1, device_id=other, device_id_type=MESH)
    gains = [g[...].astype(f32).reshape(1, shard) for g in (gain_one_ref, gain_two_ref)]
    blank = jnp.zeros((LANES - E - 2, shard), f32)
    last = jnp.concatenate([router_ref[...].astype(f32), *gains, blank], 0).T
    at = 0
    for piece in (query_ref[...], key_ref[...], value_ref[...], out_ref[...], last):
        small_all[mine, :, at : at + piece.shape[1]] = piece.astype(kind)
        at += piece.shape[1]
    pl.semaphore_wait(barrier, nf + nc - 2)

    def far_copy(o, rank):
        block = small_all.at[rank * nc + c]
        return pltpu.make_async_remote_copy(
            src_ref=block,
            dst_ref=block,
            send_sem=send_f.at[o],
            recv_sem=recv_f.at[o],
            device_id=to_peer(o),
            device_id_type=MESH,
        )

    def near_copy(p, o, rank):
        block = small_all.at[from_f(o) * nc + rank]
        return pltpu.make_async_remote_copy(
            src_ref=block,
            dst_ref=block,
            send_sem=send_c.at[p - 1, o],
            recv_sem=recv_c.at[p - 1, o],
            device_id=to_near(p),
            device_id_type=MESH,
        )

    def share(o):
        for p in range(1, nc):
            near_copy(p, o, c).start()

    loop(1, nf, lambda o: far_copy(o, f).start())
    share(0)
    for e in range(E):
        at = (e // 2) * 4 * ffn + (e % 2) * ffn
        experts_ref[:, at : at + ffn] = gate_ref[e]
        experts_ref[:, at + 2 * ffn : at + 3 * ffn] = up_ref[e]
        at = 2 * E * ffn + e * ffn
        experts_ref[:, at : at + ffn] = down_ref[e]

    def pass_on(o):
        far_copy(o, from_f(o)).wait_recv()
        share(o)

    loop(1, nf, pass_on)

    def shared(o):
        for p in range(1, nc):
            near_copy(p, o, lax.rem(c + nc - p, nc)).wait_recv()

    loop(0, nf, shared)
    last = small_all[:, :, small_all.shape[2] - LANES :]
    gains_ref[...] = last.reshape(nf * nc * shard, LANES).astype(f32).T[E : E + 8]
    loop(1, nf, lambda o: far_copy(o, f).wait_send())

    def near_sent(o):
        for p in range(1, nc):
            near_copy(p, o, c).wait_send()

    loop(0, nf, near_sent)


def front_kernel(
    n,
    nc,
    x_ref,
    small_ref,
    gains_ref,
    routes_ref,
    cos_ref,
    sin_ref,
    query_ref,
    kv_ref,
    mixed_ref,
    state_hbm,
    normed_hbm,
    gates_ref,
    kv_all,
    own,
    state_ref,
    normed_ref,
    store_sem,
    send_kv,
    recv_kv,
    *scratch,
):
    me = lax.axis_index("tp")
    places = Places(nc)
    quarter = places.quarter
    seqs = kv_ref.shape[0]
    q_wide, k_wide = query_ref.shape[1], kv_ref.shape[2] // 2
    group = q_wide // k_wide
    qkv_wide = q_wide + 2 * k_wide
    wide = small_ref.shape[1] - LANES

    def row_stores(c):
        rows = line.rows(c)
        pairs = ((state_ref, state_hbm), (normed_ref, normed_hbm))
        return [
            pltpu.make_async_copy(source.at[rows], target.at[rows], store_sem.at[i, c])
            for i, (source, target) in enumerate(pairs)
        ]

    def finish(c, rows, total):
        state = x_ref[rows].astype(f32) + total
        scale = lax.rsqrt(jnp.mean(state * state, -1, keepdims=True) + epsilon)
        normed = (state * scale * gains_ref[1:2]).astype(bf16)
        state_ref[rows] = state.astype(bf16)
        normed_ref[rows] = normed
        for copy in row_stores(c):
            copy.start()
        routes = routes_ref[rows]
        lane = lax.broadcasted_iota(jnp.int32, (line.size, LANES), 1)
        named = lane == routes[:, :1]
        for k in range(1, TOPK):
            named = named | (lane == routes[:, k : k + 1])
        logits = jnp.where(named, dot(normed, small_ref[:, wide:]), -1e30)
        top = jnp.max(logits, -1, keepdims=True)
        raised = jnp.where(named, jnp.exp(logits - top), 0.0)
        gates_ref[rows] = raised / jnp.sum(raised, -1, keepdims=True)

    line = Line(n, me, own, finish, scratch, hop=2, late=quarter // 16)
    greet(me, n, [{"ctx": places.after(o)} for o in range(1, nc)])

    def kv_copy(s, part, o, rank):
        where = kv_all.at[s, places.rows(rank, part)]
        return pltpu.make_async_remote_copy(
            src_ref=where,
            dst_ref=where,
            send_sem=send_kv.at[o - 1, s, part],
            recv_sem=recv_kv.at[o - 1, s, part],
            device_id={"ctx": places.after(o)},
            device_id_type=MESH,
        )

    def project(s):
        for part in range(2):
            rows = places.own(s, part)
            x = x_ref[rows].astype(f32)
            scale = lax.rsqrt(jnp.mean(x * x, -1, keepdims=True) + epsilon)
            normed = (x * scale * gains_ref[:1]).astype(bf16)
            qkv = dot(normed, small_ref[:, :qkv_wide])
            qk = qkv[:, : q_wide + k_wide]
            here = pl.ds(part * quarter, quarter)
            cos, sin = widened(cos_ref[here], q_wide + k_wide), widened(sin_ref[here], q_wide + k_wide)
            rot = qk * cos + swapped_halves(qk) * sin
            query_ref[rows] = (rot[:, :q_wide] * (1.0 / math.sqrt(HEAD_SIZE))).astype(bf16)
            slot = places.rows(places.c, part)
            kv_all[s, slot, :k_wide] = rot[:, q_wide:].astype(bf16)
            kv_all[s, slot, k_wide:] = qkv[:, q_wide + k_wide :].astype(bf16)
            for o in range(1, nc):
                kv_copy(s, part, o, places.c).start()

    loop(0, seqs, project)

    def attend(s):
        for part in range(2):
            for o in range(1, nc):
                kv_copy(s, part, o, places.before(o)).wait_recv()
        for part in range(2):
            rows = places.own(s, part)
            keys = places.keys(part)
            base = places.slot(places.c, part) * quarter
            allowed = lax.broadcasted_iota(jnp.int32, (quarter, keys), 1) <= (
                base + lax.broadcasted_iota(jnp.int32, (quarter, keys), 0)
            )
            for h in range(q_wide // HEAD_SIZE):
                at = h // group * HEAD_SIZE
                query = query_ref[rows, h * HEAD_SIZE : (h + 1) * HEAD_SIZE]
                key = kv_all[s, :keys, at : at + HEAD_SIZE]
                value = kv_all[s, :keys, k_wide + at : k_wide + at + HEAD_SIZE]
                scores = jnp.where(allowed, dot(query, key, (1, 1)), -1e30)
                raised = jnp.exp(scores - jnp.max(scores, -1, keepdims=True))
                probs = (raised * (1.0 / jnp.sum(raised, -1, keepdims=True))).astype(bf16)
                mixed_ref[rows, h * HEAD_SIZE : (h + 1) * HEAD_SIZE] = dot(probs, value).astype(bf16)
            own[rows] = dot(mixed_ref[rows], small_ref[:, qkv_wide:wide], (1, 1)).astype(bf16)
            per = quarter // line.size
            first = (2 * s + part) * per
            loop(first, first + per, line.offer)
            loop(first, first + per, line.step)

    loop(0, seqs, attend)
    kv_ref[...] = kv_all[...]
    line.rest(line.chunks)

    def stored(c):
        for copy in row_stores(c):
            copy.wait()

    loop(0, line.chunks, stored)

    def kv_sent(s):
        for part in range(2):
            for o in range(1, nc):
                kv_copy(s, part, o, places.c).wait_send()

    loop(0, seqs, kv_sent)


def expert_kernel(
    n,
    x_hbm,
    dy_hbm,
    gates_ref,
    w_hbm,
    state_hbm,
    router_ref,
    gains_ref,
    out_ref,
    grads_hbm,
    dstate_hbm,
    dlogits_ref,
    dgain_ref,
    x_ref,
    dy_ref,
    state_ref,
    own,
    hidden_ref,
    grad_ref,
    x_turned,
    dy_turned,
    dots,    dots_all,
    dots_rows,
    w_ref,
    dstate_out,
    row_sem,
    w_sem,
    grads_sem,
    dstate_sem,
    send_dots,
    recv_dots,
    *scratch,
):
    me = lax.axis_index("tp")
    block, steps = pl.program_id(0), pl.num_programs(0)
    size_in, width = out_ref.shape
    pair = hidden_ref.shape[1] // (E // 2)
    single = pair // 2
    gu_wide = grad_ref.shape[1]
    here = aligned(block * size_in, size_in)

    def dots_copy(o, b):
        mine = dots_all.at[me, b]
        return pltpu.make_async_remote_copy(
            src_ref=mine,
            dst_ref=mine,
            send_sem=send_dots.at[o - 1, b],
            recv_sem=recv_dots.at[o - 1, b],
            device_id={"tp": lax.rem(me + o, n)},
            device_id_type=MESH,
        )

    def w_copies(p):
        spans = (aligned(p * 4 * pair, 4 * pair), aligned(gu_wide + p * 2 * pair, 2 * pair))
        return [
            pltpu.make_async_copy(w_hbm.at[:, span], w_ref.at[:, span], w_sem.at[i, p])
            for i, span in enumerate(spans)
        ]

    def row_copy(i, b):
        source, target = ((x_hbm, x_ref), (dy_hbm, dy_ref), (state_hbm, state_ref))[i]
        rows = aligned(b * size_in, size_in)
        return pltpu.make_async_copy(source.at[rows], target.at[rows], row_sem.at[i, b])

    def fetch_rows(b):
        row_copy(0, b).start()
        row_copy(1, b).start()

    def fetch_pair(i):
        for copy in w_copies(i):
            copy.start()

    def dstate_copy(c):
        return pltpu.make_async_copy(
            dstate_out.at[lax.rem(c, 2)], dstate_hbm.at[line.rows(c)], dstate_sem.at[lax.rem(c, 2)]
        )

    def finish(c, rows, total):
        per = size_in // line.size

        @pl.when(lax.rem(c, per) == 0)
        def _():
            b = c // per
            for o in range(1, n):
                dots_copy(o, b).wait_recv()
            summed = dots_all[0, b]
            for i in range(1, n):
                summed = summed + dots_all[i, b]
            summed = jnp.concatenate(
                [summed, jnp.zeros((LANES - summed.shape[0], summed.shape[1]), f32)], 0
            )
            dots_rows[aligned(b * size_in, size_in)] = summed.T

        @pl.when(c >= 2)
        def _():
            dstate_copy(c - 2).wait()

        gates = gates_ref[rows]
        lane = lax.broadcasted_iota(jnp.int32, gates.shape, 1)
        product = gates * dots_rows[rows]
        dlogits = product - gates * jnp.sum(product, -1, keepdims=True)
        dlogits = jnp.where(lane < E, dlogits, 0.0).astype(bf16)
        dlogits_ref[rows] = dlogits
        dn = total + dot(dlogits, router_ref[...], (1, 1))
        state = state_ref[rows].astype(f32)
        scale = lax.rsqrt(jnp.mean(state * state, -1, keepdims=True) + epsilon)
        unit = state * scale
        scaled = dn * gains_ref[1:2]
        inner = jnp.mean(scaled * unit, -1, keepdims=True)
        dstate = dy_ref[rows].astype(f32) + scale * (scaled - unit * inner)
        dstate_out[lax.rem(c, 2)] = dstate.astype(bf16)
        dstate_copy(c).start()
        dgain_ref[...] += folded(dn * unit)

    line = Line(n, me, own, finish, scratch, lag=size_in // (scratch[1].shape[0] // SLOTS), hop=2)
    per = size_in // line.size

    @pl.when(block == 0)
    def _():
        fetch_rows(0)
        fetch_pair(0)
        fetch_pair(1)
        barrier = pltpu.get_barrier_semaphore()
        for o in range(1, n):
            pl.semaphore_signal(
                barrier, inc=1, device_id={"tp": lax.rem(me + o, n)}, device_id_type=MESH
            )
        pl.semaphore_wait(barrier, n - 1)
        dgain_ref[...] = jnp.zeros_like(dgain_ref)


    lane = lax.broadcasted_iota(jnp.int32, (size_in, LANES), 1)
    first = lax.broadcasted_iota(jnp.int32, (size_in, pair), 1) < single
    dots[...] = jnp.zeros_like(dots)
    row_copy(0, block).wait()
    row_copy(1, block).wait()

    def gating(p, gate_pre, up_pre, raw):
        gates = gates_ref[here]
        gate = jnp.where(
            first,
            jnp.sum(jnp.where(lane == 2 * p, gates, 0.0), 1, keepdims=True),
            jnp.sum(jnp.where(lane == 2 * p + 1, gates, 0.0), 1, keepdims=True),
        )
        sigma = jax.nn.sigmoid(gate_pre)
        silu = gate_pre * sigma
        hidden = (silu * up_pre).astype(bf16).astype(f32)
        hidden_ref[here, aligned(p * pair, pair)] = (hidden * gate).astype(bf16)
        both = hidden * raw
        dots[...] += jnp.where(
            lane == 2 * p, jnp.sum(both[:, :single], 1, keepdims=True), 0.0
        ) + jnp.where(lane == 2 * p + 1, jnp.sum(both[:, single:], 1, keepdims=True), 0.0)
        dh = raw * gate
        grad_ref[here, aligned(p * 2 * pair, pair)] = (
            dh * up_pre * (sigma + silu * (1.0 - sigma))
        ).astype(bf16)
        grad_ref[here, aligned(p * 2 * pair + pair, pair)] = (dh * silu).astype(bf16)

    def two_pairs(i):
        @pl.when(block == 0)
        def _():
            for copy in w_copies(i):
                copy.wait()

            @pl.when(i + 2 < E // 4)
            def _():
                fetch_pair(i + 2)

            @pl.when(i == E // 4 - 2)
            def _():
                loop(1, steps, fetch_rows)
                loop(0, steps, lambda b: row_copy(2, b).start())

        gu = dot(x_ref[here], w_ref[:, aligned(i * 4 * pair, 4 * pair)])
        raw = dot(dy_ref[here], w_ref[:, aligned(gu_wide + i * 2 * pair, 2 * pair)])
        for j in range(2):
            at = 2 * j * pair
            gating(
                2 * i + j,
                gu[:, at : at + pair],
                gu[:, at + pair : at + 2 * pair],
                raw[:, j * pair : (j + 1) * pair],
            )

    tile = 512

    def back(i):
        at = aligned(i * tile, tile)
        own[here, at] = dot(grad_ref[here], w_ref[at, :gu_wide], (1, 1)).astype(bf16)

    def outward(i):
        at = aligned(i * tile, tile)
        carried = jnp.where(me == n // 2, state_ref[here, at].astype(f32), 0.0)
        moe = dot(hidden_ref[here], w_ref[at, gu_wide:], (1, 1))
        out_ref[:, at] = (moe + carried).astype(bf16)

    unit = per // 4
    tiles = width // tile

    def steps_at(i):
        first = block * per + i * unit
        loop(first, first + unit, line.step)

    for i in range(2):
        loop(i * (E // 8), (i + 1) * (E // 8), two_pairs)
        steps_at(i)
    dots_all[me, block] = dots[...].T[:E]
    for o in range(1, n):
        dots_copy(o, block).start()
    loop(0, tiles, back)
    loop(block * per, block * per + per, line.offer)
    steps_at(2)
    row_copy(2, block).wait()
    loop(0, tiles, outward)
    steps_at(3)

    @pl.when(block == steps - 1)
    def _():
        tall = x_turned.shape[0]
        count = width // tall
        wide = 4 * pair

        def grads_copy(m):
            rows = aligned(m * tall, tall)
            return pltpu.make_async_copy(w_ref.at[rows], grads_hbm.at[rows], grads_sem.at[m])

        def gradients(m):
            at = aligned(m * tall, tall)
            x_turned[...] = x_ref[:, at].T
            dy_turned[...] = dy_ref[:, at].T
            for i in range(gu_wide // wide):
                to = slice(i * wide, (i + 1) * wide)
                w_ref[at, to] = dot(x_turned[...], grad_ref[:, to]).astype(bf16)
            for i in range(gu_wide // wide // 2):
                to = slice(i * wide, (i + 1) * wide)
                w_ref[at, gu_wide + i * wide : gu_wide + (i + 1) * wide] = dot(
                    dy_turned[...], hidden_ref[:, to]
                ).astype(bf16)
            grads_copy(m).start()
            loop(steps * per + m * unit, steps * per + (m + 1) * unit, line.step)

        loop(0, count, gradients)
        line.rest(steps * per + count * unit)
        for c in range(line.chunks - 2, line.chunks):
            dstate_copy(c).wait()

        def dots_sent(b):
            for o in range(1, n):
                dots_copy(o, b).wait_send()

        loop(0, steps, dots_sent)
        loop(0, count, lambda m: grads_copy(m).wait())


def rear_kernel(
    n,
    nf,
    nc,
    moe_hbm,
    low_hbm,
    small_hbm,
    query_hbm,
    kv_hbm,
    x_hbm,
    normed_two_hbm,
    mixed_hbm,
    dlogits_hbm,
    gains_ref,
    dgain_two_ref,
    cos_ref,
    sin_ref,
    act_hbm,
    input_hbm,
    dgains_ref,
    grads_ref,
    moe_ref,
    low_ref,
    wout_ref,
    query_ref,
    kv_ref,
    wqkv_ref,
    x_ref,
    normed_two_ref,
    mixed_ref,
    dlogits_ref,
    dmixed,
    dquery,
    dkv,
    dkv_in,
    dqkv_ref,
    own,
    scales,
    dgain,
    gains_in,
    grads,
    grads_near,
    grads_far,
    moe_sem,
    load_sem,
    store_sem,
    send_kv,
    recv_kv,
    send_gain,
    recv_gain,
    send_near,
    recv_near,
    send_far,
    recv_far,
    *scratch,
):
    me = lax.axis_index("tp")
    flat = lax.axis_index("fsdp") * nc + lax.axis_index("ctx")
    places = Places(nc)
    quarter = places.quarter
    seqs = kv_ref.shape[0]
    q_wide, k_wide = query_ref.shape[1], kv_ref.shape[2] // 2
    group = q_wide // k_wide
    qkv_wide = q_wide + 2 * k_wide
    kv_heads = k_wide // HEAD_SIZE
    factor = 1.0 / math.sqrt(HEAD_SIZE)
    peers, padded = grads.shape[:2]
    shard = grads_ref.shape[0]
    loads = [
        pltpu.make_async_copy(source, target, load_sem.at[i])
        for i, (source, target) in enumerate(
            (
                (low_hbm, low_ref),
                (small_hbm.at[:, pl.ds(qkv_wide, wout_ref.shape[1])], wout_ref),
                (query_hbm, query_ref),
                (kv_hbm, kv_ref),
                (small_hbm.at[:, pl.ds(0, qkv_wide)], wqkv_ref),
                (x_hbm, x_ref),
                (normed_two_hbm, normed_two_ref),
                (mixed_hbm, mixed_ref),
                (dlogits_hbm, dlogits_ref),
            )
        )
    ]
    portions = moe_sem.shape[0]
    portion = moe_ref.shape[0] // portions

    def moe_load(i):
        rows = aligned(i * portion, portion)
        return pltpu.make_async_copy(moe_hbm.at[rows], moe_ref.at[rows], moe_sem.at[i])

    loop(0, portions, lambda i: moe_load(i).start())

    def peer(o):
        other = lax.rem(flat + o, peers)
        return {"fsdp": other // nc, "ctx": lax.rem(other, nc)}

    f = lax.axis_index("fsdp")

    def near_copy(p, g):
        return pltpu.make_async_remote_copy(
            src_ref=grads.at[g * nc + places.after(p)],
            dst_ref=grads_near.at[p - 1, g],
            send_sem=send_near.at[p - 1, g],
            recv_sem=recv_near.at[p - 1, g],
            device_id={"ctx": places.after(p)},
            device_id_type=MESH,
        )

    def far_copy(o):
        other = lax.rem(f + o, nf)
        return pltpu.make_async_remote_copy(
            src_ref=grads.at[other * nc + places.c],
            dst_ref=grads_far.at[o],
            send_sem=send_far.at[o],
            recv_sem=recv_far.at[o],
            device_id={"fsdp": other},
            device_id_type=MESH,
        )

    def gain_copy(o):
        return pltpu.make_async_remote_copy(
            src_ref=gains_in.at[0],
            dst_ref=gains_in.at[o],
            send_sem=send_gain.at[o],
            recv_sem=recv_gain.at[o],
            device_id=peer(o),
            device_id_type=MESH,
        )

    def kv_copy(s, part, o, rank):
        return pltpu.make_async_remote_copy(
            src_ref=dkv.at[s, places.rows(rank, part)],
            dst_ref=dkv_in.at[o - 1, s, part],
            send_sem=send_kv.at[o - 1, s, part],
            recv_sem=recv_kv.at[o - 1, s, part],
            device_id={"ctx": places.after(o)},
            device_id_type=MESH,
        )

    def finish_out(c, rows, total):
        moe_ref[rows] = total.astype(bf16)

    def finish_in(c, rows, total):
        x = x_ref[rows].astype(f32)
        scale = lax.rsqrt(jnp.mean(x * x, -1, keepdims=True) + epsilon)
        unit = x * scale
        scaled = total * gains_ref[:1]
        inner = jnp.mean(scaled * unit, -1, keepdims=True)
        own[rows] = (low_ref[rows].astype(f32) + scale * (scaled - unit * inner)).astype(bf16)
        dgain[...] += folded(total * unit)

    outward = Line(n, me, moe_ref, finish_out, scratch[:7], lag=1, hop=2)
    inward = Line(n, me, own, finish_in, scratch[7:], hop=2)
    dgain[...] = jnp.zeros_like(dgain)
    greet(me, n, [peer(o) for o in range(1, peers)])

    def offer(i):
        per = outward.chunks // portions
        moe_load(i).wait()
        loop(i * per, (i + 1) * per, outward.offer)

    heads, early = q_wide // HEAD_SIZE, 4
    for load in loads[:4]:
        load.start()
    loop(0, portions, offer)
    loop(0, early, outward.step)
    for load in loads[:4]:
        load.wait()
    for load in loads[4:]:
        load.start()


    def turned_back(y, part):
        wide = y.shape[1]
        here = pl.ds(part * quarter, quarter)
        return y * widened(cos_ref[here], wide) - swapped_halves(y) * widened(sin_ref[here], wide)

    def attend(s):
        for part in (1, 0):
            rows = places.own(s, part)
            keys = places.keys(part)
            dmixed[...] = dot(low_ref[rows], wout_ref[...]).astype(bf16)
            start = places.slot(places.c, part) * quarter
            allowed = lax.broadcasted_iota(jnp.int32, (keys, quarter), 0) <= (
                start + lax.broadcasted_iota(jnp.int32, (keys, quarter), 1)
            )
            for k in range(kv_heads):
                at = k * HEAD_SIZE
                key = kv_ref[s, :keys, at : at + HEAD_SIZE]
                value = kv_ref[s, :keys, k_wide + at : k_wide + at + HEAD_SIZE]
                dkey = dvalue = None
                for h in range(k * group, (k + 1) * group):
                    head = slice(h * HEAD_SIZE, (h + 1) * HEAD_SIZE)
                    query = query_ref[rows, head]
                    dout = dmixed[:, head]
                    scores = jnp.where(allowed, dot(key, query, (1, 1)), -1e30)
                    raised = jnp.exp(scores - jnp.max(scores, 0, keepdims=True))
                    probs = raised * (1.0 / jnp.sum(raised, 0, keepdims=True))
                    product = probs * dot(value, dout, (1, 1))
                    dscores = product - probs * jnp.sum(product, 0, keepdims=True)
                    dscores = dscores.astype(bf16)
                    dquery[:, head] = dot(dscores, key, (0, 0)) * factor
                    dk, dv = dot(dscores, query), dot(probs.astype(bf16), dout)
                    dkey = dk if dkey is None else dkey + dk
                    dvalue = dv if dvalue is None else dvalue + dv
                    outward.step(early + (2 * s + 1 - part) * heads + h)
                for first, add in ((at, dkey), (k_wide + at, dvalue)):
                    lanes = slice(first, first + HEAD_SIZE)
                    if part == 1:
                        dkv[s, :keys, lanes] = add
                    else:
                        dkv[s, :keys, lanes] += add
            dqkv_ref[rows, :q_wide] = turned_back(dquery[...], part).astype(bf16)
        for part in range(2):
            for o in range(1, nc):
                kv_copy(s, part, o, places.after(o)).start()

    loop(0, seqs, attend)
    done = early + 2 * seqs * heads
    for load in loads[4:]:
        load.wait()
    per = quarter // inward.size

    def turn_back(s):
        for part in range(2):
            rows = places.own(s, part)
            mine = dkv[s, places.rows(places.c, part)]
            for o in range(1, nc):
                kv_copy(s, part, o, places.after(o)).wait()
                mine = mine + dkv_in[o - 1, s, part]
            dqkv_ref[rows, q_wide : q_wide + k_wide] = turned_back(mine[:, :k_wide], part).astype(
                bf16
            )
            dqkv_ref[rows, q_wide + k_wide :] = mine[:, k_wide:].astype(bf16)
            own[rows] = dot(dqkv_ref[rows], wqkv_ref[...], (1, 1)).astype(bf16)
            first = (2 * s + part) * per
            loop(first, first + per, inward.offer)
            outward.step(done + 2 * s + part)
            x = x_ref[rows].astype(f32)
            scale = lax.rsqrt(jnp.mean(x * x, -1, keepdims=True) + epsilon)
            scales[rows] = jnp.broadcast_to(scale, (quarter, LANES))

    loop(0, seqs, turn_back)
    wide, mid = dqkv_ref.shape[1], dqkv_ref.shape[1] + mixed_ref.shape[1]
    span = max(LANES, shard * LANES // math.gcd(shard, LANES))
    count = span // shard

    def weights(i):
        at = aligned(i * span, span)
        to = pl.ds(i * count, count)

        def put(lanes, value):
            value = value.reshape(count, shard, value.shape[1])
            if padded > shard:
                more = jnp.zeros((count, padded - shard, value.shape[2]), f32)
                value = jnp.concatenate([value, more], 1)
            grads[to, :, lanes] = value.astype(bf16)

        normed = x_ref[:, at].astype(f32) * widened(scales[...], span) * gains_ref[:1, at]
        put(slice(0, wide), dot(normed.astype(bf16), dqkv_ref[...], (0, 0)))
        put(slice(wide, mid), dot(low_ref[:, at], mixed_ref[...], (0, 0)))
        put(slice(mid, grads.shape[2]), dot(normed_two_ref[:, at], dlogits_ref[...], (0, 0)))
        outward.step(done + 2 * seqs + i)

    spans = x_ref.shape[1] // span
    loop(0, spans, weights)
    def send_share(g):
        for p in range(1, nc):
            near_copy(p, g).start()

    loop(0, nf, send_share)
    start = done + 2 * seqs + spans
    ahead = max(outward.steps - start, 0)

    def both(i):
        outward.step(start + i)
        inward.step(i)

    loop(0, ahead, both)
    outward.rest(start + ahead)

    def add_share(g):
        mine = g * nc + places.c
        total = grads[mine].astype(f32)
        for p in range(1, nc):
            near_copy(p, g).wait()
            total = total + grads_near[p - 1, g].astype(f32)
        grads[mine] = total.astype(bf16)

    stores = [
        pltpu.make_async_copy(source, target, store_sem.at[i])
        for i, (source, target) in enumerate(((moe_ref, act_hbm), (own, input_hbm)))
    ]
    stores[0].start()
    enough = ahead + inward.chunks // 2
    loop(ahead, enough, inward.step)
    loop(0, nf, add_share)
    loop(1, nf, lambda o: far_copy(o).start())
    inward.rest(enough)
    stores[1].start()
    one = jnp.sum(dgain[...], 0, keepdims=True)
    two = jnp.sum(dgain_two_ref[...], 0, keepdims=True)
    gains_in[0] = jnp.concatenate([one, two], 1)
    loop(1, peers, lambda o: gain_copy(o).start())
    grads_ref[...] = grads[flat].astype(f32)[:shard]

    def add_grad(o):
        far_copy(o).wait()
        grads_ref[...] += grads_far[o].astype(f32)[:shard]

    loop(1, nf, add_grad)
    loop(1, peers, lambda o: gain_copy(o).wait())
    dgains_ref[...] = gains_in[0]

    def add(o):
        dgains_ref[...] += gains_in[o]

    loop(1, peers, add)
    for store in stores:
        store.wait()


def split_kernel(
    ffn,
    nc,
    grads_ref,
    small_ref,
    dgains_ref,
    out_hbm,
    input_hbm,
    gate_ref,
    up_ref,
    down_ref,
    query_ref,
    key_ref,
    value_ref,
    out_ref,
    router_ref,
    gain_ref,
    act_hbm,
    grad_hbm,
    act,
    grad,
    load,
    store,
):
    loads = [
        pltpu.make_async_copy(input_hbm, grad, load.at[0]),
        pltpu.make_async_copy(out_hbm, act, load.at[1]),
    ]
    stores = [
        pltpu.make_async_copy(grad, grad_hbm, store.at[0]),
        pltpu.make_async_copy(act, act_hbm, store.at[1]),
    ]
    for copy in loads:
        copy.start()
    gu_wide = 2 * E * ffn
    at = 0
    for ref in (query_ref, key_ref, value_ref, out_ref):
        ref[...] = small_ref[:, at : at + ref.shape[1]]
        at += ref.shape[1]
    router_ref[...] = small_ref[:, at:].T[:E]
    width, shard = input_hbm.shape[1], small_ref.shape[0]
    flat = lax.axis_index("fsdp") * nc + lax.axis_index("ctx")
    shift = lax.rem(width - flat * shard, width)
    for i in range(2):
        row = jnp.broadcast_to(dgains_ref[:, i * width : (i + 1) * width], (8, width))
        gain_ref[i : i + 1] = pltpu.roll(row, shift, 1)[:1, :shard]
    loads[0].wait()
    stores[0].start()
    loads[1].wait()
    stores[1].start()
    for e in range(E):
        at = (e // 2) * 4 * ffn + (e % 2) * ffn
        gate_ref[e] = grads_ref[:, at : at + ffn].astype(f32)
        up_ref[e] = grads_ref[:, at + 2 * ffn : at + 3 * ffn].astype(f32)
        at = gu_wide + e * ffn
        down_ref[e] = grads_ref[:, at : at + ffn].astype(f32)
    for copy in stores:
        copy.wait()


def call(kernel, outs, scratch, collective_id, operands, specs=None):
    total = sum(math.prod(o.shape) * o.dtype.itemsize for o in [*outs, *operands])
    return pl.pallas_call(
        kernel,
        out_shape=tuple(outs),
        in_specs=[WHOLE] * len(operands),
        out_specs=specs or (WHOLE,) * len(outs),
        scratch_shapes=scratch,
        compiler_params=pltpu.CompilerParams(
            collective_id=collective_id, has_side_effects=True, vmem_limit_bytes=VMEM_BYTES
        ),
        cost_estimate=pl.CostEstimate(flops=0, bytes_accessed=total, transcendentals=0),
    )(*operands)


def per_device(
    tokens,
    routes,
    gain_attn,
    w_query,
    key_matrix,
    value_matrix,
    w_out,
    gain_moe,
    w_router,
    w_gate,
    w_up,
    w_down,
    cotangent,
):
    shaped = jax.ShapeDtypeStruct
    rows, width = tokens.shape
    nc, n = lax.axis_size("ctx"), lax.axis_size("tp")
    half = SEQUENCE_LENGTH // nc
    seqs = rows // half
    both = ("fsdp", "ctx")
    cos, sin = angle_tables(placed(lax.axis_index("ctx"), half))
    q_wide, k_wide, o_wide = w_query.shape[1], key_matrix.shape[1], w_out.shape[0]
    qkv_wide = q_wide + 2 * k_wide
    ffn = w_gate.shape[2]
    shard = w_gate.shape[1]

    gu_wide, down_wide = 2 * E * ffn, E * ffn
    small_wide = qkv_wide + o_wide + LANES
    nf = lax.axis_size("fsdp")
    peers = nf * nc
    link = bf16 if shard % 16 == 0 else f32
    def sems(*dims):
        return pltpu.SemaphoreType.DMA(dims)

    small, gains, packed = call(
        functools.partial(gather_kernel, nf, nc, ffn),
        [
            shaped((peers, shard, small_wide), link),
            shaped((8, width), f32),
            shaped((shard, gu_wide + down_wide), bf16),
        ],
        [
            sems(nf),
            sems(nf),
            sems(nc - 1, nf),
            sems(nc - 1, nf),
        ],
        4,
        (
            w_query,
            key_matrix,
            value_matrix,
            w_out.T,
            w_router.T,
            gain_attn,
            gain_moe,
            w_gate,
            w_up,
            jnp.swapaxes(w_down, 1, 2),
        ),
    )
    experts = lax.all_gather(packed, both, axis=0, tiled=True)
    small = small.reshape(width, small_wide).astype(bf16)
    kv_sems = sems(nc - 1, seqs, 2)
    anywhere = pl.BlockSpec(memory_space=pl.ANY)
    query, kv, mixed, state, normed_two, gates = call(
        functools.partial(front_kernel, n, nc),
        [
            shaped((rows, q_wide), bf16),
            shaped((seqs, SEQUENCE_LENGTH, 2 * k_wide), bf16),
            shaped((rows, q_wide), bf16),
            shaped((rows, width), bf16),
            shaped((rows, width), bf16),
            shaped((rows, LANES), f32),
        ],
        [
            pltpu.VMEM((seqs, SEQUENCE_LENGTH, 2 * k_wide), bf16),
            *[pltpu.VMEM((rows, width), bf16)] * 3,
            sems(2, rows // 32),
            kv_sems,
            kv_sems,
            *line_scratch(rows, width, 32),
        ],
        0,
        (tokens, small, gains, routes, cos, sin),
        (WHOLE, WHOLE, WHOLE, anywhere, anywhere, WHOLE),
    )

    block = 256

    def by_rows(wide):
        return pl.BlockSpec((block, wide), lambda i: (i, 0))

    def constant(*dims):
        return pl.BlockSpec(
            dims, lambda i: (0,) * len(dims), pipeline_mode=pl.Buffered(1)
        )

    anywhere = pl.BlockSpec(memory_space=pl.ANY)
    blocks = rows // block
    size, tall = 64, 256
    dots_sems = pltpu.SemaphoreType.DMA((n - 1, blocks))
    moe_part, grad_experts, low, dlogits, dgain_two = pl.pallas_call(
        functools.partial(expert_kernel, n),
        grid=(blocks,),
        out_shape=(
            shaped((rows, width), bf16),
            shaped((width, gu_wide + down_wide), bf16),
            shaped((rows, width), bf16),
            shaped((rows, LANES), bf16),
            shaped((8, width), f32),
        ),
        in_specs=[
            anywhere,
            anywhere,
            constant(rows, LANES),
            anywhere,
            anywhere,
            pl.BlockSpec(
                (width, LANES),
                lambda i: (0, small_wide // LANES - 1),
                pipeline_mode=pl.Buffered(1),
            ),
            constant(8, width),
        ],
        out_specs=(
            by_rows(width),
            anywhere,
            anywhere,
            pl.BlockSpec((rows, LANES), lambda i: (0, 0)),
            pl.BlockSpec((8, width), lambda i: (0, 0)),
        ),
        scratch_shapes=[
            *[pltpu.VMEM((rows, width), bf16)] * 4,
            pltpu.VMEM((rows, down_wide), bf16),
            pltpu.VMEM((rows, gu_wide), bf16),
            pltpu.VMEM((tall, rows), bf16),
            pltpu.VMEM((tall, rows), bf16),
            pltpu.VMEM((block, LANES), f32),
            pltpu.VMEM((n, blocks, E, block), f32),
            pltpu.VMEM((rows, LANES), f32),
            pltpu.VMEM((width, gu_wide + down_wide), bf16),
            pltpu.VMEM((2, size, width), bf16),
            sems(3, blocks),
            sems(2, E // 4),
            sems(width // tall),
            sems(2),
            dots_sems,
            dots_sems,
            *line_scratch(rows, width, size),
        ],
        compiler_params=pltpu.CompilerParams(
            collective_id=1, has_side_effects=True, vmem_limit_bytes=VMEM_BYTES
        ),
        cost_estimate=pl.CostEstimate(
            flops=18 * rows * width * down_wide,
            bytes_accessed=2 * width * (gu_wide + down_wide),
            transcendentals=0,
        ),
    )(normed_two, cotangent, gates, experts, state, small, gains)

    low, grad_experts = lax.optimization_barrier((low, grad_experts))
    grad_experts = lax.psum_scatter(grad_experts, both, scatter_dimension=0, tiled=True)

    def small_block(*dims):
        return pltpu.VMEM((*dims, -(-shard // 16) * 16, small_wide), bf16)

    whole = pltpu.VMEM((rows, width), bf16)
    sources = (moe_part, low, small, query, kv, tokens, normed_two, mixed, dlogits)
    held = (
        *[(rows, width)] * 2,
        (width, o_wide),
        query.shape,
        kv.shape,
        (width, qkv_wide),
        *[(rows, width)] * 2,
        mixed.shape,
        dlogits.shape,
    )
    activations, input_grad, dgains, grad_small = pl.pallas_call(
        functools.partial(rear_kernel, n, nf, nc),
        out_shape=(
            shaped((rows, width), bf16),
            shaped((rows, width), bf16),
            shaped((1, 2 * width), f32),
            shaped((shard, small_wide), f32),
        ),
        in_specs=[anywhere] * len(sources) + [WHOLE] * 4,
        out_specs=(anywhere, anywhere, WHOLE, WHOLE),
        scratch_shapes=[
            *[pltpu.VMEM(dims, bf16) for dims in held],
            pltpu.VMEM((half // 2, q_wide), bf16),
            pltpu.VMEM((half // 2, q_wide), f32),
            pltpu.VMEM((seqs, SEQUENCE_LENGTH, 2 * k_wide), f32),
            pltpu.VMEM((nc - 1, seqs, 2, half // 2, 2 * k_wide), f32),
            pltpu.VMEM((rows, qkv_wide), bf16),
            whole,
            pltpu.VMEM((rows, LANES), f32),
            pltpu.VMEM((8, width), f32),
            pltpu.VMEM((peers, 1, 2 * width), f32),
            small_block(peers),
            small_block(nc - 1, nf),
            small_block(nf),
            sems(4),
            sems(len(held) - 1),
            sems(2),
            kv_sems,
            kv_sems,
            *[sems(peers)] * 2,
            *[sems(nc - 1, nf)] * 2,
            *[sems(nf)] * 2,
            *line_scratch(rows, width, 32),
            *line_scratch(rows, width, 32),
        ],
        compiler_params=pltpu.CompilerParams(
            collective_id=3, has_side_effects=True, vmem_limit_bytes=VMEM_BYTES
        ),
        cost_estimate=pl.CostEstimate(
            flops=12 * rows * width * small_wide,
            bytes_accessed=16 * rows * width,
            transcendentals=0,
        ),
    )(*sources, gains, dgain_two, cos, sin)
    results = pl.pallas_call(
        functools.partial(split_kernel, ffn, nc),
        out_shape=(
            shaped((E, shard, ffn), f32),
            shaped((E, shard, ffn), f32),
            shaped((E, shard, ffn), f32),
            shaped((shard, q_wide), f32),
            shaped((shard, k_wide), f32),
            shaped((shard, k_wide), f32),
            shaped((shard, o_wide), f32),
            shaped((E, shard), f32),
            shaped((2, shard), f32),
            shaped((rows, width), bf16),
            shaped((rows, width), bf16),
        ),
        in_specs=[WHOLE, WHOLE, WHOLE, anywhere, anywhere],
        out_specs=(*[WHOLE] * 9, anywhere, anywhere),
        scratch_shapes=[
            pltpu.VMEM((rows, width), bf16),
            pltpu.VMEM((rows, width), bf16),
            sems(2),
            sems(2),
        ],
        compiler_params=pltpu.CompilerParams(vmem_limit_bytes=VMEM_BYTES),
    )(grad_experts, grad_small, dgains, activations, input_grad)
    grad_gate, grad_up, grad_down, grad_query, grad_key, grad_value, grad_out = results[:7]
    grad_router, dgains = results[7:9]
    return (
        results[9],
        results[10],
        dgains[0],
        grad_query,
        grad_key,
        grad_value,
        grad_out.T,
        dgains[1],
        grad_router.T,
        grad_gate,
        grad_up,
        jnp.swapaxes(grad_down, 1, 2),
    )


def solution(mesh):
    specs = (
        P(("fsdp", "ctx"), None),
        P(("fsdp", "ctx"), None),
        P(("fsdp", "ctx")),
        P(("fsdp", "ctx"), "tp"),
        P(("fsdp", "ctx"), "tp"),
        P(("fsdp", "ctx"), "tp"),
        P("tp", ("fsdp", "ctx")),
        P(("fsdp", "ctx")),
        P(("fsdp", "ctx"), None),
        P(None, ("fsdp", "ctx"), "tp"),
        P(None, ("fsdp", "ctx"), "tp"),
        P(None, "tp", ("fsdp", "ctx")),
        P(("fsdp", "ctx"), None),
    )
    return jax.shard_map(
        per_device,
        mesh=mesh,
        in_specs=specs,
        out_specs=(
            P(("fsdp", "ctx"), None),
            P(("fsdp", "ctx"), None),
            P(("fsdp", "ctx")),
            P(("fsdp", "ctx"), "tp"),
            P(("fsdp", "ctx"), "tp"),
            P(("fsdp", "ctx"), "tp"),
            P("tp", ("fsdp", "ctx")),
            P(("fsdp", "ctx")),
            P(("fsdp", "ctx"), None),
            P(None, ("fsdp", "ctx"), "tp"),
            P(None, ("fsdp", "ctx"), "tp"),
            P(None, "tp", ("fsdp", "ctx")),
        ),
        check_vma=False,
    )
```

```python
import functools
import math

import jax
import jax.numpy as jnp
from jax import lax
from jax.experimental import pallas as pl
from jax.experimental.pallas import tpu as pltpu
from jax.sharding import PartitionSpec as P

HEAD_SIZE = 64
TOPK = 8
E = 16
SEQUENCE_LENGTH = 1024
LANES = 128
VMEM_BYTES = 60 * 2**20

epsilon = 1e-06
f32 = jnp.float32
bf16 = jnp.bfloat16
MESH = pl.DeviceIdType.MESH
WHOLE = pl.BlockSpec(memory_space=pltpu.VMEM)


def aligned(start, size):
    return pl.ds(pl.multiple_of(start, size), size)


def dot(a, b, at=(1, 0)):
    return lax.dot_general(a, b, (((at[0],), (at[1],)), ((), ())), preferred_element_type=f32)


def swapped_halves(y):
    wide, halfway = y.shape[1], HEAD_SIZE // 2
    lane = lax.broadcasted_iota(jnp.int32, y.shape, 1)
    lower = lax.rem(lane, HEAD_SIZE) < halfway
    return jnp.where(lower, -pltpu.roll(y, wide - halfway, 1), pltpu.roll(y, halfway, 1))


def widened(table, wide):
    return jnp.concatenate([table] * (wide // LANES), 1)


SLOTS = 4


def line_scratch(rows, width, size):
    sems = pltpu.SemaphoreType.DMA((rows // size,))
    slots = pltpu.VMEM((SLOTS * size, width), bf16)
    return [pltpu.VMEM((2 * rows, width), bf16), slots, slots, *[sems] * 4]


def greet(me, n, others=()):
    barrier = pltpu.get_barrier_semaphore()

    @pl.when(me > 0)
    def _():
        pl.semaphore_signal(
            barrier, inc=1, device_id={"tp": lax.rem(me + n - 1, n)}, device_id_type=MESH
        )

    @pl.when(me < n - 1)
    def _():
        pl.semaphore_signal(
            barrier, inc=1, device_id={"tp": lax.rem(me + 1, n)}, device_id_type=MESH
        )

    for other in others:
        pl.semaphore_signal(barrier, inc=1, device_id=other, device_id_type=MESH)
    count = jnp.where(me > 0, 1, 0) + jnp.where(me < n - 1, 1, 0) + len(others)
    pl.semaphore_wait(barrier, count)


class Line:
    def __init__(self, n, me, own, finish, scratch, lag=0, hop=1, late=0):
        self.n, self.me, self.own, self.finish = n, me, own, finish
        self.arrived, self.to_right, self.to_left = scratch[:3]
        self.send_right, self.recv_left, self.send_left, self.recv_right = scratch[3:]
        self.size = self.to_right.shape[0] // SLOTS
        self.total = self.arrived.shape[0] // 2
        self.chunks = self.total // self.size
        self.lag, self.hop, self.late = lag, hop, late
        self.steps = self.chunks + lag + hop * (n - 2) + late
        self.middle = (me > 0) & (me < n - 1)

    def rows(self, c):
        return aligned(c * self.size, self.size)

    def left_rows(self, c):
        return aligned(c * self.size, self.size)

    def right_rows(self, c):
        return aligned(self.total + c * self.size, self.size)

    def slot(self, c):
        return aligned(lax.rem(c, SLOTS) * self.size, self.size)

    def right(self, c, end=False):
        return pltpu.make_async_remote_copy(
            src_ref=self.own.at[self.rows(c)] if end else self.to_right.at[self.slot(c)],
            dst_ref=self.arrived.at[self.left_rows(c)],
            send_sem=self.send_right.at[c],
            recv_sem=self.recv_left.at[c],
            device_id={"tp": lax.rem(self.me + 1, self.n)},
            device_id_type=MESH,
        )

    def left(self, c, end=False):
        return pltpu.make_async_remote_copy(
            src_ref=self.own.at[self.rows(c)] if end else self.to_left.at[self.slot(c)],
            dst_ref=self.arrived.at[self.right_rows(c)],
            send_sem=self.send_left.at[c],
            recv_sem=self.recv_right.at[c],
            device_id={"tp": lax.rem(self.me + self.n - 1, self.n)},
            device_id_type=MESH,
        )

    def offer(self, c):
        @pl.when(self.me == 0)
        def _():
            self.right(c, True).start()

        @pl.when(self.me == self.n - 1)
        def _():
            self.left(c, True).start()

    def step(self, t):
        n, me, chunks = self.n, self.me, self.chunks
        go, come = t - self.lag - self.hop * (me - 1), t - self.lag - self.hop * (n - 2 - me)
        done = jnp.minimum(go, come) - jnp.where(self.middle, 0, self.late)
        nearer_left = me < n - 1 - me

        def inside(c):
            return (c >= 0) & (c < chunks)

        @pl.when(self.middle & inside(go) & nearer_left)
        def _():
            self.right_pass(go)

        @pl.when(self.middle & inside(come))
        def _():
            self.left_pass(come)

        @pl.when(self.middle & inside(go) & jnp.logical_not(nearer_left))
        def _():
            self.right_pass(go)

        @pl.when(inside(done))
        def _():
            @pl.when(me == 0)
            def _():
                self.left(done).wait_recv()
                self.right(done, True).wait_send()

            @pl.when(me == n - 1)
            def _():
                self.right(done).wait_recv()
                self.left(done, True).wait_send()

            rows = self.rows(done)
            at = done * self.size
            one = aligned(jnp.where(me == 0, self.total, 0) + at, self.size)
            two = aligned(jnp.where(me == n - 1, 0, self.total) + at, self.size)
            total = self.own[rows].astype(f32) + self.arrived[one].astype(f32)
            other = self.arrived[two].astype(f32)
            self.finish(done, rows, total + jnp.where(self.middle, other, 0.0))

    def right_pass(self, c):
        self.right(c).wait_recv()

        @pl.when(c >= SLOTS)
        def _():
            self.right(c - SLOTS).wait_send()

        total = self.own[self.rows(c)].astype(f32) + self.arrived[self.left_rows(c)].astype(f32)
        self.to_right[self.slot(c)] = total.astype(bf16)
        self.right(c).start()

    def left_pass(self, c):
        self.left(c).wait_recv()

        @pl.when(c >= SLOTS)
        def _():
            self.left(c - SLOTS).wait_send()

        total = self.own[self.rows(c)].astype(f32) + self.arrived[self.right_rows(c)].astype(f32)
        self.to_left[self.slot(c)] = total.astype(bf16)
        self.left(c).start()

    def rest(self, start):
        loop(start, self.steps, self.step)

        @pl.when(self.middle)
        def _():
            def sent(c):
                self.right(c).wait_send()
                self.left(c).wait_send()

            loop(max(self.chunks - SLOTS, 0), self.chunks, sent)


def loop(low, high, body):
    lax.fori_loop(low, high, lambda i, carry: (body(i), carry)[1], 0)


def folded(values):
    rows, width = values.shape
    return jnp.sum(values.reshape(rows // 8, 8, width), 0)


class Places:
    def __init__(self, nc):
        self.nc = nc
        self.c = lax.axis_index("ctx")
        self.quarter = SEQUENCE_LENGTH // nc // 2

    def slot(self, rank, part):
        return rank if part == 0 else 2 * self.nc - 1 - rank

    def rows(self, rank, part):
        return aligned(self.slot(rank, part) * self.quarter, self.quarter)

    def own(self, s, part):
        return aligned((2 * s + part) * self.quarter, self.quarter)

    def keys(self, part):
        return self.quarter * (self.nc if part == 0 else 2 * self.nc)

    def after(self, o):
        return lax.rem(self.c + o, self.nc)

    def before(self, o):
        return lax.rem(self.c + self.nc - o, self.nc)


def gather_kernel(
    nf,
    nc,
    ffn,
    query_ref,
    key_ref,
    value_ref,
    out_ref,
    router_ref,
    gain_one_ref,
    gain_two_ref,
    gate_ref,
    up_ref,
    down_ref,
    routes_ref,
    small_all,
    gains_ref,
    experts_ref,
    cos_ref,
    sin_ref,
    named_ref,
    send_f,
    recv_f,
    send_c,
    recv_c,
):
    f, c = lax.axis_index("fsdp"), lax.axis_index("ctx")
    shard = small_all.shape[1]
    kind = small_all.dtype
    mine = f * nc + c

    def from_f(o):
        return lax.rem(f + nf - o, nf)

    def to_peer(o):
        return {"fsdp": lax.rem(f + o, nf)}

    def to_near(p):
        return {"ctx": lax.rem(c + p, nc)}

    relay = nf == 4 and shard % 32 == 0
    across, along = f - lax.rem(f, 2) + 1 - lax.rem(f, 2), lax.rem(f + 2, 4)
    if relay:
        far = [{"fsdp": across}, {"fsdp": along}]
    else:
        far = [to_peer(o) for o in range(1, nf)]
    barrier = pltpu.get_barrier_semaphore()
    for other in far + [to_near(p) for p in range(1, nc)]:
        pl.semaphore_signal(barrier, inc=1, device_id=other, device_id_type=MESH)
    gains = [g[...].astype(f32).reshape(1, shard) for g in (gain_one_ref, gain_two_ref)]
    blank = jnp.zeros((LANES - E - 2, shard), f32)
    last = jnp.concatenate([router_ref[...].astype(f32), *gains, blank], 0).T
    at = 0
    for piece in (query_ref[...], key_ref[...], value_ref[...], out_ref[...], last):
        small_all[mine, :, at : at + piece.shape[1]] = piece.astype(kind)
        at += piece.shape[1]
    pl.semaphore_wait(barrier, len(far) + nc - 1)

    owners = [f, across, along, 3 - f] if relay else [from_f(o) for o in range(nf)]

    def relay_copy(i):
        owner, to = ((f, across), (f, along), (across, along), (along, across))[i]
        block = small_all.at[owner * nc + c]
        if i > 1:
            block = block.at[pl.ds((i - 2) * (shard // 2), shard // 2)]
        return pltpu.make_async_remote_copy(
            src_ref=block,
            dst_ref=block,
            send_sem=send_f.at[i],
            recv_sem=recv_f.at[i],
            device_id={"fsdp": to},
            device_id_type=MESH,
        )

    def relay_arrival(i):
        block = small_all.at[(across, along, 3 - f, 3 - f)[i] * nc + c]
        if i > 1:
            block = block.at[pl.ds((i - 2) * (shard // 2), shard // 2)]
        return pltpu.make_async_remote_copy(
            src_ref=block,
            dst_ref=block,
            send_sem=send_f.at[i],
            recv_sem=recv_f.at[i],
            device_id={"fsdp": across},
            device_id_type=MESH,
        )

    def far_copy(o, rank):
        block = small_all.at[rank * nc + c]
        return pltpu.make_async_remote_copy(
            src_ref=block,
            dst_ref=block,
            send_sem=send_f.at[o],
            recv_sem=recv_f.at[o],
            device_id=to_peer(o),
            device_id_type=MESH,
        )

    def near_copy(p, o, rank):
        block = small_all.at[owners[o] * nc + rank]
        return pltpu.make_async_remote_copy(
            src_ref=block,
            dst_ref=block,
            send_sem=send_c.at[p - 1, o],
            recv_sem=recv_c.at[p - 1, o],
            device_id=to_near(p),
            device_id_type=MESH,
        )

    def share(o):
        for p in range(1, nc):
            near_copy(p, o, c).start()

    if relay:
        relay_copy(0).start()
        relay_copy(1).start()
    else:
        loop(1, nf, lambda o: far_copy(o, f).start())
    share(0)
    for e in range(E):
        at = (e // 2) * 4 * ffn + (e % 2) * ffn
        experts_ref[:, at : at + ffn] = gate_ref[e]
        experts_ref[:, at + 2 * ffn : at + 3 * ffn] = up_ref[e]
        at = 2 * E * ffn + e * ffn
        experts_ref[:, at : at + ffn] = down_ref[e]

    half = cos_ref.shape[0]
    quarter = half // 2
    row = lax.broadcasted_iota(jnp.int32, (half, LANES), 0)
    lane = lax.broadcasted_iota(jnp.int32, (half, LANES), 1)
    late = SEQUENCE_LENGTH - (c + 1) * quarter + row - quarter
    place = jnp.where(row < quarter, c * quarter + row, late)
    lane = lax.rem(lane, HEAD_SIZE // 2).astype(f32)
    angle = place.astype(f32) * jnp.exp(lane * (-2.0 * math.log(10000.0) / HEAD_SIZE))
    cos_ref[...] = jnp.cos(angle)
    sin_ref[...] = jnp.sin(angle)
    expert = lax.broadcasted_iota(jnp.int32, (LANES, LANES), 0)

    def name(i):
        rows = aligned(i * LANES, LANES)
        routes = routes_ref[:, rows]
        named = expert == routes[:1]
        for k in range(1, TOPK):
            named = named | (expert == routes[k : k + 1])
        named_ref[rows] = jnp.where(named, 1.0, 0.0).T

    loop(0, named_ref.shape[0] // LANES, name)

    if relay:
        relay_arrival(0).wait_recv()
        relay_copy(2).start()
        share(1)
        relay_arrival(1).wait_recv()
        relay_copy(3).start()
        share(2)
        relay_arrival(2).wait_recv()
        relay_arrival(3).wait_recv()
        share(3)
    else:
        for o in range(1, nf):
            far_copy(o, from_f(o)).wait_recv()
            share(o)
    for o in range(nf):
        for p in range(1, nc):
            near_copy(p, o, lax.rem(c + nc - p, nc)).wait_recv()
    last = small_all[:, :, small_all.shape[2] - LANES :]
    gains_ref[...] = last.reshape(nf * nc * shard, LANES).astype(f32).T[E : E + 8]
    if relay:
        for i in range(4):
            relay_copy(i).wait_send()
    else:
        loop(1, nf, lambda o: far_copy(o, f).wait_send())
    for o in range(nf):
        for p in range(1, nc):
            near_copy(p, o, c).wait_send()


def front_kernel(
    n,
    nc,
    x_ref,
    small_ref,
    gains_ref,
    named_ref,
    cos_ref,
    sin_ref,
    query_ref,
    kv_ref,
    mixed_ref,
    state_hbm,
    normed_hbm,
    gates_ref,
    kv_all,
    own,
    state_ref,
    normed_ref,
    store_sem,
    send_kv,
    recv_kv,
    *scratch,
):
    me = lax.axis_index("tp")
    places = Places(nc)
    quarter = places.quarter
    seqs = kv_ref.shape[0]
    q_wide, k_wide = query_ref.shape[1], kv_ref.shape[2] // 2
    group = q_wide // k_wide
    qkv_wide = q_wide + 2 * k_wide
    wide = small_ref.shape[1] - LANES

    def row_stores(c):
        rows = line.rows(c)
        pairs = ((state_ref, state_hbm), (normed_ref, normed_hbm))
        return [
            pltpu.make_async_copy(source.at[rows], target.at[rows], store_sem.at[i, c])
            for i, (source, target) in enumerate(pairs)
        ]

    def finish(c, rows, total):
        state = x_ref[rows].astype(f32) + total
        scale = lax.rsqrt(jnp.mean(state * state, -1, keepdims=True) + epsilon)
        normed = (state * scale * gains_ref[1:2]).astype(bf16)
        state_ref[rows] = state.astype(bf16)
        normed_ref[rows] = normed
        for copy in row_stores(c):
            copy.start()
        named = named_ref[rows] > 0.5
        logits = jnp.where(named, dot(normed, small_ref[:, wide:]), -1e30)
        top = jnp.max(logits, -1, keepdims=True)
        raised = jnp.where(named, jnp.exp(logits - top), 0.0)
        gates_ref[rows] = raised / jnp.sum(raised, -1, keepdims=True)

    line = Line(n, me, own, finish, scratch, hop=2, late=quarter // 16)
    greet(me, n, [{"ctx": places.after(o)} for o in range(1, nc)])

    def kv_copy(s, part, o, rank):
        where = kv_all.at[s, places.rows(rank, part)]
        return pltpu.make_async_remote_copy(
            src_ref=where,
            dst_ref=where,
            send_sem=send_kv.at[o - 1, s, part],
            recv_sem=recv_kv.at[o - 1, s, part],
            device_id={"ctx": places.after(o)},
            device_id_type=MESH,
        )

    def project(s):
        for part in range(2):
            rows = places.own(s, part)
            x = x_ref[rows].astype(f32)
            scale = lax.rsqrt(jnp.mean(x * x, -1, keepdims=True) + epsilon)
            normed = (x * scale * gains_ref[:1]).astype(bf16)
            qkv = dot(normed, small_ref[:, :qkv_wide])
            qk = qkv[:, : q_wide + k_wide]
            here = pl.ds(part * quarter, quarter)
            cos, sin = widened(cos_ref[here], q_wide + k_wide), widened(sin_ref[here], q_wide + k_wide)
            rot = qk * cos + swapped_halves(qk) * sin
            query_ref[rows] = (rot[:, :q_wide] * (1.0 / math.sqrt(HEAD_SIZE))).astype(bf16)
            slot = places.rows(places.c, part)
            kv_all[s, slot, :k_wide] = rot[:, q_wide:].astype(bf16)
            kv_all[s, slot, k_wide:] = qkv[:, q_wide + k_wide :].astype(bf16)
            for o in range(1, nc):
                kv_copy(s, part, o, places.c).start()

    loop(0, seqs, project)

    def attend(s):
        for part in range(2):
            for o in range(1, nc):
                kv_copy(s, part, o, places.before(o)).wait_recv()
        for part in range(2):
            rows = places.own(s, part)
            keys = places.keys(part)
            base = places.slot(places.c, part) * quarter
            allowed = lax.broadcasted_iota(jnp.int32, (quarter, keys), 1) <= (
                base + lax.broadcasted_iota(jnp.int32, (quarter, keys), 0)
            )
            for h in range(q_wide // HEAD_SIZE):
                at = h // group * HEAD_SIZE
                query = query_ref[rows, h * HEAD_SIZE : (h + 1) * HEAD_SIZE]
                key = kv_all[s, :keys, at : at + HEAD_SIZE]
                value = kv_all[s, :keys, k_wide + at : k_wide + at + HEAD_SIZE]
                scores = jnp.where(allowed, dot(query, key, (1, 1)), -1e30)
                raised = jnp.exp(scores - jnp.max(scores, -1, keepdims=True))
                probs = (raised * (1.0 / jnp.sum(raised, -1, keepdims=True))).astype(bf16)
                mixed_ref[rows, h * HEAD_SIZE : (h + 1) * HEAD_SIZE] = dot(probs, value).astype(bf16)
            own[rows] = dot(mixed_ref[rows], small_ref[:, qkv_wide:wide], (1, 1)).astype(bf16)
            per = quarter // line.size
            first = (2 * s + part) * per
            loop(first, first + per, line.offer)
            loop(first, first + per, line.step)

    loop(0, seqs, attend)
    kv_ref[...] = kv_all[...]
    line.rest(line.chunks)

    def stored(c):
        for copy in row_stores(c):
            copy.wait()

    loop(0, line.chunks, stored)

    def kv_sent(s):
        for part in range(2):
            for o in range(1, nc):
                kv_copy(s, part, o, places.c).wait_send()

    loop(0, seqs, kv_sent)


def expert_kernel(
    n,
    x_hbm,
    dy_hbm,
    gates_ref,
    w_hbm,
    state_hbm,
    router_ref,
    gains_ref,
    out_ref,
    grads_hbm,
    dstate_hbm,
    dlogits_ref,
    dgain_ref,
    x_ref,
    dy_ref,
    state_ref,
    own,
    hidden_ref,
    grad_ref,
    x_turned,
    dy_turned,
    dots,    dots_all,
    dots_rows,
    w_ref,
    dstate_out,
    row_sem,
    w_sem,
    grads_sem,
    dstate_sem,
    send_dots,
    recv_dots,
    *scratch,
):
    me = lax.axis_index("tp")
    block, steps = pl.program_id(0), pl.num_programs(0)
    size_in, width = out_ref.shape
    pair = hidden_ref.shape[1] // (E // 2)
    single = pair // 2
    gu_wide = grad_ref.shape[1]
    here = aligned(block * size_in, size_in)

    def dots_copy(o, b):
        mine = dots_all.at[me, b]
        return pltpu.make_async_remote_copy(
            src_ref=mine,
            dst_ref=mine,
            send_sem=send_dots.at[o - 1, b],
            recv_sem=recv_dots.at[o - 1, b],
            device_id={"tp": lax.rem(me + o, n)},
            device_id_type=MESH,
        )

    def w_copies(p):
        spans = (aligned(p * 4 * pair, 4 * pair), aligned(gu_wide + p * 2 * pair, 2 * pair))
        return [
            pltpu.make_async_copy(w_hbm.at[:, span], w_ref.at[:, span], w_sem.at[i, p])
            for i, span in enumerate(spans)
        ]

    def row_copy(i, b):
        source, target = ((x_hbm, x_ref), (dy_hbm, dy_ref), (state_hbm, state_ref))[i]
        rows = aligned(b * size_in, size_in)
        return pltpu.make_async_copy(source.at[rows], target.at[rows], row_sem.at[i, b])

    def fetch_rows(b):
        row_copy(0, b).start()
        row_copy(1, b).start()

    def fetch_pair(i):
        for copy in w_copies(i):
            copy.start()

    def dstate_copy(c):
        return pltpu.make_async_copy(
            dstate_out.at[lax.rem(c, 2)], dstate_hbm.at[line.rows(c)], dstate_sem.at[lax.rem(c, 2)]
        )

    def finish(c, rows, total):
        per = size_in // line.size

        @pl.when(lax.rem(c, per) == 0)
        def _():
            b = c // per
            for o in range(1, n):
                dots_copy(o, b).wait_recv()
            summed = dots_all[0, b]
            for i in range(1, n):
                summed = summed + dots_all[i, b]
            summed = jnp.concatenate(
                [summed, jnp.zeros((LANES - summed.shape[0], summed.shape[1]), f32)], 0
            )
            dots_rows[aligned(b * size_in, size_in)] = summed.T

        @pl.when(c >= 2)
        def _():
            dstate_copy(c - 2).wait()

        gates = gates_ref[rows]
        lane = lax.broadcasted_iota(jnp.int32, gates.shape, 1)
        product = gates * dots_rows[rows]
        dlogits = product - gates * jnp.sum(product, -1, keepdims=True)
        dlogits = jnp.where(lane < E, dlogits, 0.0).astype(bf16)
        dlogits_ref[rows] = dlogits
        dn = total + dot(dlogits, router_ref[...], (1, 1))
        state = state_ref[rows].astype(f32)
        scale = lax.rsqrt(jnp.mean(state * state, -1, keepdims=True) + epsilon)
        unit = state * scale
        scaled = dn * gains_ref[1:2]
        inner = jnp.mean(scaled * unit, -1, keepdims=True)
        dstate = dy_ref[rows].astype(f32) + scale * (scaled - unit * inner)
        dstate_out[lax.rem(c, 2)] = dstate.astype(bf16)
        dstate_copy(c).start()
        dgain_ref[...] += folded(dn * unit)

    line = Line(n, me, own, finish, scratch, lag=size_in // (scratch[1].shape[0] // SLOTS), hop=2)
    per = size_in // line.size

    @pl.when(block == 0)
    def _():
        fetch_rows(0)
        fetch_pair(0)
        fetch_pair(1)
        barrier = pltpu.get_barrier_semaphore()
        for o in range(1, n):
            pl.semaphore_signal(
                barrier, inc=1, device_id={"tp": lax.rem(me + o, n)}, device_id_type=MESH
            )
        pl.semaphore_wait(barrier, n - 1)
        dgain_ref[...] = jnp.zeros_like(dgain_ref)


    lane = lax.broadcasted_iota(jnp.int32, (size_in, LANES), 1)
    first = lax.broadcasted_iota(jnp.int32, (size_in, pair), 1) < single
    dots[...] = jnp.zeros_like(dots)
    row_copy(0, block).wait()
    row_copy(1, block).wait()

    def gating(p, gate_pre, up_pre, raw):
        gates = gates_ref[here]
        gate = jnp.where(
            first,
            jnp.sum(jnp.where(lane == 2 * p, gates, 0.0), 1, keepdims=True),
            jnp.sum(jnp.where(lane == 2 * p + 1, gates, 0.0), 1, keepdims=True),
        )
        sigma = jax.nn.sigmoid(gate_pre)
        silu = gate_pre * sigma
        hidden = (silu * up_pre).astype(bf16).astype(f32)
        hidden_ref[here, aligned(p * pair, pair)] = (hidden * gate).astype(bf16)
        both = hidden * raw
        dots[...] += jnp.where(
            lane == 2 * p, jnp.sum(both[:, :single], 1, keepdims=True), 0.0
        ) + jnp.where(lane == 2 * p + 1, jnp.sum(both[:, single:], 1, keepdims=True), 0.0)
        dh = raw * gate
        grad_ref[here, aligned(p * 2 * pair, pair)] = (
            dh * up_pre * (sigma + silu * (1.0 - sigma))
        ).astype(bf16)
        grad_ref[here, aligned(p * 2 * pair + pair, pair)] = (dh * silu).astype(bf16)

    def two_pairs(i):
        @pl.when(block == 0)
        def _():
            for copy in w_copies(i):
                copy.wait()

            @pl.when(i + 2 < E // 4)
            def _():
                fetch_pair(i + 2)

            @pl.when(i == E // 4 - 2)
            def _():
                loop(1, steps, fetch_rows)
                loop(0, steps, lambda b: row_copy(2, b).start())

        gu = dot(x_ref[here], w_ref[:, aligned(i * 4 * pair, 4 * pair)])
        raw = dot(dy_ref[here], w_ref[:, aligned(gu_wide + i * 2 * pair, 2 * pair)])
        for j in range(2):
            at = 2 * j * pair
            gating(
                2 * i + j,
                gu[:, at : at + pair],
                gu[:, at + pair : at + 2 * pair],
                raw[:, j * pair : (j + 1) * pair],
            )

    tile = 512

    def back(i):
        at = aligned(i * tile, tile)
        own[here, at] = dot(grad_ref[here], w_ref[at, :gu_wide], (1, 1)).astype(bf16)

    def outward(i):
        at = aligned(i * tile, tile)
        carried = jnp.where(me == n // 2, state_ref[here, at].astype(f32), 0.0)
        moe = dot(hidden_ref[here], w_ref[at, gu_wide:], (1, 1))
        out_ref[:, at] = (moe + carried).astype(bf16)

    unit = per // 4
    tiles = width // tile

    def steps_at(i):
        first = block * per + i * unit
        loop(first, first + unit, line.step)

    for i in range(2):
        loop(i * (E // 8), (i + 1) * (E // 8), two_pairs)
        steps_at(i)
    dots_all[me, block] = dots[...].T[:E]
    for o in range(1, n):
        dots_copy(o, block).start()
    loop(0, tiles, back)
    loop(block * per, block * per + per, line.offer)
    steps_at(2)
    row_copy(2, block).wait()
    loop(0, tiles, outward)
    steps_at(3)

    @pl.when(block == steps - 1)
    def _():
        tall = x_turned.shape[0]
        count = width // tall
        wide = 4 * pair

        def grads_copy(m):
            rows = aligned(m * tall, tall)
            return pltpu.make_async_copy(w_ref.at[rows], grads_hbm.at[rows], grads_sem.at[m])

        def gradients(m):
            at = aligned(m * tall, tall)
            x_turned[...] = x_ref[:, at].T
            dy_turned[...] = dy_ref[:, at].T
            for i in range(gu_wide // wide):
                to = slice(i * wide, (i + 1) * wide)
                w_ref[at, to] = dot(x_turned[...], grad_ref[:, to]).astype(bf16)
            for i in range(gu_wide // wide // 2):
                to = slice(i * wide, (i + 1) * wide)
                w_ref[at, gu_wide + i * wide : gu_wide + (i + 1) * wide] = dot(
                    dy_turned[...], hidden_ref[:, to]
                ).astype(bf16)
            grads_copy(m).start()
            loop(steps * per + m * unit, steps * per + (m + 1) * unit, line.step)

        loop(0, count, gradients)
        line.rest(steps * per + count * unit)
        for c in range(line.chunks - 2, line.chunks):
            dstate_copy(c).wait()

        def dots_sent(b):
            for o in range(1, n):
                dots_copy(o, b).wait_send()

        loop(0, steps, dots_sent)
        loop(0, count, lambda m: grads_copy(m).wait())


def rear_kernel(
    n,
    nf,
    nc,
    moe_hbm,
    low_hbm,
    small_hbm,
    query_hbm,
    kv_hbm,
    x_hbm,
    normed_two_hbm,
    mixed_hbm,
    dlogits_hbm,
    gains_ref,
    dgain_two_ref,
    cos_ref,
    sin_ref,
    act_hbm,
    input_hbm,
    dgains_ref,
    grads_ref,
    moe_ref,
    low_ref,
    wout_ref,
    query_ref,
    kv_ref,
    wqkv_ref,
    x_ref,
    normed_two_ref,
    mixed_ref,
    dlogits_ref,
    dmixed,
    dquery,
    dkv,
    dkv_in,
    dqkv_ref,
    own,
    scales,
    dgain,
    gains_in,
    grads,
    grads_near,
    grads_far,
    moe_sem,
    load_sem,
    store_sem,
    send_kv,
    recv_kv,
    send_gain,
    recv_gain,
    send_near,
    recv_near,
    send_far,
    recv_far,
    *scratch,
):
    me = lax.axis_index("tp")
    flat = lax.axis_index("fsdp") * nc + lax.axis_index("ctx")
    places = Places(nc)
    quarter = places.quarter
    seqs = kv_ref.shape[0]
    q_wide, k_wide = query_ref.shape[1], kv_ref.shape[2] // 2
    group = q_wide // k_wide
    qkv_wide = q_wide + 2 * k_wide
    kv_heads = k_wide // HEAD_SIZE
    factor = 1.0 / math.sqrt(HEAD_SIZE)
    peers, padded = grads.shape[:2]
    shard = grads_ref.shape[0]
    loads = [
        pltpu.make_async_copy(source, target, load_sem.at[i])
        for i, (source, target) in enumerate(
            (
                (low_hbm, low_ref),
                (small_hbm.at[:, pl.ds(qkv_wide, wout_ref.shape[1])], wout_ref),
                (query_hbm, query_ref),
                (kv_hbm, kv_ref),
                (small_hbm.at[:, pl.ds(0, qkv_wide)], wqkv_ref),
                (x_hbm, x_ref),
                (normed_two_hbm, normed_two_ref),
                (mixed_hbm, mixed_ref),
                (dlogits_hbm, dlogits_ref),
            )
        )
    ]
    portions = moe_sem.shape[0]
    portion = moe_ref.shape[0] // portions

    def moe_load(i):
        rows = aligned(i * portion, portion)
        return pltpu.make_async_copy(moe_hbm.at[rows], moe_ref.at[rows], moe_sem.at[i])

    loop(0, portions, lambda i: moe_load(i).start())

    def peer(o):
        other = lax.rem(flat + o, peers)
        return {"fsdp": other // nc, "ctx": lax.rem(other, nc)}

    f = lax.axis_index("fsdp")

    def near_copy(p, g):
        return pltpu.make_async_remote_copy(
            src_ref=grads.at[g * nc + places.after(p)],
            dst_ref=grads_near.at[p - 1, g],
            send_sem=send_near.at[p - 1, g],
            recv_sem=recv_near.at[p - 1, g],
            device_id={"ctx": places.after(p)},
            device_id_type=MESH,
        )

    def far_copy(o):
        other = lax.rem(f + o, nf)
        return pltpu.make_async_remote_copy(
            src_ref=grads.at[other * nc + places.c],
            dst_ref=grads_far.at[o],
            send_sem=send_far.at[o],
            recv_sem=recv_far.at[o],
            device_id={"fsdp": other},
            device_id_type=MESH,
        )

    def gain_copy(o):
        return pltpu.make_async_remote_copy(
            src_ref=gains_in.at[0],
            dst_ref=gains_in.at[o],
            send_sem=send_gain.at[o],
            recv_sem=recv_gain.at[o],
            device_id=peer(o),
            device_id_type=MESH,
        )

    def kv_copy(s, part, o, rank):
        return pltpu.make_async_remote_copy(
            src_ref=dkv.at[s, places.rows(rank, part)],
            dst_ref=dkv_in.at[o - 1, s, part],
            send_sem=send_kv.at[o - 1, s, part],
            recv_sem=recv_kv.at[o - 1, s, part],
            device_id={"ctx": places.after(o)},
            device_id_type=MESH,
        )

    def finish_out(c, rows, total):
        moe_ref[rows] = total.astype(bf16)

    def finish_in(c, rows, total):
        x = x_ref[rows].astype(f32)
        scale = lax.rsqrt(jnp.mean(x * x, -1, keepdims=True) + epsilon)
        unit = x * scale
        scaled = total * gains_ref[:1]
        inner = jnp.mean(scaled * unit, -1, keepdims=True)
        own[rows] = (low_ref[rows].astype(f32) + scale * (scaled - unit * inner)).astype(bf16)
        dgain[...] += folded(total * unit)

    outward = Line(n, me, moe_ref, finish_out, scratch[:7], lag=1, hop=2)
    inward = Line(n, me, own, finish_in, scratch[7:], hop=2)
    dgain[...] = jnp.zeros_like(dgain)
    greet(me, n, [peer(o) for o in range(1, peers)])

    def offer(i):
        per = outward.chunks // portions
        moe_load(i).wait()
        loop(i * per, (i + 1) * per, outward.offer)

    heads, early = q_wide // HEAD_SIZE, 4
    for load in loads[:4]:
        load.start()
    loop(0, portions, offer)
    loop(0, early, outward.step)
    for load in loads[:4]:
        load.wait()
    for load in loads[4:]:
        load.start()


    def turned_back(y, part):
        wide = y.shape[1]
        here = pl.ds(part * quarter, quarter)
        return y * widened(cos_ref[here], wide) - swapped_halves(y) * widened(sin_ref[here], wide)

    def attend(s):
        for part in (1, 0):
            rows = places.own(s, part)
            keys = places.keys(part)
            dmixed[...] = dot(low_ref[rows], wout_ref[...]).astype(bf16)
            start = places.slot(places.c, part) * quarter
            allowed = lax.broadcasted_iota(jnp.int32, (keys, quarter), 0) <= (
                start + lax.broadcasted_iota(jnp.int32, (keys, quarter), 1)
            )
            for k in range(kv_heads):
                at = k * HEAD_SIZE
                key = kv_ref[s, :keys, at : at + HEAD_SIZE]
                value = kv_ref[s, :keys, k_wide + at : k_wide + at + HEAD_SIZE]
                dkey = dvalue = None
                for h in range(k * group, (k + 1) * group):
                    head = slice(h * HEAD_SIZE, (h + 1) * HEAD_SIZE)
                    query = query_ref[rows, head]
                    dout = dmixed[:, head]
                    scores = jnp.where(allowed, dot(key, query, (1, 1)), -1e30)
                    raised = jnp.exp(scores - jnp.max(scores, 0, keepdims=True))
                    probs = raised * (1.0 / jnp.sum(raised, 0, keepdims=True))
                    product = probs * dot(value, dout, (1, 1))
                    dscores = product - probs * jnp.sum(product, 0, keepdims=True)
                    dscores = dscores.astype(bf16)
                    dquery[:, head] = dot(dscores, key, (0, 0)) * factor
                    dk, dv = dot(dscores, query), dot(probs.astype(bf16), dout)
                    dkey = dk if dkey is None else dkey + dk
                    dvalue = dv if dvalue is None else dvalue + dv
                    outward.step(early + (2 * s + 1 - part) * heads + h)
                for first, add in ((at, dkey), (k_wide + at, dvalue)):
                    lanes = slice(first, first + HEAD_SIZE)
                    if part == 1:
                        dkv[s, :keys, lanes] = add
                    else:
                        dkv[s, :keys, lanes] += add
            dqkv_ref[rows, :q_wide] = turned_back(dquery[...], part).astype(bf16)
        for part in range(2):
            for o in range(1, nc):
                kv_copy(s, part, o, places.after(o)).start()

    loop(0, seqs, attend)
    done = early + 2 * seqs * heads
    for load in loads[4:]:
        load.wait()
    per = quarter // inward.size

    def turn_back(s):
        for part in range(2):
            rows = places.own(s, part)
            mine = dkv[s, places.rows(places.c, part)]
            for o in range(1, nc):
                kv_copy(s, part, o, places.after(o)).wait()
                mine = mine + dkv_in[o - 1, s, part]
            dqkv_ref[rows, q_wide : q_wide + k_wide] = turned_back(mine[:, :k_wide], part).astype(
                bf16
            )
            dqkv_ref[rows, q_wide + k_wide :] = mine[:, k_wide:].astype(bf16)
            own[rows] = dot(dqkv_ref[rows], wqkv_ref[...], (1, 1)).astype(bf16)
            first = (2 * s + part) * per
            loop(first, first + per, inward.offer)
            outward.step(done + 2 * s + part)
            x = x_ref[rows].astype(f32)
            scale = lax.rsqrt(jnp.mean(x * x, -1, keepdims=True) + epsilon)
            scales[rows] = jnp.broadcast_to(scale, (quarter, LANES))

    loop(0, seqs, turn_back)
    wide, mid = dqkv_ref.shape[1], dqkv_ref.shape[1] + mixed_ref.shape[1]
    span = max(LANES, shard * LANES // math.gcd(shard, LANES))
    count = span // shard

    def weights(i):
        at = aligned(i * span, span)
        to = pl.ds(i * count, count)

        def put(lanes, value):
            value = value.reshape(count, shard, value.shape[1])
            if padded > shard:
                more = jnp.zeros((count, padded - shard, value.shape[2]), f32)
                value = jnp.concatenate([value, more], 1)
            grads[to, :, lanes] = value.astype(bf16)

        normed = x_ref[:, at].astype(f32) * widened(scales[...], span) * gains_ref[:1, at]
        put(slice(0, wide), dot(normed.astype(bf16), dqkv_ref[...], (0, 0)))
        put(slice(wide, mid), dot(low_ref[:, at], mixed_ref[...], (0, 0)))
        put(slice(mid, grads.shape[2]), dot(normed_two_ref[:, at], dlogits_ref[...], (0, 0)))
        outward.step(done + 2 * seqs + i)

    spans = x_ref.shape[1] // span
    loop(0, spans, weights)
    def send_share(g):
        for p in range(1, nc):
            near_copy(p, g).start()

    loop(0, nf, send_share)
    start = done + 2 * seqs + spans
    ahead = max(outward.steps - start, 0)

    def both(i):
        outward.step(start + i)
        inward.step(i)

    loop(0, ahead, both)
    outward.rest(start + ahead)

    def add_share(g):
        mine = g * nc + places.c
        total = grads[mine].astype(f32)
        for p in range(1, nc):
            near_copy(p, g).wait()
            total = total + grads_near[p - 1, g].astype(f32)
        grads[mine] = total.astype(bf16)

    stores = [
        pltpu.make_async_copy(source, target, store_sem.at[i])
        for i, (source, target) in enumerate(((moe_ref, act_hbm), (own, input_hbm)))
    ]
    stores[0].start()
    enough = ahead + inward.chunks // 2
    loop(ahead, enough, inward.step)
    loop(0, nf, add_share)
    loop(1, nf, lambda o: far_copy(o).start())
    inward.rest(enough)
    stores[1].start()
    one = jnp.sum(dgain[...], 0, keepdims=True)
    two = jnp.sum(dgain_two_ref[...], 0, keepdims=True)
    gains_in[0] = jnp.concatenate([one, two], 1)
    loop(1, peers, lambda o: gain_copy(o).start())
    grads_ref[...] = grads[flat].astype(f32)[:shard]

    def add_grad(o):
        far_copy(o).wait()
        grads_ref[...] += grads_far[o].astype(f32)[:shard]

    loop(1, nf, add_grad)
    loop(1, peers, lambda o: gain_copy(o).wait())
    dgains_ref[...] = gains_in[0]

    def add(o):
        dgains_ref[...] += gains_in[o]

    loop(1, peers, add)
    for store in stores:
        store.wait()


def split_kernel(
    ffn,
    nc,
    grads_ref,
    small_ref,
    dgains_ref,
    out_hbm,
    input_hbm,
    gate_ref,
    up_ref,
    down_ref,
    query_ref,
    key_ref,
    value_ref,
    out_ref,
    router_ref,
    gain_ref,
    act_hbm,
    grad_hbm,
    act,
    grad,
    load,
    store,
):
    loads = [
        pltpu.make_async_copy(input_hbm, grad, load.at[0]),
        pltpu.make_async_copy(out_hbm, act, load.at[1]),
    ]
    stores = [
        pltpu.make_async_copy(grad, grad_hbm, store.at[0]),
        pltpu.make_async_copy(act, act_hbm, store.at[1]),
    ]
    for copy in loads:
        copy.start()
    gu_wide = 2 * E * ffn
    at = 0
    for ref in (query_ref, key_ref, value_ref, out_ref):
        ref[...] = small_ref[:, at : at + ref.shape[1]]
        at += ref.shape[1]
    router_ref[...] = small_ref[:, at:].T[:E]
    width, shard = input_hbm.shape[1], small_ref.shape[0]
    flat = lax.axis_index("fsdp") * nc + lax.axis_index("ctx")
    shift = lax.rem(width - flat * shard, width)
    for i in range(2):
        row = jnp.broadcast_to(dgains_ref[:, i * width : (i + 1) * width], (8, width))
        gain_ref[i : i + 1] = pltpu.roll(row, shift, 1)[:1, :shard]
    loads[0].wait()
    stores[0].start()
    loads[1].wait()
    stores[1].start()
    for e in range(E):
        at = (e // 2) * 4 * ffn + (e % 2) * ffn
        gate_ref[e] = grads_ref[:, at : at + ffn].astype(f32)
        up_ref[e] = grads_ref[:, at + 2 * ffn : at + 3 * ffn].astype(f32)
        at = gu_wide + e * ffn
        down_ref[e] = grads_ref[:, at : at + ffn].astype(f32)
    for copy in stores:
        copy.wait()


def call(kernel, outs, scratch, collective_id, operands, specs=None):
    total = sum(math.prod(o.shape) * o.dtype.itemsize for o in [*outs, *operands])
    return pl.pallas_call(
        kernel,
        out_shape=tuple(outs),
        in_specs=[WHOLE] * len(operands),
        out_specs=specs or (WHOLE,) * len(outs),
        scratch_shapes=scratch,
        compiler_params=pltpu.CompilerParams(
            collective_id=collective_id, has_side_effects=True, vmem_limit_bytes=VMEM_BYTES
        ),
        cost_estimate=pl.CostEstimate(flops=0, bytes_accessed=total, transcendentals=0),
    )(*operands)


def per_device(
    tokens,
    routes,
    gain_attn,
    w_query,
    key_matrix,
    value_matrix,
    w_out,
    gain_moe,
    w_router,
    w_gate,
    w_up,
    w_down,
    cotangent,
):
    shaped = jax.ShapeDtypeStruct
    rows, width = tokens.shape
    nc, n = lax.axis_size("ctx"), lax.axis_size("tp")
    half = SEQUENCE_LENGTH // nc
    seqs = rows // half
    both = ("fsdp", "ctx")
    q_wide, k_wide, o_wide = w_query.shape[1], key_matrix.shape[1], w_out.shape[0]
    qkv_wide = q_wide + 2 * k_wide
    ffn = w_gate.shape[2]
    shard = w_gate.shape[1]

    gu_wide, down_wide = 2 * E * ffn, E * ffn
    small_wide = qkv_wide + o_wide + LANES
    nf = lax.axis_size("fsdp")
    peers = nf * nc
    link = bf16 if shard % 16 == 0 else f32
    def sems(*dims):
        return pltpu.SemaphoreType.DMA(dims)

    small, gains, packed, cos, sin, named = call(
        functools.partial(gather_kernel, nf, nc, ffn),
        [
            shaped((peers, shard, small_wide), link),
            shaped((8, width), f32),
            shaped((shard, gu_wide + down_wide), bf16),
            shaped((half, LANES), f32),
            shaped((half, LANES), f32),
            shaped((rows, LANES), f32),
        ],
        [
            sems(nf),
            sems(nf),
            sems(nc - 1, nf),
            sems(nc - 1, nf),
        ],
        4,
        (
            w_query,
            key_matrix,
            value_matrix,
            w_out.T,
            w_router.T,
            gain_attn,
            gain_moe,
            w_gate,
            w_up,
            jnp.swapaxes(w_down, 1, 2),
            routes.T,
        ),
    )
    experts = lax.all_gather(packed, both, axis=0, tiled=True)
    small = small.reshape(width, small_wide).astype(bf16)
    kv_sems = sems(nc - 1, seqs, 2)
    anywhere = pl.BlockSpec(memory_space=pl.ANY)
    query, kv, mixed, state, normed_two, gates = call(
        functools.partial(front_kernel, n, nc),
        [
            shaped((rows, q_wide), bf16),
            shaped((seqs, SEQUENCE_LENGTH, 2 * k_wide), bf16),
            shaped((rows, q_wide), bf16),
            shaped((rows, width), bf16),
            shaped((rows, width), bf16),
            shaped((rows, LANES), f32),
        ],
        [
            pltpu.VMEM((seqs, SEQUENCE_LENGTH, 2 * k_wide), bf16),
            *[pltpu.VMEM((rows, width), bf16)] * 3,
            sems(2, rows // 32),
            kv_sems,
            kv_sems,
            *line_scratch(rows, width, 32),
        ],
        0,
        (tokens, small, gains, named, cos, sin),
        (WHOLE, WHOLE, WHOLE, anywhere, anywhere, WHOLE),
    )

    block = 256

    def by_rows(wide):
        return pl.BlockSpec((block, wide), lambda i: (i, 0))

    def constant(*dims):
        return pl.BlockSpec(
            dims, lambda i: (0,) * len(dims), pipeline_mode=pl.Buffered(1)
        )

    anywhere = pl.BlockSpec(memory_space=pl.ANY)
    blocks = rows // block
    size, tall = 64, 256
    dots_sems = pltpu.SemaphoreType.DMA((n - 1, blocks))
    moe_part, grad_experts, low, dlogits, dgain_two = pl.pallas_call(
        functools.partial(expert_kernel, n),
        grid=(blocks,),
        out_shape=(
            shaped((rows, width), bf16),
            shaped((width, gu_wide + down_wide), bf16),
            shaped((rows, width), bf16),
            shaped((rows, LANES), bf16),
            shaped((8, width), f32),
        ),
        in_specs=[
            anywhere,
            anywhere,
            constant(rows, LANES),
            anywhere,
            anywhere,
            pl.BlockSpec(
                (width, LANES),
                lambda i: (0, small_wide // LANES - 1),
                pipeline_mode=pl.Buffered(1),
            ),
            constant(8, width),
        ],
        out_specs=(
            by_rows(width),
            anywhere,
            anywhere,
            pl.BlockSpec((rows, LANES), lambda i: (0, 0)),
            pl.BlockSpec((8, width), lambda i: (0, 0)),
        ),
        scratch_shapes=[
            *[pltpu.VMEM((rows, width), bf16)] * 4,
            pltpu.VMEM((rows, down_wide), bf16),
            pltpu.VMEM((rows, gu_wide), bf16),
            pltpu.VMEM((tall, rows), bf16),
            pltpu.VMEM((tall, rows), bf16),
            pltpu.VMEM((block, LANES), f32),
            pltpu.VMEM((n, blocks, E, block), f32),
            pltpu.VMEM((rows, LANES), f32),
            pltpu.VMEM((width, gu_wide + down_wide), bf16),
            pltpu.VMEM((2, size, width), bf16),
            sems(3, blocks),
            sems(2, E // 4),
            sems(width // tall),
            sems(2),
            dots_sems,
            dots_sems,
            *line_scratch(rows, width, size),
        ],
        compiler_params=pltpu.CompilerParams(
            collective_id=1, has_side_effects=True, vmem_limit_bytes=VMEM_BYTES
        ),
        cost_estimate=pl.CostEstimate(
            flops=18 * rows * width * down_wide,
            bytes_accessed=2 * width * (gu_wide + down_wide),
            transcendentals=0,
        ),
    )(normed_two, cotangent, gates, experts, state, small, gains)

    low, grad_experts = lax.optimization_barrier((low, grad_experts))
    grad_experts = lax.psum_scatter(grad_experts, both, scatter_dimension=0, tiled=True)

    def small_block(*dims):
        return pltpu.VMEM((*dims, -(-shard // 16) * 16, small_wide), bf16)

    whole = pltpu.VMEM((rows, width), bf16)
    sources = (moe_part, low, small, query, kv, tokens, normed_two, mixed, dlogits)
    held = (
        *[(rows, width)] * 2,
        (width, o_wide),
        query.shape,
        kv.shape,
        (width, qkv_wide),
        *[(rows, width)] * 2,
        mixed.shape,
        dlogits.shape,
    )
    activations, input_grad, dgains, grad_small = pl.pallas_call(
        functools.partial(rear_kernel, n, nf, nc),
        out_shape=(
            shaped((rows, width), bf16),
            shaped((rows, width), bf16),
            shaped((1, 2 * width), f32),
            shaped((shard, small_wide), f32),
        ),
        in_specs=[anywhere] * len(sources) + [WHOLE] * 4,
        out_specs=(anywhere, anywhere, WHOLE, WHOLE),
        scratch_shapes=[
            *[pltpu.VMEM(dims, bf16) for dims in held],
            pltpu.VMEM((half // 2, q_wide), bf16),
            pltpu.VMEM((half // 2, q_wide), f32),
            pltpu.VMEM((seqs, SEQUENCE_LENGTH, 2 * k_wide), f32),
            pltpu.VMEM((nc - 1, seqs, 2, half // 2, 2 * k_wide), f32),
            pltpu.VMEM((rows, qkv_wide), bf16),
            whole,
            pltpu.VMEM((rows, LANES), f32),
            pltpu.VMEM((8, width), f32),
            pltpu.VMEM((peers, 1, 2 * width), f32),
            small_block(peers),
            small_block(nc - 1, nf),
            small_block(nf),
            sems(4),
            sems(len(held) - 1),
            sems(2),
            kv_sems,
            kv_sems,
            *[sems(peers)] * 2,
            *[sems(nc - 1, nf)] * 2,
            *[sems(nf)] * 2,
            *line_scratch(rows, width, 32),
            *line_scratch(rows, width, 32),
        ],
        compiler_params=pltpu.CompilerParams(
            collective_id=3, has_side_effects=True, vmem_limit_bytes=VMEM_BYTES
        ),
        cost_estimate=pl.CostEstimate(
            flops=12 * rows * width * small_wide,
            bytes_accessed=16 * rows * width,
            transcendentals=0,
        ),
    )(*sources, gains, dgain_two, cos, sin)
    results = pl.pallas_call(
        functools.partial(split_kernel, ffn, nc),
        out_shape=(
            shaped((E, shard, ffn), f32),
            shaped((E, shard, ffn), f32),
            shaped((E, shard, ffn), f32),
            shaped((shard, q_wide), f32),
            shaped((shard, k_wide), f32),
            shaped((shard, k_wide), f32),
            shaped((shard, o_wide), f32),
            shaped((E, shard), f32),
            shaped((2, shard), f32),
            shaped((rows, width), bf16),
            shaped((rows, width), bf16),
        ),
        in_specs=[WHOLE, WHOLE, WHOLE, anywhere, anywhere],
        out_specs=(*[WHOLE] * 9, anywhere, anywhere),
        scratch_shapes=[
            pltpu.VMEM((rows, width), bf16),
            pltpu.VMEM((rows, width), bf16),
            sems(2),
            sems(2),
        ],
        compiler_params=pltpu.CompilerParams(vmem_limit_bytes=VMEM_BYTES),
    )(grad_experts, grad_small, dgains, activations, input_grad)
    grad_gate, grad_up, grad_down, grad_query, grad_key, grad_value, grad_out = results[:7]
    grad_router, dgains = results[7:9]
    return (
        results[9],
        results[10],
        dgains[0],
        grad_query,
        grad_key,
        grad_value,
        grad_out.T,
        dgains[1],
        grad_router.T,
        grad_gate,
        grad_up,
        jnp.swapaxes(grad_down, 1, 2),
    )


def solution(mesh):
    specs = (
        P(("fsdp", "ctx"), None),
        P(("fsdp", "ctx"), None),
        P(("fsdp", "ctx")),
        P(("fsdp", "ctx"), "tp"),
        P(("fsdp", "ctx"), "tp"),
        P(("fsdp", "ctx"), "tp"),
        P("tp", ("fsdp", "ctx")),
        P(("fsdp", "ctx")),
        P(("fsdp", "ctx"), None),
        P(None, ("fsdp", "ctx"), "tp"),
        P(None, ("fsdp", "ctx"), "tp"),
        P(None, "tp", ("fsdp", "ctx")),
        P(("fsdp", "ctx"), None),
    )
    return jax.shard_map(
        per_device,
        mesh=mesh,
        in_specs=specs,
        out_specs=(
            P(("fsdp", "ctx"), None),
            P(("fsdp", "ctx"), None),
            P(("fsdp", "ctx")),
            P(("fsdp", "ctx"), "tp"),
            P(("fsdp", "ctx"), "tp"),
            P(("fsdp", "ctx"), "tp"),
            P("tp", ("fsdp", "ctx")),
            P(("fsdp", "ctx")),
            P(("fsdp", "ctx"), None),
            P(None, ("fsdp", "ctx"), "tp"),
            P(None, ("fsdp", "ctx"), "tp"),
            P(None, "tp", ("fsdp", "ctx")),
        ),
        check_vma=False,
    )
```

```python
import functools
import math

import jax
import jax.numpy as jnp
from jax import lax
from jax.experimental import pallas as pl
from jax.experimental.pallas import tpu as pltpu
from jax.sharding import PartitionSpec as P

HEAD_SIZE = 64
TOPK = 8
E = 16
SEQUENCE_LENGTH = 1024
LANES = 128
VMEM_BYTES = 60 * 2**20

epsilon = 1e-06
f32 = jnp.float32
bf16 = jnp.bfloat16
MESH = pl.DeviceIdType.MESH
WHOLE = pl.BlockSpec(memory_space=pltpu.VMEM)


def aligned(start, size):
    return pl.ds(pl.multiple_of(start, size), size)


def dot(a, b, at=(1, 0)):
    return lax.dot_general(a, b, (((at[0],), (at[1],)), ((), ())), preferred_element_type=f32)


def swapped_halves(y):
    wide, halfway = y.shape[1], HEAD_SIZE // 2
    lane = lax.broadcasted_iota(jnp.int32, y.shape, 1)
    lower = lax.rem(lane, HEAD_SIZE) < halfway
    return jnp.where(lower, -pltpu.roll(y, wide - halfway, 1), pltpu.roll(y, halfway, 1))


def widened(table, wide):
    return jnp.concatenate([table] * (wide // LANES), 1)


SLOTS = 4


def line_scratch(rows, width, size):
    sems = pltpu.SemaphoreType.DMA((rows // size,))
    slots = pltpu.VMEM((SLOTS * size, width), bf16)
    return [pltpu.VMEM((2 * rows, width), bf16), slots, slots, *[sems] * 4]


def greet(me, n, others=()):
    barrier = pltpu.get_barrier_semaphore()

    @pl.when(me > 0)
    def _():
        pl.semaphore_signal(
            barrier, inc=1, device_id={"tp": lax.rem(me + n - 1, n)}, device_id_type=MESH
        )

    @pl.when(me < n - 1)
    def _():
        pl.semaphore_signal(
            barrier, inc=1, device_id={"tp": lax.rem(me + 1, n)}, device_id_type=MESH
        )

    for other in others:
        pl.semaphore_signal(barrier, inc=1, device_id=other, device_id_type=MESH)
    count = jnp.where(me > 0, 1, 0) + jnp.where(me < n - 1, 1, 0) + len(others)
    pl.semaphore_wait(barrier, count)


class Line:
    def __init__(self, n, me, own, finish, scratch, lag=0, hop=1, late=0):
        self.n, self.me, self.own, self.finish = n, me, own, finish
        self.arrived, self.to_right, self.to_left = scratch[:3]
        self.send_right, self.recv_left, self.send_left, self.recv_right = scratch[3:]
        self.size = self.to_right.shape[0] // SLOTS
        self.total = self.arrived.shape[0] // 2
        self.chunks = self.total // self.size
        self.lag, self.hop, self.late = lag, hop, late
        self.steps = self.chunks + lag + hop * (n - 2) + late
        self.middle = (me > 0) & (me < n - 1)

    def rows(self, c):
        return aligned(c * self.size, self.size)

    def left_rows(self, c):
        return aligned(c * self.size, self.size)

    def right_rows(self, c):
        return aligned(self.total + c * self.size, self.size)

    def slot(self, c):
        return aligned(lax.rem(c, SLOTS) * self.size, self.size)

    def right(self, c, end=False):
        return pltpu.make_async_remote_copy(
            src_ref=self.own.at[self.rows(c)] if end else self.to_right.at[self.slot(c)],
            dst_ref=self.arrived.at[self.left_rows(c)],
            send_sem=self.send_right.at[c],
            recv_sem=self.recv_left.at[c],
            device_id={"tp": lax.rem(self.me + 1, self.n)},
            device_id_type=MESH,
        )

    def left(self, c, end=False):
        return pltpu.make_async_remote_copy(
            src_ref=self.own.at[self.rows(c)] if end else self.to_left.at[self.slot(c)],
            dst_ref=self.arrived.at[self.right_rows(c)],
            send_sem=self.send_left.at[c],
            recv_sem=self.recv_right.at[c],
            device_id={"tp": lax.rem(self.me + self.n - 1, self.n)},
            device_id_type=MESH,
        )

    def offer(self, c):
        @pl.when(self.me == 0)
        def _():
            self.right(c, True).start()

        @pl.when(self.me == self.n - 1)
        def _():
            self.left(c, True).start()

    def step(self, t):
        n, me, chunks = self.n, self.me, self.chunks
        go, come = t - self.lag - self.hop * (me - 1), t - self.lag - self.hop * (n - 2 - me)
        done = jnp.minimum(go, come) - jnp.where(self.middle, 0, self.late)
        nearer_left = me < n - 1 - me

        def inside(c):
            return (c >= 0) & (c < chunks)

        @pl.when(self.middle & inside(go) & nearer_left)
        def _():
            self.right_pass(go)

        @pl.when(self.middle & inside(come))
        def _():
            self.left_pass(come)

        @pl.when(self.middle & inside(go) & jnp.logical_not(nearer_left))
        def _():
            self.right_pass(go)

        @pl.when(inside(done))
        def _():
            @pl.when(me == 0)
            def _():
                self.left(done).wait_recv()
                self.right(done, True).wait_send()

            @pl.when(me == n - 1)
            def _():
                self.right(done).wait_recv()
                self.left(done, True).wait_send()

            rows = self.rows(done)
            at = done * self.size
            one = aligned(jnp.where(me == 0, self.total, 0) + at, self.size)
            two = aligned(jnp.where(me == n - 1, 0, self.total) + at, self.size)
            total = self.own[rows].astype(f32) + self.arrived[one].astype(f32)
            other = self.arrived[two].astype(f32)
            self.finish(done, rows, total + jnp.where(self.middle, other, 0.0))

    def right_pass(self, c):
        self.right(c).wait_recv()

        @pl.when(c >= SLOTS)
        def _():
            self.right(c - SLOTS).wait_send()

        total = self.own[self.rows(c)].astype(f32) + self.arrived[self.left_rows(c)].astype(f32)
        self.to_right[self.slot(c)] = total.astype(bf16)
        self.right(c).start()

    def left_pass(self, c):
        self.left(c).wait_recv()

        @pl.when(c >= SLOTS)
        def _():
            self.left(c - SLOTS).wait_send()

        total = self.own[self.rows(c)].astype(f32) + self.arrived[self.right_rows(c)].astype(f32)
        self.to_left[self.slot(c)] = total.astype(bf16)
        self.left(c).start()

    def rest(self, start):
        loop(start, self.steps, self.step)

        @pl.when(self.middle)
        def _():
            def sent(c):
                self.right(c).wait_send()
                self.left(c).wait_send()

            loop(max(self.chunks - SLOTS, 0), self.chunks, sent)


def loop(low, high, body):
    lax.fori_loop(low, high, lambda i, carry: (body(i), carry)[1], 0)


def folded(values):
    rows, width = values.shape
    return jnp.sum(values.reshape(rows // 8, 8, width), 0)


class Places:
    def __init__(self, nc):
        self.nc = nc
        self.c = lax.axis_index("ctx")
        self.quarter = SEQUENCE_LENGTH // nc // 2

    def slot(self, rank, part):
        return rank if part == 0 else 2 * self.nc - 1 - rank

    def rows(self, rank, part):
        return aligned(self.slot(rank, part) * self.quarter, self.quarter)

    def own(self, s, part):
        return aligned((2 * s + part) * self.quarter, self.quarter)

    def keys(self, part):
        return self.quarter * (self.nc if part == 0 else 2 * self.nc)

    def after(self, o):
        return lax.rem(self.c + o, self.nc)

    def before(self, o):
        return lax.rem(self.c + self.nc - o, self.nc)


def gather_kernel(
    nf,
    nc,
    ffn,
    query_ref,
    key_ref,
    value_ref,
    out_ref,
    router_ref,
    gain_one_ref,
    gain_two_ref,
    gate_ref,
    up_ref,
    down_ref,
    routes_ref,
    small_all,
    gains_ref,
    experts_ref,
    cos_ref,
    sin_ref,
    named_ref,
    send_f,
    recv_f,
    send_c,
    recv_c,
):
    f, c = lax.axis_index("fsdp"), lax.axis_index("ctx")
    shard = small_all.shape[1]
    kind = small_all.dtype
    mine = f * nc + c

    def from_f(o):
        return lax.rem(f + nf - o, nf)

    def to_peer(o):
        return {"fsdp": lax.rem(f + o, nf)}

    def to_near(p):
        return {"ctx": lax.rem(c + p, nc)}

    relay = nf == 4 and shard % 32 == 0
    across, along = f - lax.rem(f, 2) + 1 - lax.rem(f, 2), lax.rem(f + 2, 4)
    if relay:
        far = [{"fsdp": across}, {"fsdp": along}]
    else:
        far = [to_peer(o) for o in range(1, nf)]
    barrier = pltpu.get_barrier_semaphore()
    for other in far + [to_near(p) for p in range(1, nc)]:
        pl.semaphore_signal(barrier, inc=1, device_id=other, device_id_type=MESH)
    gains = [g[...].astype(f32).reshape(1, shard) for g in (gain_one_ref, gain_two_ref)]
    blank = jnp.zeros((LANES - E - 2, shard), f32)
    last = jnp.concatenate([router_ref[...].astype(f32), *gains, blank], 0).T
    at = 0
    for piece in (query_ref[...], key_ref[...], value_ref[...], out_ref[...], last):
        small_all[mine, :, at : at + piece.shape[1]] = piece.astype(kind)
        at += piece.shape[1]
    pl.semaphore_wait(barrier, len(far) + nc - 1)

    owners = [f, across, along, 3 - f] if relay else [from_f(o) for o in range(nf)]

    def relay_copy(i):
        owner, to = ((f, across), (f, along), (across, along), (along, across))[i]
        block = small_all.at[owner * nc + c]
        if i > 1:
            block = block.at[pl.ds((i - 2) * (shard // 2), shard // 2)]
        return pltpu.make_async_remote_copy(
            src_ref=block,
            dst_ref=block,
            send_sem=send_f.at[i],
            recv_sem=recv_f.at[i],
            device_id={"fsdp": to},
            device_id_type=MESH,
        )

    def relay_arrival(i):
        block = small_all.at[(across, along, 3 - f, 3 - f)[i] * nc + c]
        if i > 1:
            block = block.at[pl.ds((i - 2) * (shard // 2), shard // 2)]
        return pltpu.make_async_remote_copy(
            src_ref=block,
            dst_ref=block,
            send_sem=send_f.at[i],
            recv_sem=recv_f.at[i],
            device_id={"fsdp": across},
            device_id_type=MESH,
        )

    def far_copy(o, rank):
        block = small_all.at[rank * nc + c]
        return pltpu.make_async_remote_copy(
            src_ref=block,
            dst_ref=block,
            send_sem=send_f.at[o],
            recv_sem=recv_f.at[o],
            device_id=to_peer(o),
            device_id_type=MESH,
        )

    def near_copy(p, o, rank):
        block = small_all.at[owners[o] * nc + rank]
        return pltpu.make_async_remote_copy(
            src_ref=block,
            dst_ref=block,
            send_sem=send_c.at[p - 1, o],
            recv_sem=recv_c.at[p - 1, o],
            device_id=to_near(p),
            device_id_type=MESH,
        )

    def share(o):
        for p in range(1, nc):
            near_copy(p, o, c).start()

    if relay:
        relay_copy(0).start()
        relay_copy(1).start()
    else:
        loop(1, nf, lambda o: far_copy(o, f).start())
    share(0)
    for e in range(E):
        at = (e // 2) * 4 * ffn + (e % 2) * ffn
        experts_ref[:, at : at + ffn] = gate_ref[e]
        experts_ref[:, at + 2 * ffn : at + 3 * ffn] = up_ref[e]
        at = 2 * E * ffn + e * ffn
        experts_ref[:, at : at + ffn] = down_ref[e]

    half = cos_ref.shape[0]
    quarter = half // 2
    row = lax.broadcasted_iota(jnp.int32, (half, LANES), 0)
    lane = lax.broadcasted_iota(jnp.int32, (half, LANES), 1)
    late = SEQUENCE_LENGTH - (c + 1) * quarter + row - quarter
    place = jnp.where(row < quarter, c * quarter + row, late)
    lane = lax.rem(lane, HEAD_SIZE // 2).astype(f32)
    angle = place.astype(f32) * jnp.exp(lane * (-2.0 * math.log(10000.0) / HEAD_SIZE))
    cos_ref[...] = jnp.cos(angle)
    sin_ref[...] = jnp.sin(angle)
    expert = lax.broadcasted_iota(jnp.int32, (LANES, LANES), 0)

    def name(i):
        rows = aligned(i * LANES, LANES)
        routes = routes_ref[:, rows]
        named = expert == routes[:1]
        for k in range(1, TOPK):
            named = named | (expert == routes[k : k + 1])
        named_ref[rows] = jnp.where(named, 1.0, 0.0).T

    loop(0, named_ref.shape[0] // LANES, name)

    if relay:
        relay_arrival(0).wait_recv()
        relay_copy(2).start()
        share(1)
        relay_arrival(1).wait_recv()
        relay_copy(3).start()
        share(2)
        relay_arrival(2).wait_recv()
        relay_arrival(3).wait_recv()
        share(3)
    else:
        for o in range(1, nf):
            far_copy(o, from_f(o)).wait_recv()
            share(o)
    for o in range(nf):
        for p in range(1, nc):
            near_copy(p, o, lax.rem(c + nc - p, nc)).wait_recv()
    last = small_all[:, :, small_all.shape[2] - LANES :]
    gains_ref[...] = last.reshape(nf * nc * shard, LANES).astype(f32).T[E : E + 8]
    if relay:
        for i in range(4):
            relay_copy(i).wait_send()
    else:
        loop(1, nf, lambda o: far_copy(o, f).wait_send())
    for o in range(nf):
        for p in range(1, nc):
            near_copy(p, o, c).wait_send()


def front_kernel(
    n,
    nc,
    x_ref,
    small_ref,
    gains_ref,
    named_ref,
    cos_ref,
    sin_ref,
    query_ref,
    kv_ref,
    mixed_ref,
    state_hbm,
    normed_hbm,
    gates_ref,
    kv_all,
    own,
    state_ref,
    normed_ref,
    store_sem,
    send_kv,
    recv_kv,
    *scratch,
):
    me = lax.axis_index("tp")
    places = Places(nc)
    quarter = places.quarter
    seqs = kv_ref.shape[0]
    q_wide, k_wide = query_ref.shape[1], kv_ref.shape[2] // 2
    group = q_wide // k_wide
    qkv_wide = q_wide + 2 * k_wide
    wide = small_ref.shape[1] - LANES

    def row_stores(c):
        rows = line.rows(c)
        pairs = ((state_ref, state_hbm), (normed_ref, normed_hbm))
        return [
            pltpu.make_async_copy(source.at[rows], target.at[rows], store_sem.at[i, c])
            for i, (source, target) in enumerate(pairs)
        ]

    def finish(c, rows, total):
        state = x_ref[rows].astype(f32) + total
        scale = lax.rsqrt(jnp.mean(state * state, -1, keepdims=True) + epsilon)
        normed = (state * scale * gains_ref[1:2]).astype(bf16)
        state_ref[rows] = state.astype(bf16)
        normed_ref[rows] = normed
        for copy in row_stores(c):
            copy.start()
        named = named_ref[rows] > 0.5
        logits = jnp.where(named, dot(normed, small_ref[:, wide:]), -1e30)
        top = jnp.max(logits, -1, keepdims=True)
        raised = jnp.where(named, jnp.exp(logits - top), 0.0)
        gates_ref[rows] = raised / jnp.sum(raised, -1, keepdims=True)

    line = Line(n, me, own, finish, scratch, hop=2, late=quarter // 16)
    greet(me, n, [{"ctx": places.after(o)} for o in range(1, nc)])

    def kv_copy(s, part, o, rank):
        where = kv_all.at[s, places.rows(rank, part)]
        return pltpu.make_async_remote_copy(
            src_ref=where,
            dst_ref=where,
            send_sem=send_kv.at[o - 1, s, part],
            recv_sem=recv_kv.at[o - 1, s, part],
            device_id={"ctx": places.after(o)},
            device_id_type=MESH,
        )

    def project(s):
        for part in range(2):
            rows = places.own(s, part)
            x = x_ref[rows].astype(f32)
            scale = lax.rsqrt(jnp.mean(x * x, -1, keepdims=True) + epsilon)
            normed = (x * scale * gains_ref[:1]).astype(bf16)
            qkv = dot(normed, small_ref[:, :qkv_wide])
            qk = qkv[:, : q_wide + k_wide]
            here = pl.ds(part * quarter, quarter)
            cos, sin = widened(cos_ref[here], q_wide + k_wide), widened(sin_ref[here], q_wide + k_wide)
            rot = qk * cos + swapped_halves(qk) * sin
            query_ref[rows] = (rot[:, :q_wide] * (1.0 / math.sqrt(HEAD_SIZE))).astype(bf16)
            slot = places.rows(places.c, part)
            kv_all[s, slot, :k_wide] = rot[:, q_wide:].astype(bf16)
            kv_all[s, slot, k_wide:] = qkv[:, q_wide + k_wide :].astype(bf16)
            for o in range(1, nc):
                kv_copy(s, part, o, places.c).start()

    loop(0, seqs, project)

    def attend(s):
        for part in range(2):
            for o in range(1, nc):
                kv_copy(s, part, o, places.before(o)).wait_recv()
        for part in range(2):
            rows = places.own(s, part)
            keys = places.keys(part)
            base = places.slot(places.c, part) * quarter
            allowed = lax.broadcasted_iota(jnp.int32, (quarter, keys), 1) <= (
                base + lax.broadcasted_iota(jnp.int32, (quarter, keys), 0)
            )
            for h in range(q_wide // HEAD_SIZE):
                at = h // group * HEAD_SIZE
                query = query_ref[rows, h * HEAD_SIZE : (h + 1) * HEAD_SIZE]
                key = kv_all[s, :keys, at : at + HEAD_SIZE]
                value = kv_all[s, :keys, k_wide + at : k_wide + at + HEAD_SIZE]
                scores = jnp.where(allowed, dot(query, key, (1, 1)), -1e30)
                raised = jnp.exp(scores - jnp.max(scores, -1, keepdims=True))
                probs = (raised * (1.0 / jnp.sum(raised, -1, keepdims=True))).astype(bf16)
                mixed_ref[rows, h * HEAD_SIZE : (h + 1) * HEAD_SIZE] = dot(probs, value).astype(bf16)
            own[rows] = dot(mixed_ref[rows], small_ref[:, qkv_wide:wide], (1, 1)).astype(bf16)
            per = quarter // line.size
            first = (2 * s + part) * per
            loop(first, first + per, line.offer)
            loop(first, first + per, line.step)

    loop(0, seqs, attend)
    kv_ref[...] = kv_all[...]
    line.rest(line.chunks)

    def stored(c):
        for copy in row_stores(c):
            copy.wait()

    loop(0, line.chunks, stored)

    def kv_sent(s):
        for part in range(2):
            for o in range(1, nc):
                kv_copy(s, part, o, places.c).wait_send()

    loop(0, seqs, kv_sent)


def expert_kernel(
    n,
    x_hbm,
    dy_hbm,
    gates_ref,
    w_hbm,
    state_hbm,
    router_ref,
    gains_ref,
    out_ref,
    grads_hbm,
    dstate_hbm,
    dlogits_ref,
    dgain_ref,
    x_ref,
    dy_ref,
    state_ref,
    own,
    hidden_ref,
    grad_ref,
    x_turned,
    dy_turned,
    dots,    dots_all,
    dots_rows,
    w_ref,
    dstate_out,
    row_sem,
    w_sem,
    grads_sem,
    dstate_sem,
    send_dots,
    recv_dots,
    *scratch,
):
    me = lax.axis_index("tp")
    block, steps = pl.program_id(0), pl.num_programs(0)
    size_in, width = out_ref.shape
    pair = hidden_ref.shape[1] // (E // 2)
    single = pair // 2
    gu_wide = grad_ref.shape[1]
    here = aligned(block * size_in, size_in)

    def dots_copy(o, b):
        mine = dots_all.at[me, b]
        return pltpu.make_async_remote_copy(
            src_ref=mine,
            dst_ref=mine,
            send_sem=send_dots.at[o - 1, b],
            recv_sem=recv_dots.at[o - 1, b],
            device_id={"tp": lax.rem(me + o, n)},
            device_id_type=MESH,
        )

    def w_copies(p):
        spans = (aligned(p * 4 * pair, 4 * pair), aligned(gu_wide + p * 2 * pair, 2 * pair))
        return [
            pltpu.make_async_copy(w_hbm.at[:, span], w_ref.at[:, span], w_sem.at[i, p])
            for i, span in enumerate(spans)
        ]

    def row_copy(i, b):
        source, target = ((x_hbm, x_ref), (dy_hbm, dy_ref), (state_hbm, state_ref))[i]
        rows = aligned(b * size_in, size_in)
        return pltpu.make_async_copy(source.at[rows], target.at[rows], row_sem.at[i, b])

    def fetch_rows(b):
        row_copy(0, b).start()
        row_copy(1, b).start()

    def fetch_pair(i):
        for copy in w_copies(i):
            copy.start()

    def dstate_copy(c):
        return pltpu.make_async_copy(
            dstate_out.at[lax.rem(c, 2)], dstate_hbm.at[line.rows(c)], dstate_sem.at[lax.rem(c, 2)]
        )

    def finish(c, rows, total):
        per = size_in // line.size

        @pl.when(lax.rem(c, per) == 0)
        def _():
            b = c // per
            for o in range(1, n):
                dots_copy(o, b).wait_recv()
            summed = dots_all[0, b]
            for i in range(1, n):
                summed = summed + dots_all[i, b]
            summed = jnp.concatenate(
                [summed, jnp.zeros((LANES - summed.shape[0], summed.shape[1]), f32)], 0
            )
            dots_rows[aligned(b * size_in, size_in)] = summed.T

        @pl.when(c >= 2)
        def _():
            dstate_copy(c - 2).wait()

        gates = gates_ref[rows]
        lane = lax.broadcasted_iota(jnp.int32, gates.shape, 1)
        product = gates * dots_rows[rows]
        dlogits = product - gates * jnp.sum(product, -1, keepdims=True)
        dlogits = jnp.where(lane < E, dlogits, 0.0).astype(bf16)
        dlogits_ref[rows] = dlogits
        dn = total + dot(dlogits, router_ref[...], (1, 1))
        state = state_ref[rows].astype(f32)
        scale = lax.rsqrt(jnp.mean(state * state, -1, keepdims=True) + epsilon)
        unit = state * scale
        scaled = dn * gains_ref[1:2]
        inner = jnp.mean(scaled * unit, -1, keepdims=True)
        dstate = dy_ref[rows].astype(f32) + scale * (scaled - unit * inner)
        dstate_out[lax.rem(c, 2)] = dstate.astype(bf16)
        dstate_copy(c).start()
        dgain_ref[...] += folded(dn * unit)

    line = Line(n, me, own, finish, scratch, lag=size_in // (scratch[1].shape[0] // SLOTS), hop=2)
    per = size_in // line.size

    @pl.when(block == 0)
    def _():
        fetch_rows(0)
        fetch_pair(0)
        fetch_pair(1)
        barrier = pltpu.get_barrier_semaphore()
        for o in range(1, n):
            pl.semaphore_signal(
                barrier, inc=1, device_id={"tp": lax.rem(me + o, n)}, device_id_type=MESH
            )
        pl.semaphore_wait(barrier, n - 1)
        dgain_ref[...] = jnp.zeros_like(dgain_ref)


    lane = lax.broadcasted_iota(jnp.int32, (size_in, LANES), 1)
    first = lax.broadcasted_iota(jnp.int32, (size_in, pair), 1) < single
    dots[...] = jnp.zeros_like(dots)
    row_copy(0, block).wait()
    row_copy(1, block).wait()

    def gating(p, gate_pre, up_pre, raw):
        gates = gates_ref[here]
        gate = jnp.where(
            first,
            jnp.sum(jnp.where(lane == 2 * p, gates, 0.0), 1, keepdims=True),
            jnp.sum(jnp.where(lane == 2 * p + 1, gates, 0.0), 1, keepdims=True),
        )
        sigma = jax.nn.sigmoid(gate_pre)
        silu = gate_pre * sigma
        hidden = (silu * up_pre).astype(bf16).astype(f32)
        hidden_ref[here, aligned(p * pair, pair)] = (hidden * gate).astype(bf16)
        both = hidden * raw
        dots[...] += jnp.where(
            lane == 2 * p, jnp.sum(both[:, :single], 1, keepdims=True), 0.0
        ) + jnp.where(lane == 2 * p + 1, jnp.sum(both[:, single:], 1, keepdims=True), 0.0)
        dh = raw * gate
        grad_ref[here, aligned(p * 2 * pair, pair)] = (
            dh * up_pre * (sigma + silu * (1.0 - sigma))
        ).astype(bf16)
        grad_ref[here, aligned(p * 2 * pair + pair, pair)] = (dh * silu).astype(bf16)

    def two_pairs(i):
        @pl.when(block == 0)
        def _():
            for copy in w_copies(i):
                copy.wait()

            @pl.when(i + 2 < E // 4)
            def _():
                fetch_pair(i + 2)

            @pl.when(i == E // 4 - 2)
            def _():
                loop(1, steps, fetch_rows)
                loop(0, steps, lambda b: row_copy(2, b).start())

        gu = dot(x_ref[here], w_ref[:, aligned(i * 4 * pair, 4 * pair)])
        raw = dot(dy_ref[here], w_ref[:, aligned(gu_wide + i * 2 * pair, 2 * pair)])
        for j in range(2):
            at = 2 * j * pair
            gating(
                2 * i + j,
                gu[:, at : at + pair],
                gu[:, at + pair : at + 2 * pair],
                raw[:, j * pair : (j + 1) * pair],
            )

    tile = 512

    def back(i):
        at = aligned(i * tile, tile)
        own[here, at] = dot(grad_ref[here], w_ref[at, :gu_wide], (1, 1)).astype(bf16)

    def outward(i):
        at = aligned(i * tile, tile)
        carried = jnp.where(me == n // 2, state_ref[here, at].astype(f32), 0.0)
        moe = dot(hidden_ref[here], w_ref[at, gu_wide:], (1, 1))
        out_ref[:, at] = (moe + carried).astype(bf16)

    unit = per // 4
    tiles = width // tile

    def steps_at(i):
        first = block * per + i * unit
        loop(first, first + unit, line.step)

    for i in range(2):
        loop(i * (E // 8), (i + 1) * (E // 8), two_pairs)
        steps_at(i)
    dots_all[me, block] = dots[...].T[:E]
    for o in range(1, n):
        dots_copy(o, block).start()
    loop(0, tiles, back)
    loop(block * per, block * per + per, line.offer)
    steps_at(2)
    row_copy(2, block).wait()
    loop(0, tiles, outward)
    steps_at(3)

    @pl.when(block == steps - 1)
    def _():
        tall = x_turned.shape[0]
        count = width // tall
        wide = 4 * pair

        def grads_copy(m):
            rows = aligned(m * tall, tall)
            return pltpu.make_async_copy(w_ref.at[rows], grads_hbm.at[rows], grads_sem.at[m])

        def gradients(m):
            at = aligned(m * tall, tall)
            x_turned[...] = x_ref[:, at].T
            dy_turned[...] = dy_ref[:, at].T
            for i in range(gu_wide // wide):
                to = slice(i * wide, (i + 1) * wide)
                w_ref[at, to] = dot(x_turned[...], grad_ref[:, to]).astype(bf16)
            for i in range(gu_wide // wide // 2):
                to = slice(i * wide, (i + 1) * wide)
                w_ref[at, gu_wide + i * wide : gu_wide + (i + 1) * wide] = dot(
                    dy_turned[...], hidden_ref[:, to]
                ).astype(bf16)
            grads_copy(m).start()
            loop(steps * per + m * unit, steps * per + (m + 1) * unit, line.step)

        loop(0, count, gradients)
        line.rest(steps * per + count * unit)
        for c in range(line.chunks - 2, line.chunks):
            dstate_copy(c).wait()

        def dots_sent(b):
            for o in range(1, n):
                dots_copy(o, b).wait_send()

        loop(0, steps, dots_sent)
        loop(0, count, lambda m: grads_copy(m).wait())


def rear_kernel(
    n,
    nf,
    nc,
    moe_hbm,
    low_hbm,
    small_hbm,
    query_hbm,
    kv_hbm,
    x_hbm,
    normed_two_hbm,
    mixed_hbm,
    dlogits_hbm,
    gains_ref,
    dgain_two_ref,
    cos_ref,
    sin_ref,
    act_hbm,
    input_hbm,
    dgains_ref,
    grads_ref,
    moe_ref,
    low_ref,
    wout_ref,
    query_ref,
    kv_ref,
    wqkv_ref,
    x_ref,
    normed_two_ref,
    mixed_ref,
    dlogits_ref,
    dmixed,
    dquery,
    dkv,
    dkv_in,
    dqkv_ref,
    own,
    scales,
    dgain,
    gains_in,
    grads,
    grads_near,
    grads_far,
    moe_sem,
    load_sem,
    store_sem,
    send_kv,
    recv_kv,
    send_gain,
    recv_gain,
    send_near,
    recv_near,
    send_far,
    recv_far,
    *scratch,
):
    me = lax.axis_index("tp")
    flat = lax.axis_index("fsdp") * nc + lax.axis_index("ctx")
    places = Places(nc)
    quarter = places.quarter
    seqs = kv_ref.shape[0]
    q_wide, k_wide = query_ref.shape[1], kv_ref.shape[2] // 2
    group = q_wide // k_wide
    qkv_wide = q_wide + 2 * k_wide
    kv_heads = k_wide // HEAD_SIZE
    factor = 1.0 / math.sqrt(HEAD_SIZE)
    peers, padded = grads.shape[:2]
    shard = grads_ref.shape[0]
    loads = [
        pltpu.make_async_copy(source, target, load_sem.at[i])
        for i, (source, target) in enumerate(
            (
                (low_hbm, low_ref),
                (small_hbm.at[:, pl.ds(qkv_wide, wout_ref.shape[1])], wout_ref),
                (query_hbm, query_ref),
                (kv_hbm, kv_ref),
                (small_hbm.at[:, pl.ds(0, qkv_wide)], wqkv_ref),
                (x_hbm, x_ref),
                (normed_two_hbm, normed_two_ref),
                (mixed_hbm, mixed_ref),
                (dlogits_hbm, dlogits_ref),
            )
        )
    ]
    portions = moe_sem.shape[0]
    portion = moe_ref.shape[0] // portions

    def moe_load(i):
        rows = aligned(i * portion, portion)
        return pltpu.make_async_copy(moe_hbm.at[rows], moe_ref.at[rows], moe_sem.at[i])

    loop(0, portions, lambda i: moe_load(i).start())

    def peer(o):
        other = lax.rem(flat + o, peers)
        return {"fsdp": other // nc, "ctx": lax.rem(other, nc)}

    f = lax.axis_index("fsdp")

    def near_copy(p, g):
        return pltpu.make_async_remote_copy(
            src_ref=grads.at[g * nc + places.after(p)],
            dst_ref=grads_near.at[p - 1, g],
            send_sem=send_near.at[p - 1, g],
            recv_sem=recv_near.at[p - 1, g],
            device_id={"ctx": places.after(p)},
            device_id_type=MESH,
        )

    def far_copy(o):
        other = lax.rem(f + o, nf)
        return pltpu.make_async_remote_copy(
            src_ref=grads.at[other * nc + places.c],
            dst_ref=grads_far.at[o],
            send_sem=send_far.at[o],
            recv_sem=recv_far.at[o],
            device_id={"fsdp": other},
            device_id_type=MESH,
        )

    def gain_copy(o):
        return pltpu.make_async_remote_copy(
            src_ref=gains_in.at[0],
            dst_ref=gains_in.at[o],
            send_sem=send_gain.at[o],
            recv_sem=recv_gain.at[o],
            device_id=peer(o),
            device_id_type=MESH,
        )

    def kv_copy(s, part, o, rank):
        return pltpu.make_async_remote_copy(
            src_ref=dkv.at[s, places.rows(rank, part)],
            dst_ref=dkv_in.at[o - 1, s, part],
            send_sem=send_kv.at[o - 1, s, part],
            recv_sem=recv_kv.at[o - 1, s, part],
            device_id={"ctx": places.after(o)},
            device_id_type=MESH,
        )

    def finish_out(c, rows, total):
        moe_ref[rows] = total.astype(bf16)

    def finish_in(c, rows, total):
        x = x_ref[rows].astype(f32)
        scale = lax.rsqrt(jnp.mean(x * x, -1, keepdims=True) + epsilon)
        unit = x * scale
        scaled = total * gains_ref[:1]
        inner = jnp.mean(scaled * unit, -1, keepdims=True)
        own[rows] = (low_ref[rows].astype(f32) + scale * (scaled - unit * inner)).astype(bf16)
        dgain[...] += folded(total * unit)

    outward = Line(n, me, moe_ref, finish_out, scratch[:7], lag=1, hop=2)
    inward = Line(n, me, own, finish_in, scratch[7:], hop=3)
    dgain[...] = jnp.zeros_like(dgain)
    greet(me, n, [peer(o) for o in range(1, peers)])

    def offer(i):
        per = outward.chunks // portions
        moe_load(i).wait()
        loop(i * per, (i + 1) * per, outward.offer)

    heads, early = q_wide // HEAD_SIZE, 4
    for load in loads[:4]:
        load.start()
    loop(0, portions, offer)
    loop(0, early, outward.step)
    for load in loads[:4]:
        load.wait()
    for load in loads[4:]:
        load.start()


    def turned_back(y, part):
        wide = y.shape[1]
        here = pl.ds(part * quarter, quarter)
        return y * widened(cos_ref[here], wide) - swapped_halves(y) * widened(sin_ref[here], wide)

    def attend(s):
        for part in (1, 0):
            rows = places.own(s, part)
            keys = places.keys(part)
            dmixed[...] = dot(low_ref[rows], wout_ref[...]).astype(bf16)
            start = places.slot(places.c, part) * quarter
            allowed = lax.broadcasted_iota(jnp.int32, (keys, quarter), 0) <= (
                start + lax.broadcasted_iota(jnp.int32, (keys, quarter), 1)
            )
            for k in range(kv_heads):
                at = k * HEAD_SIZE
                key = kv_ref[s, :keys, at : at + HEAD_SIZE]
                value = kv_ref[s, :keys, k_wide + at : k_wide + at + HEAD_SIZE]
                dkey = dvalue = None
                for h in range(k * group, (k + 1) * group):
                    head = slice(h * HEAD_SIZE, (h + 1) * HEAD_SIZE)
                    query = query_ref[rows, head]
                    dout = dmixed[:, head]
                    scores = jnp.where(allowed, dot(key, query, (1, 1)), -1e30)
                    raised = jnp.exp(scores - jnp.max(scores, 0, keepdims=True))
                    probs = raised * (1.0 / jnp.sum(raised, 0, keepdims=True))
                    product = probs * dot(value, dout, (1, 1))
                    dscores = product - probs * jnp.sum(product, 0, keepdims=True)
                    dscores = dscores.astype(bf16)
                    dquery[:, head] = dot(dscores, key, (0, 0)) * factor
                    dk, dv = dot(dscores, query), dot(probs.astype(bf16), dout)
                    dkey = dk if dkey is None else dkey + dk
                    dvalue = dv if dvalue is None else dvalue + dv
                    outward.step(early + (2 * s + 1 - part) * heads + h)
                for first, add in ((at, dkey), (k_wide + at, dvalue)):
                    lanes = slice(first, first + HEAD_SIZE)
                    if part == 1:
                        dkv[s, :keys, lanes] = add
                    else:
                        dkv[s, :keys, lanes] += add
            dqkv_ref[rows, :q_wide] = turned_back(dquery[...], part).astype(bf16)
        for part in range(2):
            for o in range(1, nc):
                kv_copy(s, part, o, places.after(o)).start()

    loop(0, seqs, attend)
    done = early + 2 * seqs * heads
    for load in loads[4:]:
        load.wait()
    per = quarter // inward.size

    def turn_back(s):
        for part in range(2):
            rows = places.own(s, part)
            mine = dkv[s, places.rows(places.c, part)]
            for o in range(1, nc):
                kv_copy(s, part, o, places.after(o)).wait()
                mine = mine + dkv_in[o - 1, s, part]
            dqkv_ref[rows, q_wide : q_wide + k_wide] = turned_back(mine[:, :k_wide], part).astype(
                bf16
            )
            dqkv_ref[rows, q_wide + k_wide :] = mine[:, k_wide:].astype(bf16)
            own[rows] = dot(dqkv_ref[rows], wqkv_ref[...], (1, 1)).astype(bf16)
            first = (2 * s + part) * per
            loop(first, first + per, inward.offer)
            outward.step(done + 2 * s + part)
            x = x_ref[rows].astype(f32)
            scale = lax.rsqrt(jnp.mean(x * x, -1, keepdims=True) + epsilon)
            scales[rows] = jnp.broadcast_to(scale, (quarter, LANES))

    loop(0, seqs, turn_back)
    wide, mid = dqkv_ref.shape[1], dqkv_ref.shape[1] + mixed_ref.shape[1]
    span = max(LANES, shard * LANES // math.gcd(shard, LANES))
    count = span // shard

    def weights(i):
        at = aligned(i * span, span)
        to = pl.ds(i * count, count)

        def put(lanes, value):
            value = value.reshape(count, shard, value.shape[1])
            if padded > shard:
                more = jnp.zeros((count, padded - shard, value.shape[2]), f32)
                value = jnp.concatenate([value, more], 1)
            grads[to, :, lanes] = value.astype(bf16)

        normed = x_ref[:, at].astype(f32) * widened(scales[...], span) * gains_ref[:1, at]
        put(slice(0, wide), dot(normed.astype(bf16), dqkv_ref[...], (0, 0)))
        put(slice(wide, mid), dot(low_ref[:, at], mixed_ref[...], (0, 0)))
        put(slice(mid, grads.shape[2]), dot(normed_two_ref[:, at], dlogits_ref[...], (0, 0)))
        outward.step(done + 2 * seqs + i)

    spans = x_ref.shape[1] // span
    loop(0, spans, weights)
    def send_share(g):
        for p in range(1, nc):
            near_copy(p, g).start()

    loop(0, nf, send_share)
    start = done + 2 * seqs + spans
    ahead = max(outward.steps - start, 0)

    def both(i):
        outward.step(start + i)
        inward.step(i)

    loop(0, ahead, both)
    outward.rest(start + ahead)

    def add_share(g):
        mine = g * nc + places.c
        total = grads[mine].astype(f32)
        for p in range(1, nc):
            near_copy(p, g).wait()
            total = total + grads_near[p - 1, g].astype(f32)
        grads[mine] = total.astype(bf16)

    stores = [
        pltpu.make_async_copy(source, target, store_sem.at[i])
        for i, (source, target) in enumerate(((moe_ref, act_hbm), (own, input_hbm)))
    ]
    stores[0].start()
    enough = ahead + inward.chunks // 2
    loop(ahead, enough, inward.step)
    loop(0, nf, add_share)
    loop(1, nf, lambda o: far_copy(o).start())
    inward.rest(enough)
    stores[1].start()
    one = jnp.sum(dgain[...], 0, keepdims=True)
    two = jnp.sum(dgain_two_ref[...], 0, keepdims=True)
    gains_in[0] = jnp.concatenate([one, two], 1)
    loop(1, peers, lambda o: gain_copy(o).start())
    grads_ref[...] = grads[flat].astype(f32)[:shard]

    def add_grad(o):
        far_copy(o).wait()
        grads_ref[...] += grads_far[o].astype(f32)[:shard]

    loop(1, nf, add_grad)
    loop(1, peers, lambda o: gain_copy(o).wait())
    dgains_ref[...] = gains_in[0]

    def add(o):
        dgains_ref[...] += gains_in[o]

    loop(1, peers, add)
    for store in stores:
        store.wait()


def split_kernel(
    ffn,
    nc,
    grads_ref,
    small_ref,
    dgains_ref,
    out_hbm,
    input_hbm,
    gate_hbm,
    up_hbm,
    down_hbm,
    query_ref,
    key_ref,
    value_ref,
    out_ref,
    router_ref,
    gain_ref,
    act_hbm,
    grad_hbm,
    act,
    grad,
    gate_ref,
    up_ref,
    down_ref,
    load,
    store,
):
    loads = [
        pltpu.make_async_copy(input_hbm, grad, load.at[0]),
        pltpu.make_async_copy(out_hbm, act, load.at[1]),
    ]
    stores = [
        pltpu.make_async_copy(grad, grad_hbm, store.at[0]),
        pltpu.make_async_copy(act, act_hbm, store.at[1]),
        pltpu.make_async_copy(gate_ref, gate_hbm, store.at[2]),
        pltpu.make_async_copy(up_ref, up_hbm, store.at[3]),
        pltpu.make_async_copy(down_ref, down_hbm, store.at[4]),
    ]
    for copy in loads:
        copy.start()
    gu_wide = 2 * E * ffn
    at = 0
    for ref in (query_ref, key_ref, value_ref, out_ref):
        ref[...] = small_ref[:, at : at + ref.shape[1]]
        at += ref.shape[1]
    router_ref[...] = small_ref[:, at:].T[:E]
    width, shard = input_hbm.shape[1], small_ref.shape[0]
    flat = lax.axis_index("fsdp") * nc + lax.axis_index("ctx")
    shift = lax.rem(width - flat * shard, width)
    for i in range(2):
        row = jnp.broadcast_to(dgains_ref[:, i * width : (i + 1) * width], (8, width))
        gain_ref[i : i + 1] = pltpu.roll(row, shift, 1)[:1, :shard]
    loads[0].wait()
    stores[0].start()
    loads[1].wait()
    stores[1].start()
    for kind, ref in enumerate((gate_ref, up_ref, down_ref)):
        for e in range(E):
            at = (e // 2) * 4 * ffn + (e % 2) * ffn + kind * 2 * ffn
            if kind == 2:
                at = gu_wide + e * ffn
            ref[e] = grads_ref[:, at : at + ffn].astype(f32)
        stores[2 + kind].start()
    for copy in stores:
        copy.wait()


def call(kernel, outs, scratch, collective_id, operands, specs=None):
    total = sum(math.prod(o.shape) * o.dtype.itemsize for o in [*outs, *operands])
    return pl.pallas_call(
        kernel,
        out_shape=tuple(outs),
        in_specs=[WHOLE] * len(operands),
        out_specs=specs or (WHOLE,) * len(outs),
        scratch_shapes=scratch,
        compiler_params=pltpu.CompilerParams(
            collective_id=collective_id, has_side_effects=True, vmem_limit_bytes=VMEM_BYTES
        ),
        cost_estimate=pl.CostEstimate(flops=0, bytes_accessed=total, transcendentals=0),
    )(*operands)


def per_device(
    tokens,
    routes,
    gain_attn,
    w_query,
    key_matrix,
    value_matrix,
    w_out,
    gain_moe,
    w_router,
    w_gate,
    w_up,
    w_down,
    cotangent,
):
    shaped = jax.ShapeDtypeStruct
    rows, width = tokens.shape
    nc, n = lax.axis_size("ctx"), lax.axis_size("tp")
    half = SEQUENCE_LENGTH // nc
    seqs = rows // half
    both = ("fsdp", "ctx")
    q_wide, k_wide, o_wide = w_query.shape[1], key_matrix.shape[1], w_out.shape[0]
    qkv_wide = q_wide + 2 * k_wide
    ffn = w_gate.shape[2]
    shard = w_gate.shape[1]

    gu_wide, down_wide = 2 * E * ffn, E * ffn
    small_wide = qkv_wide + o_wide + LANES
    nf = lax.axis_size("fsdp")
    peers = nf * nc
    link = bf16 if shard % 16 == 0 else f32
    def sems(*dims):
        return pltpu.SemaphoreType.DMA(dims)

    small, gains, packed, cos, sin, named = call(
        functools.partial(gather_kernel, nf, nc, ffn),
        [
            shaped((peers, shard, small_wide), link),
            shaped((8, width), f32),
            shaped((shard, gu_wide + down_wide), bf16),
            shaped((half, LANES), f32),
            shaped((half, LANES), f32),
            shaped((rows, LANES), f32),
        ],
        [
            sems(nf),
            sems(nf),
            sems(nc - 1, nf),
            sems(nc - 1, nf),
        ],
        4,
        (
            w_query,
            key_matrix,
            value_matrix,
            w_out.T,
            w_router.T,
            gain_attn,
            gain_moe,
            w_gate,
            w_up,
            jnp.swapaxes(w_down, 1, 2),
            routes.T,
        ),
    )
    experts = lax.all_gather(packed, both, axis=0, tiled=True)
    small = small.reshape(width, small_wide).astype(bf16)
    kv_sems = sems(nc - 1, seqs, 2)
    anywhere = pl.BlockSpec(memory_space=pl.ANY)
    query, kv, mixed, state, normed_two, gates = call(
        functools.partial(front_kernel, n, nc),
        [
            shaped((rows, q_wide), bf16),
            shaped((seqs, SEQUENCE_LENGTH, 2 * k_wide), bf16),
            shaped((rows, q_wide), bf16),
            shaped((rows, width), bf16),
            shaped((rows, width), bf16),
            shaped((rows, LANES), f32),
        ],
        [
            pltpu.VMEM((seqs, SEQUENCE_LENGTH, 2 * k_wide), bf16),
            *[pltpu.VMEM((rows, width), bf16)] * 3,
            sems(2, rows // 32),
            kv_sems,
            kv_sems,
            *line_scratch(rows, width, 32),
        ],
        0,
        (tokens, small, gains, named, cos, sin),
        (WHOLE, WHOLE, WHOLE, anywhere, anywhere, WHOLE),
    )

    block = 256

    def by_rows(wide):
        return pl.BlockSpec((block, wide), lambda i: (i, 0))

    def constant(*dims):
        return pl.BlockSpec(
            dims, lambda i: (0,) * len(dims), pipeline_mode=pl.Buffered(1)
        )

    anywhere = pl.BlockSpec(memory_space=pl.ANY)
    blocks = rows // block
    size, tall = 64, 256
    dots_sems = pltpu.SemaphoreType.DMA((n - 1, blocks))
    moe_part, grad_experts, low, dlogits, dgain_two = pl.pallas_call(
        functools.partial(expert_kernel, n),
        grid=(blocks,),
        out_shape=(
            shaped((rows, width), bf16),
            shaped((width, gu_wide + down_wide), bf16),
            shaped((rows, width), bf16),
            shaped((rows, LANES), bf16),
            shaped((8, width), f32),
        ),
        in_specs=[
            anywhere,
            anywhere,
            constant(rows, LANES),
            anywhere,
            anywhere,
            pl.BlockSpec(
                (width, LANES),
                lambda i: (0, small_wide // LANES - 1),
                pipeline_mode=pl.Buffered(1),
            ),
            constant(8, width),
        ],
        out_specs=(
            by_rows(width),
            anywhere,
            anywhere,
            pl.BlockSpec((rows, LANES), lambda i: (0, 0)),
            pl.BlockSpec((8, width), lambda i: (0, 0)),
        ),
        scratch_shapes=[
            *[pltpu.VMEM((rows, width), bf16)] * 4,
            pltpu.VMEM((rows, down_wide), bf16),
            pltpu.VMEM((rows, gu_wide), bf16),
            pltpu.VMEM((tall, rows), bf16),
            pltpu.VMEM((tall, rows), bf16),
            pltpu.VMEM((block, LANES), f32),
            pltpu.VMEM((n, blocks, E, block), f32),
            pltpu.VMEM((rows, LANES), f32),
            pltpu.VMEM((width, gu_wide + down_wide), bf16),
            pltpu.VMEM((2, size, width), bf16),
            sems(3, blocks),
            sems(2, E // 4),
            sems(width // tall),
            sems(2),
            dots_sems,
            dots_sems,
            *line_scratch(rows, width, size),
        ],
        compiler_params=pltpu.CompilerParams(
            collective_id=1, has_side_effects=True, vmem_limit_bytes=VMEM_BYTES
        ),
        cost_estimate=pl.CostEstimate(
            flops=18 * rows * width * down_wide,
            bytes_accessed=2 * width * (gu_wide + down_wide),
            transcendentals=0,
        ),
    )(normed_two, cotangent, gates, experts, state, small, gains)

    low, grad_experts = lax.optimization_barrier((low, grad_experts))
    grad_experts = lax.psum_scatter(grad_experts, both, scatter_dimension=0, tiled=True)

    def small_block(*dims):
        return pltpu.VMEM((*dims, -(-shard // 16) * 16, small_wide), bf16)

    whole = pltpu.VMEM((rows, width), bf16)
    sources = (moe_part, low, small, query, kv, tokens, normed_two, mixed, dlogits)
    held = (
        *[(rows, width)] * 2,
        (width, o_wide),
        query.shape,
        kv.shape,
        (width, qkv_wide),
        *[(rows, width)] * 2,
        mixed.shape,
        dlogits.shape,
    )
    activations, input_grad, dgains, grad_small = pl.pallas_call(
        functools.partial(rear_kernel, n, nf, nc),
        out_shape=(
            shaped((rows, width), bf16),
            shaped((rows, width), bf16),
            shaped((1, 2 * width), f32),
            shaped((shard, small_wide), f32),
        ),
        in_specs=[anywhere] * len(sources) + [WHOLE] * 4,
        out_specs=(anywhere, anywhere, WHOLE, WHOLE),
        scratch_shapes=[
            *[pltpu.VMEM(dims, bf16) for dims in held],
            pltpu.VMEM((half // 2, q_wide), bf16),
            pltpu.VMEM((half // 2, q_wide), f32),
            pltpu.VMEM((seqs, SEQUENCE_LENGTH, 2 * k_wide), f32),
            pltpu.VMEM((nc - 1, seqs, 2, half // 2, 2 * k_wide), f32),
            pltpu.VMEM((rows, qkv_wide), bf16),
            whole,
            pltpu.VMEM((rows, LANES), f32),
            pltpu.VMEM((8, width), f32),
            pltpu.VMEM((peers, 1, 2 * width), f32),
            small_block(peers),
            small_block(nc - 1, nf),
            small_block(nf),
            sems(4),
            sems(len(held) - 1),
            sems(2),
            kv_sems,
            kv_sems,
            *[sems(peers)] * 2,
            *[sems(nc - 1, nf)] * 2,
            *[sems(nf)] * 2,
            *line_scratch(rows, width, 32),
            *line_scratch(rows, width, 32),
        ],
        compiler_params=pltpu.CompilerParams(
            collective_id=3, has_side_effects=True, vmem_limit_bytes=VMEM_BYTES
        ),
        cost_estimate=pl.CostEstimate(
            flops=12 * rows * width * small_wide,
            bytes_accessed=16 * rows * width,
            transcendentals=0,
        ),
    )(*sources, gains, dgain_two, cos, sin)
    results = pl.pallas_call(
        functools.partial(split_kernel, ffn, nc),
        out_shape=(
            shaped((E, shard, ffn), f32),
            shaped((E, shard, ffn), f32),
            shaped((E, shard, ffn), f32),
            shaped((shard, q_wide), f32),
            shaped((shard, k_wide), f32),
            shaped((shard, k_wide), f32),
            shaped((shard, o_wide), f32),
            shaped((E, shard), f32),
            shaped((2, shard), f32),
            shaped((rows, width), bf16),
            shaped((rows, width), bf16),
        ),
        in_specs=[WHOLE, WHOLE, WHOLE, anywhere, anywhere],
        out_specs=(*[anywhere] * 3, *[WHOLE] * 6, anywhere, anywhere),
        scratch_shapes=[
            pltpu.VMEM((rows, width), bf16),
            pltpu.VMEM((rows, width), bf16),
            *[pltpu.VMEM((E, shard, ffn), f32)] * 3,
            sems(2),
            sems(5),
        ],
        compiler_params=pltpu.CompilerParams(vmem_limit_bytes=VMEM_BYTES),
    )(grad_experts, grad_small, dgains, activations, input_grad)
    grad_gate, grad_up, grad_down, grad_query, grad_key, grad_value, grad_out = results[:7]
    grad_router, dgains = results[7:9]
    return (
        results[9],
        results[10],
        dgains[0],
        grad_query,
        grad_key,
        grad_value,
        grad_out.T,
        dgains[1],
        grad_router.T,
        grad_gate,
        grad_up,
        jnp.swapaxes(grad_down, 1, 2),
    )


def solution(mesh):
    specs = (
        P(("fsdp", "ctx"), None),
        P(("fsdp", "ctx"), None),
        P(("fsdp", "ctx")),
        P(("fsdp", "ctx"), "tp"),
        P(("fsdp", "ctx"), "tp"),
        P(("fsdp", "ctx"), "tp"),
        P("tp", ("fsdp", "ctx")),
        P(("fsdp", "ctx")),
        P(("fsdp", "ctx"), None),
        P(None, ("fsdp", "ctx"), "tp"),
        P(None, ("fsdp", "ctx"), "tp"),
        P(None, "tp", ("fsdp", "ctx")),
        P(("fsdp", "ctx"), None),
    )
    return jax.shard_map(
        per_device,
        mesh=mesh,
        in_specs=specs,
        out_specs=(
            P(("fsdp", "ctx"), None),
            P(("fsdp", "ctx"), None),
            P(("fsdp", "ctx")),
            P(("fsdp", "ctx"), "tp"),
            P(("fsdp", "ctx"), "tp"),
            P(("fsdp", "ctx"), "tp"),
            P("tp", ("fsdp", "ctx")),
            P(("fsdp", "ctx")),
            P(("fsdp", "ctx"), None),
            P(None, ("fsdp", "ctx"), "tp"),
            P(None, ("fsdp", "ctx"), "tp"),
            P(None, "tp", ("fsdp", "ctx")),
        ),
        check_vma=False,
    )
```
